32 devices in a mesh: mesh: 2 (over core), blk: 16 (over z, y, x).
Axes of the slice: x: 2, y: 2, z: 4, core: 2. Of those that a mesh axis runs over, the one named last changes fastest.
Arguments:
- rotation_step: int32 [1], replicated, may hold values from 1 to 7
- field_state: float32 [2, 16, 4, 128, 256], P('mesh', 'blk'), may hold values from -6 to 6
- diffusivity: float32 [2, 16, 2, 128, 256], P('mesh', 'blk'), may hold values from 0.05 to 2
- stretch: float32 [2, 16, 128, 256], P('mesh', 'blk'), may hold values from 100 to 3000
- donor_base: int32 [2, 16, 4096], P('mesh', 'blk'), may hold values from 0 to 32478, as said below
- donor_frac: float32 [2, 16, 3, 4096], P('mesh', 'blk'), may hold values from 0 to 1
- fringe_cell: int32 [2, 16, 4096], P('mesh', 'blk'), may hold values from 0 to 32768, as said below
Outputs:
- new_fields: float32 [2, 16, 4, 128, 256], P('mesh', 'blk')
The draws below stay inside these ranges and needn't reach their ends.
Inputs may be any that keep to these rules, and one draw needn't show every extreme that they name: `donor_base`: each entry is z * 8 * 32 + x * 32 + y with z < 127, x < 7 and y < 31. `fringe_cell`: in each block, the slots p * 256 to (p + 1) * 256 - 1 hold the cells that receive values from block p of the other mesh, used slots first; every fringe cell of the block is named by exactly one used slot; an unused slot holds 32768. A group has 0 to 256 used slots, and in every block some group is full and some is empty.
All inputs are finite; a program needn't handle non-finite values.
Results may differ from the reference program's by a relative error of at most 0.00017.
Values sent between devices are 32-bit elements; how exact they have to be, the bound alone decides.
No kernel may reach another device: no remote copies, remote signals or barrier semaphores. Data moves between devices by JAX's collectives and lax.ppermute only.
A program may use at most 64 MiB of HBM per device.

```python
import math
from functools import partial
import jax
import jax.numpy as jnp
from jax import lax

CX = 8
CY = 32
CZ = 128
ITERS = 2
TURN_MOST = 7
NB = 16
SLOTS = 4096
CAP = 256


def fringe_block(block_key):
    key_pair, key_shift, key_cells = jax.random.split(block_key, 3)
    half_cap = CAP // 2
    pairing = jax.random.permutation(key_pair, NB)
    transfer = jax.random.randint(key_shift, (NB // 2,), 0, half_cap + 1)
    transfer = transfer.at[0].set(half_cap)
    counts = jnp.zeros((NB,), jnp.int32)
    counts = counts.at[pairing[0::2]].set(half_cap + transfer)
    counts = counts.at[pairing[1::2]].set(half_cap - transfer)
    offsets = jnp.cumsum(counts) - counts
    slot_ids = jnp.arange(SLOTS, dtype=jnp.int32)
    group_ids = slot_ids // CAP
    within = slot_ids % CAP
    is_live = within < counts[group_ids]
    ranks = jnp.minimum(offsets[group_ids] + within, SLOTS // 2 - 1)
    shuffled = jax.random.permutation(key_cells, SLOTS // 2)
    picked = shuffled[ranks]
    depth = picked // (2 * CX)
    remains = picked % (2 * CX)
    row_pos = remains // 2
    col_pos = remains % 2 * (CY - 1)
    flat_cell = depth * CX * CY + row_pos * CY + col_pos
    return jnp.where(is_live, flat_cell, CZ * CX * CY).astype(jnp.int32)


def draw_fringe_cell(key, part):
    block_keys = jax.vmap(lambda index_value: jax.random.fold_in(key, index_value))(jnp.arange(2 * NB))
    return jax.vmap(fringe_block)(block_keys).reshape(2, NB, SLOTS)


def draw_donor_base(key, part):
    key_depth, key_row, key_col = jax.random.split(jax.random.fold_in(key, 7), 3)
    shape_all = (2, NB, SLOTS)
    depth = jax.random.randint(key_depth, shape_all, 0, CZ - 1)
    row_pos = jax.random.randint(key_row, shape_all, 0, CX - 1)
    col_pos = jax.random.randint(key_col, shape_all, 0, CY - 1)
    flat_cell = depth * CX * CY + row_pos * CY + col_pos
    flat_cell = flat_cell.at[0, 0, 0].set((CZ - 2) * CX * CY + (CX - 2) * CY + CY - 2)
    return flat_cell.astype(jnp.int32)


def steps_of(own_key, shape, cuts, low, top_value):
    loudness, own = 1.0, jax.random.fold_in(own_key, 6)
    for position, shards_of in cuts:
        steps = jnp.exp(jax.random.uniform(jax.random.fold_in(own, position), (shards_of,), jnp.float32, low / len(cuts), top_value / len(cuts)))
        loudness = loudness * jnp.repeat(steps, shape[position] // shards_of).reshape([-1 if axis == position else 1 for axis in range(len(shape))])
    return loudness


def centred(key, shape, deviation, bound, pieces=(), kind=jnp.bfloat16):
    array = jax.random.normal(key, shape, jnp.float32) * deviation
    if len(pieces) > 0:
        array = steps_of(key, shape, pieces, -0.22, 0.18) * array
    return jnp.clip(array, min=-bound, max=bound).astype(kind)


def setup_inputs(seed: int = 0) -> dict:
    streams_of = jax.random.split(jax.random.key(seed), 8)
    rotation_step = jax.random.randint(streams_of[0], (1,), 1, TURN_MOST + 1).astype(jnp.int32)
    field_state = centred(streams_of[1], (2, NB, 4, CZ, CX * CY), 1.0, 6.0, ((0, 2), (1, 16)), jnp.float32)
    diffusivity = jnp.clip(jnp.exp(math.log(2.0) - 3.6888794 * jax.random.uniform(streams_of[2], (2, NB, 2, CZ, CX * CY), jnp.float32) ** steps_of(streams_of[2], (2, NB, 2, CZ, CX * CY), ((0, 2), (1, 16)), -0.2, 0.2)), 0.05, 2.0)
    stretch = jnp.clip(jnp.exp(math.log(3000.0) - 3.4011974 * jax.random.uniform(streams_of[3], (2, NB, CZ, CX * CY), jnp.float32) ** steps_of(streams_of[3], (2, NB, CZ, CX * CY), ((0, 2), (1, 16)), -0.2, 0.2)), 100.0, 3000.0)
    donor_base = draw_donor_base(jax.random.fold_in(streams_of[7], 71), 0)
    donor_frac = jnp.clip(1.0 * jax.random.uniform(streams_of[5], (2, NB, 3, SLOTS), jnp.float32) ** steps_of(streams_of[5], (2, NB, 3, SLOTS), ((0, 2), (1, 16)), -0.2, 0.2), 0.0, 1.0)
    fringe_cell = draw_fringe_cell(jax.random.fold_in(streams_of[7], 71), 0)
    return {"rotation_step": rotation_step, "field_state": field_state, "diffusivity": diffusivity, "stretch": stretch, "donor_base": donor_base, "donor_frac": donor_frac, "fringe_cell": fringe_cell}


def before(values, stride, filler):
    length = values.shape[-2]
    padding = jnp.full(values.shape[:-2] + (stride,) + values.shape[-1:], filler, values.dtype)
    return jnp.concatenate([padding, values[..., :length - stride, :]], axis=-2)


def behind(values, stride, filler):
    length = values.shape[-2]
    padding = jnp.full(values.shape[:-2] + (stride,) + values.shape[-1:], filler, values.dtype)
    return jnp.concatenate([values[..., stride:, :], padding], axis=-2)


def solve_lines(lower_band, middle, upper_band, right_side):
    length = middle.shape[-2]
    stride = 1
    while stride < length:
        factor_low = -lower_band / before(middle, stride, 1.0)
        factor_high = -upper_band / behind(middle, stride, 1.0)
        new_lower = factor_low * before(lower_band, stride, 0.0)
        new_upper = factor_high * behind(upper_band, stride, 0.0)
        new_middle = middle + factor_low * before(upper_band, stride, 0.0) + factor_high * behind(lower_band, stride, 0.0)
        new_right = right_side + factor_low * before(right_side, stride, 0.0) + factor_high * behind(right_side, stride, 0.0)
        lower_band, upper_band, middle, right_side = new_lower, new_upper, new_middle, new_right
        stride = stride * 2
    return right_side / middle


def interpolate(fields, donor_bases, donor_fracs, row_length):
    plane_size = fields.shape[-1]
    flattened = fields.reshape(fields.shape[0], -1)
    summed = jnp.zeros((fields.shape[0], donor_bases.shape[-1]), fields.dtype)
    for depth_step in (0, 1):
        weight_z = donor_fracs[0] if depth_step else 1.0 - donor_fracs[0]
        for row_step in (0, 1):
            weight_x = donor_fracs[1] if row_step else 1.0 - donor_fracs[1]
            for col_step in (0, 1):
                weight_y = donor_fracs[2] if col_step else 1.0 - donor_fracs[2]
                offset = depth_step * plane_size + row_step * row_length + col_step
                picked = jnp.take(flattened, donor_bases + offset, axis=1)
                summed = summed + (weight_z * weight_x * weight_y)[None, :] * picked
    return summed


def place_donors(fields, target_cells, arrived):
    flattened = fields.reshape(fields.shape[0], -1)
    flattened = flattened.at[:, target_cells].set(arrived, mode="drop")
    return flattened.reshape(fields.shape)


def relax_block(filled, extended, initial, coeffs, along):
    width = filled.shape[-1]
    rim_width = (extended.shape[-1] - width) // 2
    across = extended[..., :width] + extended[..., 2 * rim_width:]
    zero_column = jnp.zeros(filled.shape[:-1] + (1,), filled.dtype)
    sideways = jnp.concatenate([zero_column, filled[..., :-1]], axis=-1) + jnp.concatenate([filled[..., 1:], zero_column], axis=-1)
    per_field = jnp.concatenate([coeffs[0:1], coeffs[0:1], coeffs[0:1], coeffs[1:2]], axis=0)
    right_side = initial + per_field * (across + sideways)
    along_full = jnp.broadcast_to(along[None], filled.shape)
    middle = 1.0 + 2.0 * along_full + 4.0 * per_field
    depth_index = lax.broadcasted_iota(jnp.int32, filled.shape, 1)
    lower_band = jnp.where(depth_index == 0, 0.0, -along_full)
    upper_band = jnp.where(depth_index == filled.shape[1] - 1, 0.0, -along_full)
    solved = solve_lines(lower_band, middle, upper_band, right_side)
    column = lax.broadcasted_iota(jnp.int32, filled.shape, 2) % rim_width
    fringe = (column == 0) | (column == rim_width - 1)
    return jnp.where(fringe, filled, solved)


def reference(rotation_step, field_state, diffusivity, stretch, donor_base, donor_frac, fringe_cell):
    rotation = rotation_step[0]

    def migrate(values):
        return jnp.stack([values[0], jnp.roll(values[1], rotation, axis=0)])

    initial = migrate(field_state)
    coeffs = migrate(diffusivity)
    alongs = migrate(stretch)
    donor_bases = migrate(donor_base)
    donor_fracs = migrate(donor_frac)
    target_cells = migrate(fringe_cell)
    blocks = field_state.shape[1]
    per_peer = target_cells.shape[-1] // blocks
    fields = initial
    inner = jax.vmap(jax.vmap(partial(interpolate, row_length=CY)))
    placing = jax.vmap(jax.vmap(place_donors))
    for sweep_index in range(ITERS):
        outbound = inner(fields, donor_bases, donor_fracs)
        grouped = outbound.reshape(2, blocks, 4, blocks, per_peer).transpose(0, 3, 2, 1, 4)
        grouped = grouped.reshape(2, blocks, 4, blocks * per_peer)[::-1]
        filled = placing(fields, target_cells, grouped)
        left_rim = jnp.roll(filled, 1, axis=1)[..., -CY:]
        right_rim = jnp.roll(filled, -1, axis=1)[..., :CY]
        extended = jnp.concatenate([left_rim, filled, right_rim], axis=-1)
        flat_shape = (2 * blocks,)

        def relax_one(packed):
            return relax_block(packed[0], packed[1], packed[2], packed[3], packed[4])

        relaxed = lax.map(relax_one, (filled.reshape(flat_shape + filled.shape[2:]), extended.reshape(flat_shape + extended.shape[2:]), initial.reshape(flat_shape + initial.shape[2:]), coeffs.reshape(flat_shape + coeffs.shape[2:]), alongs.reshape(flat_shape + alongs.shape[2:])))
        fields = relaxed.reshape(filled.shape)
    return fields
```

```python
import functools
import jax
import jax.numpy as jnp
from jax import lax
from jax.experimental import pallas as pl
from jax.experimental.pallas import tpu as pltpu
from jax.sharding import PartitionSpec as P

CY = 32
ITERS = 2
TURN_MOST = 7
F32, BF = jnp.float32, jnp.bfloat16
VM = pl.BlockSpec(memory_space=pltpu.VMEM)
SM = pl.BlockSpec(memory_space=pltpu.SMEM)
CP = pltpu.CompilerParams(vmem_limit_bytes=48 * 1024 * 1024)


def split2(v):
    hi = v.astype(BF)
    lo = (v - hi.astype(F32)).astype(BF)
    return hi, lo


def interp_kernel(info_ref, f_ref, base_ref, frac_ref, o_ref, a_ref, *, tile):
    nf, nz, npl = f_ref.shape
    nx = npl // CY
    for f in range(nf):
        hi, lo = split2(f_ref[f].T)
        for i, part in enumerate((hi, hi, lo, lo)):
            a_ref[f * npl:(f + 1) * npl, i * nz:(i + 1) * nz] = part
    nt = base_ref.shape[1] // tile
    o_ref[pl.ds(nt - info_ref[1], nt)] = jnp.zeros((nt,) + o_ref.shape[1:], F32)

    def body(t, carry):
        g = lax.rem(t + info_ref[0], nt)
        off = pl.multiple_of(g * tile, tile)
        b = base_ref[0:1, pl.ds(off, tile)]
        fz, fx, fy = [frac_ref[i:i + 1, pl.ds(off, tile)] for i in range(3)]
        z0 = b // npl
        x0 = b // CY % nx
        y0 = b % CY
        iz = lax.broadcasted_iota(jnp.int32, (nz, tile), 0)
        whi, wlo = split2(jnp.where(iz == z0, 1.0 - fz, jnp.where(iz == z0 + 1, fz, 0.0)))
        w = jnp.concatenate([whi, wlo, whi, wlo], axis=0)
        iy = lax.broadcasted_iota(jnp.int32, (CY, tile), 0)
        wy = jnp.where(iy == y0, 1.0 - fy, jnp.where(iy == y0 + 1, fy, 0.0))
        wx = [jnp.where(x0 == x, 1.0 - fx, jnp.where(x0 == x - 1, fx, 0.0)) for x in range(nx)]
        rows = []
        for f in range(nf):
            p = jnp.dot(a_ref[f * npl:(f + 1) * npl, :], w, preferred_element_type=F32)
            acc = wx[0] * p[:CY]
            for x in range(1, nx):
                acc = acc + wx[x] * p[x * CY:(x + 1) * CY]
            r = jnp.sum(acc * wy, axis=0, keepdims=True)
            rows += [r[:, i * 128:(i + 1) * 128] for i in range(tile // 128)]
        o_ref[info_ref[1] + t] = jnp.concatenate(rows, axis=0)
        return carry

    lax.fori_loop(0, nt, body, 0, unroll=nt)


def interp(info, fields, base, frac, tile):
    nf, nz, npl = fields.shape
    slots = base.shape[-1]
    return pl.pallas_call(
        functools.partial(interp_kernel, tile=tile),
        out_shape=jax.ShapeDtypeStruct((2 * slots // tile, nf * tile // 128, 128), F32),
        in_specs=[SM] + [VM] * 3,
        out_specs=VM,
        scratch_shapes=[pltpu.VMEM((nf * npl, 4 * nz), BF)],
        compiler_params=CP,
        name="interp",
    )(info, fields, base.reshape(1, slots), frac)


def down(v, k):
    return pltpu.roll(v, k, axis=0)
def up(v, k):
    return pltpu.roll(v, v.shape[0] - k, axis=0)

def factor(g_ref, q0, q1, p1, q2, p2, h, iv):
    nz, w = g_ref.shape
    for c in range(0, w, 128):
        s = slice(c, c+128)
        z = lax.broadcasted_iota(jnp.int32, (nz, 128), 0)
        g = g_ref[:, s]
        q = 1.0 / g
        q0[:, s] = q
        qd = jnp.where(z >= 1, down(q, 1), 0.0)
        qu = jnp.where(z < nz-1, up(q, 1), 0.0)
        g = g - qd - qu
        p = jnp.where(z >= 2, qd, 0.0)
        for k, (qr, pr) in ((2, (q1, p1)), (4, (q2, p2))):
            q = 1.0 / g
            qr[:, s] = q
            pr[:, s] = p
            pq = p * q
            ppq = p * pq
            g = g - p * p * down(q, k) - up(ppq, k)
            p = p * down(pq, k)
            p = jnp.where(z >= 2*k, p, 0.0)
        g_ref[:, s] = g
        h[:, s] = p
    prev = None
    for r in range(0, nz, 8):
        g = g_ref[r:r+8, :]
        if prev is None:
            hk = jnp.zeros_like(g)
        else:
            p = h[r:r+8, :]
            hk = p * prev
            g = g - p * hk
        prev = 1.0 / g
        h[r:r+8, :] = hk
        iv[r:r+8, :] = prev

def reduce_rhs(r, s, fs):
    q0, q1, p1, q2, p2 = fs
    nz = r.shape[0]
    z = lax.broadcasted_iota(jnp.int32, r.shape, 0)
    w = q0[:, s] * r
    r = r + jnp.where(z >= 1, down(w, 1), 0.0) + jnp.where(z < nz-1, up(w, 1), 0.0)
    for k, qr, pr in ((2, q1, p1), (4, q2, p2)):
        w = qr[:, s] * r
        p = pr[:, s]
        r = r + p * down(w, k) + up(p * w, k)
    return r

def widen(v, sets):
    half = v.shape[1] // 2
    m, p = v[:, :half], v[:, half:]
    return jnp.concatenate([m, m, m, p], axis=1)

def substitute(y, h, iv):
    nz = y.shape[0]
    prev = y[0:8, :]
    for r in range(8, nz, 8):
        prev = y[r:r+8, :] + widen(h[r:r+8, :], 0) * prev
        y[r:r+8, :] = prev
    prev = prev * widen(iv[nz-8:nz, :], 0)
    y[nz-8:nz, :] = prev
    for r in range(nz-16, -1, -8):
        prev = y[r:r+8, :] * widen(iv[r:r+8, :], 0) + widen(h[r+8:r+16, :], 0) * prev
        y[r:r+8, :] = prev

def place(shift_ref, arr_ref, cells_ref, row0, nf, nz, npl):
    slots = cells_ref.shape[1]
    rows = arr_ref.shape[1]
    per = rows // nf
    tile = per * 128
    nt = slots // tile
    nx = npl // CY
    nq = 2 * nx
    zo, av = [], []
    for t in range(nt):
        g = lax.rem(t + shift_ref[0], nt)
        c = cells_ref[0:1, pl.ds(pl.multiple_of(g*tile, tile), tile)]
        cz = c // npl
        q = (c // CY) % nx * 2 + (c & 1)
        zo.append((lax.broadcasted_iota(jnp.int32, (nz, tile), 0) == cz).astype(F32).astype(BF))
        oh = lax.broadcasted_iota(jnp.int32, (nq, tile), 0) == q
        a = arr_ref[row0 + t]
        his, los = [], []
        for f in range(nf):
            row = jnp.concatenate([a[f*per+i:f*per+i+1] for i in range(per)], axis=1)
            v = jnp.where(oh, row, 0.0)
            hi, lo = split2(v)
            his.append(hi); los.append(lo)
        av.append(jnp.concatenate(his + los, axis=0))
    zo = jnp.concatenate(zo, axis=1)
    av = jnp.concatenate(av, axis=1)
    small = lax.dot_general(zo, av, (((1,), (1,)), ((), ())), preferred_element_type=F32)
    kk = lax.broadcasted_iota(jnp.int32, (2*nf*nq, 1), 0) % (nf*nq)
    target = kk // nq * npl + (kk % nq) // 2 * CY + (kk & 1) * (CY - 1)
    e = (lax.broadcasted_iota(jnp.int32, (2*nf*nq, nf*npl), 1) == target).astype(F32).astype(BF)
    return jnp.dot(small.astype(BF), e, preferred_element_type=F32)

def relax_kernel(info_ref, arr_ref, cells_ref, start_ref, fields_ref, kap_ref, al_ref, hl_ref, hr_ref,
                 o_ref, *rest, pack):
    nf, nz, npl = start_ref.shape
    nt = npl // 128
    if pack:
        pl_ref, pr_ref, *rest = rest
    fr, y, g, q0, q1, p1, q2, p2, h, iv, si = rest
    for k in range(2):
        s = al_ref[...]
        inv = 1.0 / s
        si[...] = inv
        g[:, k*npl:(k+1)*npl] = 2.0 + (1.0 + 4.0 * kap_ref[k]) * inv
    factor(g, q0, q1, p1, q2, p2, h, iv)
    fr[...] = place(info_ref, arr_ref, cells_ref, info_ref[1], nf, nz, npl)
    lane = lax.broadcasted_iota(jnp.int32, (nz, 128), 1)
    fringe = (lane % CY == 0) | (lane % CY == CY - 1)
    lpt = 128 // CY
    for f in range(nf):
        k = 1 if f == nf - 1 else 0
        tiles = [jnp.where(fringe, fr[:, f*npl+t*128:f*npl+(t+1)*128], fields_ref[f, :, t*128:(t+1)*128]) for t in range(nt)]
        rp = [pltpu.roll(v, CY, axis=1) for v in tiles]
        rm = [pltpu.roll(v, 128 - CY, axis=1) for v in tiles]
        hl = hl_ref[...] if f == 0 else pltpu.roll(hl_ref[...], 128 - f*CY, axis=1)
        hr = hr_ref[...] if f == lpt - 1 else pltpu.roll(hr_ref[...], 128 - CY - f*CY, axis=1)
        for t in range(nt):
            left = jnp.where(lane < CY, hl if t == 0 else rp[t-1], rp[t])
            right = jnp.where(lane >= 128 - CY, hr if t == nt - 1 else rm[t+1], rm[t])
            side = pltpu.roll(tiles[t], 1, axis=1) + pltpu.roll(tiles[t], 127, axis=1)
            sl = slice(t*128, (t+1)*128)
            r = (start_ref[f, :, sl] + kap_ref[k, :, sl] * (left + right + side)) * si[:, sl]
            fsl = slice(k*npl + t*128, k*npl + (t+1)*128)
            y[:, f*npl+t*128:f*npl+(t+1)*128] = reduce_rhs(r, fsl, (q0, q1, p1, q2, p2))
    substitute(y, h, iv)
    for f in range(nf):
        for t in range(nt):
            sl = slice(f*npl+t*128, f*npl+(t+1)*128)
            o_ref[f, :, t*128:(t+1)*128] = jnp.where(fringe, fr[:, sl], y[:, sl])
    if pack:
        pack_planes(lambda f, t: y[:, f*npl+t*128:f*npl+(t+1)*128], nf, nt, lane, pl_ref, pr_ref)

def pack_planes(get, nf, nt, lane, lo_ref, hi_ref):
    lo = hi = None
    for f in range(nf):
        a = get(f, 0)
        b = get(f, nt - 1)
        a = a if f == 0 else pltpu.roll(a, f*CY, axis=1)
        sh = (f*CY - (128 - CY)) % 128
        b = b if sh == 0 else pltpu.roll(b, sh, axis=1)
        m = (lane >= f*CY) & (lane < (f+1)*CY)
        lo = a if lo is None else jnp.where(m, a, lo)
        hi = b if hi is None else jnp.where(m, b, hi)
    lo_ref[...] = lo
    hi_ref[...] = hi

def pack_kernel(f_ref, lo_ref, hi_ref):
    nf, nz, npl = f_ref.shape
    lane = lax.broadcasted_iota(jnp.int32, (nz, 128), 1)
    nt = npl // 128
    pack_planes(lambda f, t: f_ref[f, :, t*128:(t+1)*128], nf, nt, lane, lo_ref, hi_ref)

def pack(fields):
    nf, nz, npl = fields.shape
    sh = jax.ShapeDtypeStruct((nz, nf*CY), F32)
    return pl.pallas_call(pack_kernel, out_shape=(sh, sh), in_specs=[VM], out_specs=(VM, VM), compiler_params=CP, name="pack")(fields)

def relax(info, arrived, cells, start, fields, kappa, along, hl, hr, with_pack):
    nf, nz, npl = start.shape
    out = [jax.ShapeDtypeStruct(start.shape, F32)]
    if with_pack:
        out += [jax.ShapeDtypeStruct((nz, nf*CY), F32)]*2
    wide, half = pltpu.VMEM((nz, nf*npl), F32), pltpu.VMEM((nz, 2*npl), F32)
    return pl.pallas_call(
        functools.partial(relax_kernel, pack=with_pack),
        out_shape=out, in_specs=[SM] + [VM]*8, out_specs=[VM]*len(out),
        scratch_shapes=[wide, wide] + [half]*8 + [pltpu.VMEM((nz, npl), F32)],
        compiler_params=CP, name="relax",
    )(info, arrived, cells.reshape(1, -1), start, fields, kappa, along, hl, hr)


TILE = 256


def exchange(values, blocks, cap, nf):
    if cap == TILE:
        return lax.all_to_all(values, ("mesh", "blk"), 0, 0, tiled=True)
    halves = values.reshape(2, -1, nf, TILE).transpose(0, 2, 1, 3).reshape(2, nf, blocks, cap)
    sent = halves.transpose(0, 2, 1, 3).reshape(2 * blocks, nf, cap)
    got = lax.all_to_all(sent, ("mesh", "blk"), 0, 0, tiled=True)
    got = got.reshape(2, blocks, nf, cap).transpose(0, 2, 1, 3).reshape(2, nf, -1, TILE)
    return got.transpose(0, 2, 1, 3).reshape(values.shape)


def turn(values, cap, by):
    groups = values.reshape(values.shape[:-1] + (-1, cap))
    return jnp.roll(groups, -by, axis=-2).reshape(values.shape)


def migrate(fields, rotation, blocks):
    def branch(distance):
        stay = [(i, i) for i in range(blocks)]
        move = [(blocks + (i - distance) % blocks, blocks + i) for i in range(blocks)]
        return lambda v: lax.ppermute(v, ("mesh", "blk"), stay + move)

    return lax.switch(rotation - 1, [branch(d) for d in range(1, TURN_MOST + 1)], fields)


def local(rotation_step, field_state, diffusivity, stretch, donor_base, donor_frac, fringe_cell):
    on_back = lax.axis_index("mesh") == 1
    blocks = lax.axis_size("blk")
    rotation = rotation_step[0]
    start, kappa, along = field_state[0, 0], diffusivity[0, 0], stretch[0, 0]
    base, frac, cells = donor_base[0, 0], donor_frac[0, 0], fringe_cell[0, 0]
    nf = start.shape[0]
    slots = base.shape[0]
    cap = slots // blocks
    by = jnp.where(on_back, 0, rotation)
    if cap != TILE:
        base, frac, cells = turn(base, cap, by), turn(frac, cap, by), turn(cells, cap, by)
        by = jnp.zeros_like(by)
    half = jnp.where(on_back, 0, slots // TILE)
    info = jnp.stack([by, half]).astype(jnp.int32)
    ring = [(i, (i + 1) % blocks) for i in range(blocks)]
    back = [((i + 1) % blocks, i) for i in range(blocks)]
    low, high = pack(start)
    fields = start
    for sweep in range(ITERS):
        before = lax.ppermute(high, "blk", ring)
        behind = lax.ppermute(low, "blk", back)
        values = interp(info, fields, base, frac, TILE)
        arrived = exchange(values, blocks, cap, nf)
        last = sweep == ITERS - 1
        out = relax(info, arrived, cells, start, fields, kappa, along, before, behind, not last)
        fields = out[0]
        if not last:
            low, high = out[1:]
    return migrate(fields, rotation, blocks)[None, None]


def solution(mesh):
    placed = (
        P(),
        P("mesh", "blk", None, None, None),
        P("mesh", "blk", None, None, None),
        P("mesh", "blk", None, None),
        P("mesh", "blk", None),
        P("mesh", "blk", None, None),
        P("mesh", "blk", None),
    )
    return jax.shard_map(
        local,
        mesh=mesh,
        in_specs=placed,
        out_specs=P("mesh", "blk", None, None, None),
        check_vma=False,
    )
```

```python
import functools
import jax
import jax.numpy as jnp
from jax import lax
from jax.experimental import pallas as pl
from jax.experimental.pallas import tpu as pltpu
from jax.sharding import PartitionSpec as P

CY = 32
ITERS = 2
TURN_MOST = 7
F32, BF = jnp.float32, jnp.bfloat16
VM = pl.BlockSpec(memory_space=pltpu.VMEM)
SM = pl.BlockSpec(memory_space=pltpu.SMEM)
ANY = pl.BlockSpec(memory_space=pl.ANY)
WHOLE = pltpu.CompilerParams(vmem_limit_bytes=64 * 1024 * 1024)
CP = pltpu.CompilerParams(vmem_limit_bytes=48 * 1024 * 1024)


def split2(v):
    hi = v.astype(BF)
    lo = (v - hi.astype(F32)).astype(BF)
    return hi, lo


def down(v, k):
    return pltpu.roll(v, k, axis=0)
def up(v, k):
    return pltpu.roll(v, v.shape[0] - k, axis=0)

def factor(g_ref, q0, q1, p1, q2, p2, h, iv):
    nz, w = g_ref.shape
    for c in range(0, w, 128):
        s = slice(c, c+128)
        z = lax.broadcasted_iota(jnp.int32, (nz, 128), 0)
        g = g_ref[:, s]
        q = 1.0 / g
        q0[:, s] = q
        qd = jnp.where(z >= 1, down(q, 1), 0.0)
        qu = jnp.where(z < nz-1, up(q, 1), 0.0)
        g = g - qd - qu
        p = jnp.where(z >= 2, qd, 0.0)
        for k, (qr, pr) in ((2, (q1, p1)), (4, (q2, p2))):
            q = 1.0 / g
            qr[:, s] = q
            pr[:, s] = p
            pq = p * q
            ppq = p * pq
            g = g - p * p * down(q, k) - up(ppq, k)
            p = p * down(pq, k)
            p = jnp.where(z >= 2*k, p, 0.0)
        g_ref[:, s] = g
        h[:, s] = p
    prev = None
    for r in range(0, nz, 8):
        g = g_ref[r:r+8, :]
        if prev is None:
            hk = jnp.zeros_like(g)
        else:
            p = h[r:r+8, :]
            hk = p * prev
            g = g - p * hk
        prev = 1.0 / g
        h[r:r+8, :] = hk
        iv[r:r+8, :] = prev

def reduce_rhs(r, s, fs):
    q0, q1, p1, q2, p2 = fs
    nz = r.shape[0]
    z = lax.broadcasted_iota(jnp.int32, r.shape, 0)
    w = q0[:, s] * r
    r = r + jnp.where(z >= 1, down(w, 1), 0.0) + jnp.where(z < nz-1, up(w, 1), 0.0)
    for k, qr, pr in ((2, q1, p1), (4, q2, p2)):
        w = qr[:, s] * r
        p = pr[:, s]
        r = r + p * down(w, k) + up(p * w, k)
    return r


def substitute(y, h, iv, widen):
    nz = y.shape[0]
    prev = y[0:8, :]
    for r in range(8, nz, 8):
        prev = y[r:r+8, :] + widen(h[r:r+8, :]) * prev
        y[r:r+8, :] = prev
    prev = prev * widen(iv[nz-8:nz, :])
    y[nz-8:nz, :] = prev
    for r in range(nz-16, -1, -8):
        prev = y[r:r+8, :] * widen(iv[r:r+8, :]) + widen(h[r+8:r+16, :]) * prev
        y[r:r+8, :] = prev


def same(v):
    return v


def lanes(nz):
    return lax.broadcasted_iota(jnp.int32, (nz, 128), 1)


def on_fringe(lane):
    return (lane % CY == 0) | (lane % CY == CY - 1)


def pack_planes(get, nf, t, x, lane):
    out = None
    for f in range(nf):
        v = get(f, t)
        by = (f - x) * CY % 128
        v = v if by == 0 else pltpu.roll(v, by, axis=1)
        out = v if out is None else jnp.where(lane >= f * CY, v, out)
    return out


def pack_kernel(f_any, kap_any, al_any, lo_ref, hi_ref, f_ref, kap_ref, al_ref, sems):
    nf, nz, npl = f_ref.shape
    copies = [pltpu.make_async_copy(f_any.at[f], f_ref.at[f], sems.at[f]) for f in range(nf)]
    copies += [pltpu.make_async_copy(kap_any.at[k], kap_ref.at[k], sems.at[nf + k]) for k in range(2)]
    copies += [pltpu.make_async_copy(al_any, al_ref, sems.at[nf + 2])]
    for c in copies:
        c.start()
    for c in copies:
        c.wait()
    lane = lanes(nz)
    per, nt = 128 // CY, npl // 128

    def field(f, t):
        return f_ref[f, :, t*128:(t+1)*128]

    def coef(f, t):
        sl = slice(t*128, (t+1)*128)
        return kap_ref[f, :, sl] if f < 2 else al_ref[:, sl]

    for ref, t, x, step in ((lo_ref, 0, 0, 1), (hi_ref, nt - 1, per - 1, -1)):
        ref[0] = pack_planes(field, nf, t, x, lane)
        ref[1] = pack_planes(field, nf, t, x + step, lane)
        ref[2] = pack_planes(coef, 3, t, x, lane)


def pack(fields, kappa, along):
    nf, nz, npl = fields.shape
    sh = jax.ShapeDtypeStruct((3, nz, nf * CY), F32)
    return pl.pallas_call(
        pack_kernel,
        out_shape=(sh, sh),
        in_specs=[ANY] * 3,
        out_specs=(VM, VM),
        scratch_shapes=[pltpu.VMEM(v.shape, F32) for v in (fields, kappa, along)] + [pltpu.SemaphoreType.DMA((nf + 3,))],
        compiler_params=WHOLE,
        name="pack",
    )(fields, kappa, along)


def places(turn, tiles, blocks, turned):
    back = lax.axis_index("mesh")
    me = lax.axis_index("blk")
    by = 0 if turned else turn * (1 - back)
    return by, tiles * (1 - back), lax.rem(me + turn * back, blocks), back, lax.rem(me + blocks - turn * back, blocks)


def load_tiles(unroll, o_ref, info_ref, base_ref, frac_ref, a_ref, shift, nf, nz, npl, tile):
    nx = npl // CY
    nt = base_ref.shape[1] // tile
    o_ref[pl.ds(nt - info_ref[1], nt)] = jnp.zeros((nt,) + o_ref.shape[1:], F32)

    def body(t, carry):
        g = t if shift is None else lax.rem(t + shift, nt)
        off = pl.multiple_of(g * tile, tile)
        b = base_ref[0:1, pl.ds(off, tile)]
        fz, fx, fy = [frac_ref[i, :, pl.ds(off, tile)] for i in range(3)]
        z0 = b // npl
        x0 = b // CY % nx
        y0 = b % CY
        iz = lax.broadcasted_iota(jnp.int32, (nz, tile), 0)
        whi, wlo = split2(jnp.where(iz == z0, 1.0 - fz, jnp.where(iz == z0 + 1, fz, 0.0)))
        w = jnp.concatenate([whi, wlo, whi, wlo], axis=0)
        iy = lax.broadcasted_iota(jnp.int32, (CY, tile), 0)
        wy = jnp.where(iy == y0, 1.0 - fy, jnp.where(iy == y0 + 1, fy, 0.0))
        wx = [jnp.where(x0 == x, 1.0 - fx, jnp.where(x0 == x - 1, fx, 0.0)) for x in range(nx)]
        rows = []
        for f in range(nf):
            p = jnp.dot(a_ref[f * npl:(f + 1) * npl, :], w, preferred_element_type=F32)
            acc = wx[0] * p[:CY]
            for x in range(1, nx):
                acc = acc + wx[x] * p[x * CY:(x + 1) * CY]
            r = jnp.sum(acc * wy, axis=0, keepdims=True)
            rows += [r[:, i * 128:(i + 1) * 128] for i in range(tile // 128)]
        o_ref[info_ref[1] + t] = jnp.concatenate(rows, axis=0)
        return carry

    lax.fori_loop(0, nt, body, 0, unroll=unroll)


def split_into(a_ref, row, v):
    n, nz = v.shape
    hi, lo = split2(v)
    for i, part in enumerate((hi, hi, lo, lo)):
        a_ref[row:row + n, i * nz:(i + 1) * nz] = part


def interp_kernel(turn_any, f_any, base_any, frac_any, o_ref, a_ref, f_ref, base_ref, frac_ref, turn_ref, sems, *, tile, blocks, turned):
    nf, nz, npl = f_ref.shape
    copies = [pltpu.make_async_copy(f_any.at[f], f_ref.at[f], sems.at[f]) for f in range(nf)]
    copies += [pltpu.make_async_copy(base_any, base_ref, sems.at[nf])]
    copies += [pltpu.make_async_copy(frac_any, frac_ref, sems.at[nf + 1])]
    copies += [pltpu.make_async_copy(turn_any, turn_ref, sems.at[nf + 2])]
    for c in copies:
        c.start()
    for f in range(nf):
        copies[f].wait()
        split_into(a_ref, f * npl, f_ref[f].T)
    for c in copies[nf:]:
        c.wait()
    info_ref = places(turn_ref[0], base_ref.shape[1] // tile, blocks, turned)
    load_tiles(16, o_ref, info_ref, base_ref, frac_ref, a_ref, info_ref[0], nf, nz, npl, tile)


def interp(turn, fields, base, frac, tile, blocks, turned):
    nf, nz, npl = fields.shape
    slots = base.shape[-1]
    return pl.pallas_call(
        functools.partial(interp_kernel, tile=tile, blocks=blocks, turned=turned),
        out_shape=jax.ShapeDtypeStruct((2 * slots // tile, nf * tile // 128, 128), F32),
        in_specs=[ANY] * 4,
        out_specs=VM,
        scratch_shapes=[pltpu.VMEM((nf * npl, 4 * nz), BF), pltpu.VMEM(fields.shape, F32),
                        pltpu.VMEM(base.shape, jnp.int32), pltpu.VMEM(frac.shape, F32),
                        pltpu.SMEM((1,), jnp.int32), pltpu.SemaphoreType.DMA((nf + 3,))],
        compiler_params=CP,
        name="interp",
    )(turn, fields, base, frac)


def right_sides(start_ref, tiles, hl, hr, kap_ref, si, y, fs, lane):
    nf, nz, npl = start_ref.shape
    nt = npl // 128
    for f in range(nf):
        k = 1 if f == nf - 1 else 0
        v = tiles(f)
        rp = [pltpu.roll(u, CY, axis=1) for u in v]
        rm = [pltpu.roll(u, 128 - CY, axis=1) for u in v]
        left_in = hl if f == 0 else pltpu.roll(hl, 128 - f * CY, axis=1)
        by = (128 - CY - f * CY) % 128
        right_in = hr if by == 0 else pltpu.roll(hr, by, axis=1)
        for t in range(nt):
            left = jnp.where(lane < CY, left_in if t == 0 else rp[t-1], rp[t])
            right = jnp.where(lane >= 128 - CY, right_in if t == nt - 1 else rm[t+1], rm[t])
            side = pltpu.roll(v[t], 1, axis=1) + pltpu.roll(v[t], 127, axis=1)
            sl = slice(t * 128, (t + 1) * 128)
            r = (start_ref[f, :, sl] + kap_ref[k, :, sl] * (left + right + side)) * si[:, sl]
            y[:, f*npl+t*128:f*npl+(t+1)*128] = reduce_rhs(r, slice(k*npl + t*128, k*npl + (t+1)*128), fs)


def march_kernel(start_ref, kap_ref, al_ref, lo_ref, hi_ref, left_ref, right_ref, cells_ref,
                 f1t_ref, pay_ref, fac_ref, y, y2, g, q0, q1, p1, q2, p2, h, iv, si, gs):
    nf, nz, npl = start_ref.shape
    nt = npl // 128
    own = 2 * npl
    lane = lanes(nz)
    fringe = on_fringe(lane)
    inv = 1.0 / al_ref[...]
    si[...] = inv
    for k in range(2):
        g[:, k*npl:(k+1)*npl] = 2.0 + (1.0 + 4.0 * kap_ref[k]) * inv
    outer = []
    for i, (near, mine) in enumerate(((left_ref, lo_ref), (right_ref, hi_ref))):
        c3 = near[2]
        r32, r64, r96 = [pltpu.roll(c3, j, axis=1) for j in (32, 64, 96)]
        c = jnp.where(lane < CY, c3, jnp.where(lane < 2*CY, r32, r64))
        s = jnp.where(lane < CY, r64, jnp.where(lane < 2*CY, r96, jnp.where(lane < 3*CY, c3, r32)))
        inv = 1.0 / s
        g[:, own+i*128:own+(i+1)*128] = 2.0 + (1.0 + 4.0 * c) * inv
        v = near[0]
        z = jnp.where(fringe, 0.0, v)
        side = pltpu.roll(z, 1, axis=1) + pltpu.roll(z, 127, axis=1)
        outer.append((v + c * (near[1] + mine[0] + side)) * inv)
    fs = (q0, q1, p1, q2, p2)
    factor(g, q0, q1, p1, q2, p2, h, iv)

    def clear(v):
        return jnp.where(fringe, 0.0, v)

    right_sides(start_ref, lambda f: [clear(start_ref[f, :, t*128:(t+1)*128]) for t in range(nt)],
                left_ref[0], right_ref[0], kap_ref, si, y, fs, lane)
    for i in range(2):
        y[:, nf*npl+i*128:nf*npl+(i+1)*128] = reduce_rhs(outer[i], slice(own+i*128, own+(i+1)*128), fs)

    def widen(v):
        m, p = v[:, :npl], v[:, npl:own]
        return jnp.concatenate([m] * (nf - 1) + [p, v[:, own:]], axis=1)

    def widen_own(v):
        m, p = v[:, :npl], v[:, npl:own]
        return jnp.concatenate([m] * (nf - 1) + [p], axis=1)

    substitute(y, h, iv, widen)

    def first(f):
        return [clear(y[:, f*npl+t*128:f*npl+(t+1)*128]) for t in range(nt)]

    right_sides(start_ref, first, y[:, nf*npl:nf*npl+128], y[:, nf*npl+128:nf*npl+256], kap_ref, si, y2, fs, lane)
    substitute(y2, h, iv, widen_own)
    for f in range(nf):
        for t in range(nt):
            j = f * nt + t
            pay_ref[j*nz:(j+1)*nz, :] = y2[:, f*npl+t*128:f*npl+(t+1)*128]
    for f in range(nf):
        v = first(f)
        for t in range(nt):
            f1t_ref[f*npl+t*128:f*npl+(t+1)*128, :] = v[t].T
    nx = npl // CY
    half = nf * 2 * nx
    ln = lane % half
    x, side, deep = ln // 2 % nx, ln % 2, jnp.where(lane >= half, 2, 1)
    src = x % (128 // CY) * CY + jnp.where(side == 0, deep, CY - 1 - deep)

    def pick(get):
        out = None
        for t in range(nt):
            v = jnp.take_along_axis(get(t), src, axis=1)
            out = v if out is None else jnp.where(x // (128 // CY) == t, v, out)
        return out

    ck = [pick(lambda t, k=k: kap_ref[k, :, t*128:(t+1)*128]) for k in range(2)]
    c = jnp.where(ln // (2 * nx) == nf - 1, ck[1], ck[0])
    inv = pick(lambda t: si[:, t*128:(t+1)*128])
    cs = c * inv
    gg = 2.0 + (inv + 4.0 * cs)
    j = nf * nt
    pay_ref[j*nz:(j+1)*nz, :] = cs
    pay_ref[(j+1)*nz:(j+2)*nz, :] = gg
    pay_ref[(j+2)*nz:, :] = cells_ref[...].astype(F32)
    gs[...] = gg
    refs = [fac_ref.at[i*nz:(i+1)*nz] for i in range(7)]
    factor(gs, *refs)
    fac_ref[7*nz:, :] = cs


def march(start, kappa, along, low, high, left, right, cells):
    nf, nz, npl = start.shape
    nt = npl // 128
    rows = (nf * nt + 2) * nz + cells.shape[0]
    w = 2 * npl + 256
    return pl.pallas_call(
        march_kernel,
        out_shape=(jax.ShapeDtypeStruct((nf * npl, nz), F32), jax.ShapeDtypeStruct((rows, 128), F32),
                   jax.ShapeDtypeStruct((8 * nz, 128), F32)),
        in_specs=[VM] * 8,
        out_specs=(VM, VM, VM),
        scratch_shapes=[pltpu.VMEM((nz, nf*npl+256), F32), pltpu.VMEM((nz, nf*npl), F32)]
        + [pltpu.VMEM((nz, w), F32)] * 8 + [pltpu.VMEM((nz, npl), F32), pltpu.VMEM((nz, 128), F32)],
        compiler_params=CP,
        name="march",
    )(start, kappa, along, low, high, left, right, cells)


def place_small(shift, arr_ref, row0, cell_row, slots, nf, nz, npl):
    rows = arr_ref.shape[1]
    per = rows // nf
    tile = per * 128
    nt = slots // tile
    nx = npl // CY
    nq = 2 * nx
    zo, av = [], []
    for t in range(nt):
        c = cell_row(lax.rem(t + shift, nt), tile)
        cz = c // npl
        q = c // CY % nx * 2 + c % 2
        zo.append((lax.broadcasted_iota(jnp.int32, (nz, tile), 0) == cz).astype(F32).astype(BF))
        oh = lax.broadcasted_iota(jnp.int32, (nq, tile), 0) == q
        a = arr_ref[row0 + t]
        his, los = [], []
        for f in range(nf):
            row = jnp.concatenate([a[f*per+i:f*per+i+1] for i in range(per)], axis=1)
            hi, lo = split2(jnp.where(oh, row, 0.0))
            his.append(hi)
            los.append(lo)
        av.append(jnp.concatenate(his + los, axis=0))
    zo = jnp.concatenate(zo, axis=1)
    av = jnp.concatenate(av, axis=1)
    return lax.dot_general(zo, av, (((1,), (1,)), ((), ())), preferred_element_type=F32)


def spots(k, nf, npl, low, high):
    nq = 2 * npl // CY
    return k // nq % nf * npl + k % nq // 2 * CY + jnp.where(k % 2 == 0, low, high)


def relay_kernel(turn_ref, arr_ref, cells_ref, f1t_ref, fac_ref, base_ref, frac_ref, o_ref, e_ref, a_ref, ys, *, tile, nf, edges, blocks, turned):
    nz = f1t_ref.shape[1]
    info_ref = places(turn_ref[0], base_ref.shape[1] // tile, blocks, turned)
    npl = f1t_ref.shape[0] // nf
    slots = base_ref.shape[1]
    half = nf * 2 * npl // CY
    lane = lanes(nz)

    def cell_row(g, tile):
        return cells_ref[0:1, pl.ds(pl.multiple_of(g * tile, tile), tile)]

    sm = place_small(info_ref[0], arr_ref, info_ref[1], cell_row, slots, nf, nz, npl)
    fr = sm + pltpu.roll(sm, half, axis=1)
    fac = [fac_ref.at[i*nz:(i+1)*nz] for i in range(8)]
    ys[...] = reduce_rhs(fac[7][...] * fr, slice(0, 128), fac[:5])
    substitute(ys, fac[5], fac[6], same)
    e = ys[...]
    e_ref[...] = e
    hi, lo = split2(e)
    both = jnp.where(lane < half, hi.astype(F32), pltpu.roll(lo.astype(F32), half, axis=1))
    terms = jnp.concatenate([sm.astype(BF), both.astype(BF)], axis=1)
    k = lax.broadcasted_iota(jnp.int32, (1, 256), 1)
    target = jnp.where(k < 128, spots(k, nf, npl, 0, CY - 1), spots(k, nf, npl, 1, CY - 2))
    for f in range(nf):
        row = lax.broadcasted_iota(jnp.int32, (npl, 256), 0) + f * npl
        put = (row == target).astype(F32).astype(BF)
        add = lax.dot_general(put, terms, (((1,), (1,)), ((), ())), preferred_element_type=F32)
        split_into(a_ref, f * npl, f1t_ref[f*npl:(f+1)*npl, :] + add)
    load_tiles(UNROLL, o_ref, info_ref, base_ref, frac_ref, a_ref, None, nf, nz, npl, tile)
    if edges:
        turned = e.T
        nt = slots // tile
        nq = half // nf
        for col, by in ((nq - 2, 1), (0, nt - 1)):
            rows = jnp.concatenate([turned[f*nq+col:f*nq+col+2] for f in range(nf)], axis=0)
            o_ref[nt - info_ref[1] + lax.rem(info_ref[2] + by, nt)] = rows


def relay(turn, arrived, cells, f1t, fac, base, frac, tile, nf, edges, blocks, turned):
    nz = f1t.shape[1]
    return pl.pallas_call(
        functools.partial(relay_kernel, tile=tile, nf=nf, edges=edges, blocks=blocks, turned=turned),
        out_shape=(jax.ShapeDtypeStruct(arrived.shape, F32), jax.ShapeDtypeStruct((nz, 128), F32)),
        in_specs=[SM] + [VM] * 6,
        out_specs=(VM, VM),
        scratch_shapes=[pltpu.VMEM((f1t.shape[0], 4 * nz), BF), pltpu.VMEM((nz, 128), F32)],
        compiler_params=CP,
        name="relay",
    )(turn, arrived, cells, f1t, fac, base, frac)


def finish_kernel(turn_ref, arr_ref, own_ref, moved_ref, e_ref, came_ref, *rest, edges, blocks, turned):
    if edges:
        o_ref, pay_ref, ys, gs, *fac, sems = rest
    else:
        el_ref, er_ref, o_ref, pay_ref, ys, gs, *fac, sems = rest
    nf, nz, npl = o_ref.shape
    nt = npl // 128
    nx = npl // CY
    nq = 2 * nx
    half = nf * nq
    j = nf * nt
    cells0 = (j + 2) * nz
    slots = (pay_ref.shape[0] - cells0) * 128
    info_ref = places(turn_ref[0], arr_ref.shape[0] // 2, blocks, turned)

    lines = slice(j * nz, pay_ref.shape[0])
    rest = slice(0, j * nz)

    def copies(ref):
        return [pltpu.make_async_copy(ref.at[s], pay_ref.at[s], sems.at[i]) for i, s in enumerate((lines, rest))]

    @pl.when(info_ref[3] == 0)
    def _():
        for c in copies(own_ref):
            c.start()

    @pl.when(info_ref[3] != 0)
    def _():
        for c in copies(moved_ref):
            c.start()

    lane = lanes(nz)
    q = lane % nq
    e = jnp.where(info_ref[3] == 0, e_ref[...], came_ref[...])
    if edges:
        chunks = arr_ref.shape[0] // 2
        el = arr_ref[chunks - info_ref[1] + lax.rem(info_ref[4] + chunks - 1, chunks)]
        er = arr_ref[chunks - info_ref[1] + lax.rem(info_ref[4] + 1, chunks)]
        none = jnp.zeros((nq - 4, nz), F32)
        parts = []
        for f in range(nf):
            parts += [el[2*f:2*f+2], none, er[2*f:2*f+2]]
        parts = jnp.concatenate(parts, axis=0)
        outer = jnp.concatenate([parts, parts], axis=0).T
        left = right = outer
    else:
        left = pltpu.roll(el_ref[...], 128 - (nq - 2), axis=1)
        right = pltpu.roll(er_ref[...], nq - 2, axis=1)
    left = jnp.where(q < 2, left, pltpu.roll(e, 2, axis=1))
    right = jnp.where(q >= nq - 2, right, pltpu.roll(e, 126, axis=1))
    deep = pltpu.roll(e, half, axis=1)
    copies(own_ref)[0].wait()
    gs[...] = pay_ref[(j+1)*nz:(j+2)*nz, :]
    factor(gs, *fac)

    def cell_row(g, tile):
        per = tile // 128
        rows = [pay_ref[pl.ds(cells0 + g * per + i, 1), :] for i in range(per)]
        return jnp.concatenate(rows, axis=1).astype(jnp.int32)

    sm = place_small(info_ref[0], arr_ref, info_ref[1], cell_row, slots, nf, nz, npl)
    fr = sm + pltpu.roll(sm, half, axis=1)
    cs = pay_ref[j*nz:(j+1)*nz, :]
    r = cs * jnp.where(lane < half, fr + left + right, deep)
    ys[...] = reduce_rhs(r, slice(0, 128), fac[:5])
    substitute(ys, fac[5], fac[6], same)
    hi, lo = split2(ys[...])
    terms = jnp.concatenate([sm.astype(BF), hi, lo], axis=1)
    k = lax.broadcasted_iota(jnp.int32, (384, 1), 0)
    near = jnp.where(k % 128 < half, 1, 2)
    target = jnp.where(k < 128, spots(k, nf, npl, 0, CY - 1), spots(k, nf, npl, near, CY - 1 - near))
    fringe = on_fringe(lane)
    copies(own_ref)[1].wait()
    for f in range(nf):
        put = (lax.broadcasted_iota(jnp.int32, (384, npl), 1) + f * npl == target).astype(F32).astype(BF)
        add = jnp.dot(terms, put, preferred_element_type=F32)
        for t in range(nt):
            v = pay_ref[(f*nt+t)*nz:(f*nt+t+1)*nz, :]
            o_ref[f, :, t*128:(t+1)*128] = jnp.where(fringe, 0.0, v) + add[:, t*128:(t+1)*128]


def finish(turn, shape, arrived, own, moved, e, blocks, turned):
    nz = shape[1]
    return pl.pallas_call(
        functools.partial(finish_kernel, edges=len(e) == 2, blocks=blocks, turned=turned),
        out_shape=jax.ShapeDtypeStruct(shape, F32),
        in_specs=[SM, VM, ANY, ANY] + [VM] * len(e),
        out_specs=VM,
        scratch_shapes=[pltpu.VMEM(own.shape, F32)] + [pltpu.VMEM((nz, 128), F32)] * 9 + [pltpu.SemaphoreType.DMA((2,))],
        compiler_params=CP,
        name="finish",
    )(turn, arrived, own, moved, *e)


TILE = 256
UNROLL = 4


def exchange(values, blocks, cap, nf):
    if cap == TILE:
        return lax.all_to_all(values, ("mesh", "blk"), 0, 0, tiled=True)
    halves = values.reshape(2, -1, nf, TILE).transpose(0, 2, 1, 3).reshape(2, nf, blocks, cap)
    sent = halves.transpose(0, 2, 1, 3).reshape(2 * blocks, nf, cap)
    got = lax.all_to_all(sent, ("mesh", "blk"), 0, 0, tiled=True)
    got = got.reshape(2, blocks, nf, cap).transpose(0, 2, 1, 3).reshape(2, nf, -1, TILE)
    return got.transpose(0, 2, 1, 3).reshape(values.shape)


def turn(values, cap, by):
    groups = values.reshape(values.shape[:-1] + (-1, cap))
    return jnp.roll(groups, -by, axis=-2).reshape(values.shape)


def local(rotation_step, field_state, diffusivity, stretch, donor_base, donor_frac, fringe_cell):
    on_back = lax.axis_index("mesh") == 1
    blocks = lax.axis_size("blk")
    rotation = rotation_step[0]
    start, kappa, along = field_state[0, 0], diffusivity[0, 0], stretch[0, 0]
    base, frac, cells = donor_base[0, 0], donor_frac[0, 0], fringe_cell[0, 0]
    nf = start.shape[0]
    slots = base.shape[0]
    cap = slots // blocks
    turned = cap != TILE
    send0, frac0, cells0 = base, frac, cells
    if turned:
        by = jnp.where(on_back, 0, rotation)
        send0, frac0, cells0 = turn(base, cap, by), turn(frac, cap, by), turn(cells, cap, by)
    edges = cap == TILE and 2 * nf == nf * TILE // 128
    row = (1, slots)
    low, high = pack(start, kappa, along)
    left = lax.ppermute(high, "blk", [(i, (i + 1) % blocks) for i in range(blocks)])
    right = lax.ppermute(low, "blk", [((i + 1) % blocks, i) for i in range(blocks)])
    values = interp(rotation_step, start, send0.reshape(row), frac0.reshape(3, 1, slots), TILE, blocks, turned)

    def branch(distance):
        def shift(v, off, blade):
            pairs = [(i, (i + off) % blocks) for i in range(blocks)] if blade else []
            pairs = pairs + [(blocks + i, blocks + (i + distance + off) % blocks) for i in range(blocks)]
            return lax.ppermute(v, ("mesh", "blk"), pairs)

        def run(pay, step, arrived, f1t, fac, base, frac, cells0):
            moved = shift(pay, 0, False)
            values, e = relay(
                step, arrived, cells0.reshape(row), f1t, fac, base.reshape(row), frac.reshape(3, 1, slots), TILE, nf, edges,
                blocks, turned,
            )
            arrived = exchange(values, blocks, cap, nf)
            near = () if edges else (shift(e, 1, True), shift(e, -1, True))
            return arrived, moved, e, shift(e, 0, False), *near

        return run

    values, left, right = lax.optimization_barrier((values, left, right))
    arrived = exchange(values, blocks, cap, nf)
    f1t, pay, fac = march(start, kappa, along, low, high, left, right, cells0.reshape(-1, 128))
    arrived, moved, e, came, *near = lax.switch(
        rotation - 1, [branch(d) for d in range(1, TURN_MOST + 1)], pay, rotation_step, arrived, f1t, fac, base, frac, cells0
    )
    return finish(rotation_step, start.shape, arrived, pay, moved, (e, came, *near), blocks, turned)[None, None]


def solution(mesh):
    placed = (
        P(),
        P("mesh", "blk", None, None, None),
        P("mesh", "blk", None, None, None),
        P("mesh", "blk", None, None),
        P("mesh", "blk", None),
        P("mesh", "blk", None, None),
        P("mesh", "blk", None),
    )
    return jax.shard_map(
        local,
        mesh=mesh,
        in_specs=placed,
        out_specs=P("mesh", "blk", None, None, None),
        check_vma=False,
    )
```

```python
import functools
import jax
import jax.numpy as jnp
from jax import lax
from jax.experimental import pallas as pl
from jax.experimental.pallas import tpu as pltpu
from jax.sharding import PartitionSpec as P

CY = 32
ITERS = 2
TURN_MOST = 7
F32, BF = jnp.float32, jnp.bfloat16
VM = pl.BlockSpec(memory_space=pltpu.VMEM)
SM = pl.BlockSpec(memory_space=pltpu.SMEM)
ANY = pl.BlockSpec(memory_space=pl.ANY)
WHOLE = pltpu.CompilerParams(vmem_limit_bytes=64 * 1024 * 1024)
CP = pltpu.CompilerParams(vmem_limit_bytes=48 * 1024 * 1024)


def split2(v):
    hi = v.astype(BF)
    lo = (v - hi.astype(F32)).astype(BF)
    return hi, lo


def down(v, k):
    return pltpu.roll(v, k, axis=0)
def up(v, k):
    return pltpu.roll(v, v.shape[0] - k, axis=0)

def factor(g_ref, q0, q1, p1, q2, p2, h, iv):
    nz, w = g_ref.shape
    for c in range(0, w, 128):
        s = slice(c, c+128)
        z = lax.broadcasted_iota(jnp.int32, (nz, 128), 0)
        g = g_ref[:, s]
        q = 1.0 / g
        q0[:, s] = q
        qd = jnp.where(z >= 1, down(q, 1), 0.0)
        qu = jnp.where(z < nz-1, up(q, 1), 0.0)
        g = g - qd - qu
        p = jnp.where(z >= 2, qd, 0.0)
        for k, (qr, pr) in ((2, (q1, p1)), (4, (q2, p2))):
            q = 1.0 / g
            qr[:, s] = q
            pr[:, s] = p
            pq = p * q
            ppq = p * pq
            g = g - p * p * down(q, k) - up(ppq, k)
            p = p * down(pq, k)
            p = jnp.where(z >= 2*k, p, 0.0)
        g_ref[:, s] = g
        h[:, s] = p
    prev = None
    for r in range(0, nz, 8):
        g = g_ref[r:r+8, :]
        if prev is None:
            hk = jnp.zeros_like(g)
        else:
            p = h[r:r+8, :]
            hk = p * prev
            g = g - p * hk
        prev = 1.0 / g
        h[r:r+8, :] = hk
        iv[r:r+8, :] = prev

def reduce_rhs(r, s, fs):
    q0, q1, p1, q2, p2 = fs
    nz = r.shape[0]
    z = lax.broadcasted_iota(jnp.int32, r.shape, 0)
    w = q0[:, s] * r
    r = r + jnp.where(z >= 1, down(w, 1), 0.0) + jnp.where(z < nz-1, up(w, 1), 0.0)
    for k, qr, pr in ((2, q1, p1), (4, q2, p2)):
        w = qr[:, s] * r
        p = pr[:, s]
        r = r + p * down(w, k) + up(p * w, k)
    return r


def substitute(y, h, iv, widen):
    nz = y.shape[0]
    prev = y[0:8, :]
    for r in range(8, nz, 8):
        prev = y[r:r+8, :] + widen(h[r:r+8, :]) * prev
        y[r:r+8, :] = prev
    prev = prev * widen(iv[nz-8:nz, :])
    y[nz-8:nz, :] = prev
    for r in range(nz-16, -1, -8):
        prev = y[r:r+8, :] * widen(iv[r:r+8, :]) + widen(h[r+8:r+16, :]) * prev
        y[r:r+8, :] = prev


def same(v):
    return v


def lanes(nz):
    return lax.broadcasted_iota(jnp.int32, (nz, 128), 1)


def on_fringe(lane):
    return (lane % CY == 0) | (lane % CY == CY - 1)


def pack_planes(get, nf, t, x, lane):
    out = None
    for f in range(nf):
        v = get(f, t)
        by = (f - x) * CY % 128
        v = v if by == 0 else pltpu.roll(v, by, axis=1)
        out = v if out is None else jnp.where(lane >= f * CY, v, out)
    return out


def pack_kernel(f_any, kap_any, al_any, lo_any, hi_any, f_ref, kap_ref, al_ref, lo_ref, hi_ref, sems):
    nf, nz, npl = f_ref.shape
    copies = [pltpu.make_async_copy(f_any.at[f], f_ref.at[f], sems.at[f]) for f in range(nf)]
    copies += [pltpu.make_async_copy(kap_any.at[k], kap_ref.at[k], sems.at[nf + k]) for k in range(2)]
    copies += [pltpu.make_async_copy(al_any, al_ref, sems.at[nf + 2])]
    for c in copies:
        c.start()
    lane = lanes(nz)
    per, nt = 128 // CY, npl // 128

    def field(f, t):
        return f_ref[f, :, t*128:(t+1)*128]

    def coef(f, t):
        sl = slice(t*128, (t+1)*128)
        return kap_ref[f, :, sl] if f < 2 else al_ref[:, sl]

    sides = ((lo_ref, lo_any, 0, 0, 1), (hi_ref, hi_any, nt - 1, per - 1, -1))
    back = [pltpu.make_async_copy(ref.at[j], out.at[j], sems.at[nf + 3 + 3 * i + j])
            for i, (ref, out, *_) in enumerate(sides) for j in range(3)]
    for c in copies[:nf]:
        c.wait()
    for i, (ref, _, t, x, step) in enumerate(sides):
        ref[0] = pack_planes(field, nf, t, x, lane)
        back[3 * i].start()
        ref[1] = pack_planes(field, nf, t, x + step, lane)
        back[3 * i + 1].start()
    for c in copies[nf:]:
        c.wait()
    for i, (ref, _, t, x, step) in enumerate(sides):
        ref[2] = pack_planes(coef, 3, t, x, lane)
        back[3 * i + 2].start()
    for c in back:
        c.wait()


def pack(fields, kappa, along):
    nf, nz, npl = fields.shape
    sh = jax.ShapeDtypeStruct((3, nz, nf * CY), F32)
    return pl.pallas_call(
        pack_kernel,
        out_shape=(sh, sh),
        in_specs=[ANY] * 3,
        out_specs=(ANY, ANY),
        scratch_shapes=[pltpu.VMEM(v.shape, F32) for v in (fields, kappa, along, sh, sh)]
        + [pltpu.SemaphoreType.DMA((nf + 9,))],
        compiler_params=WHOLE,
        name="pack",
    )(fields, kappa, along)


def places(turn, tiles, blocks, turned):
    back = lax.axis_index("mesh")
    me = lax.axis_index("blk")
    by = 0 if turned else turn * (1 - back)
    return by, tiles * (1 - back), lax.rem(me + turn * back, blocks), back, lax.rem(me + blocks - turn * back, blocks)


def load_tiles(unroll, o_ref, info_ref, base_ref, frac_ref, a_ref, shift, nf, nz, npl, tile):
    nx = npl // CY
    nt = base_ref.shape[1] // tile
    o_ref[pl.ds(nt - info_ref[1], nt)] = jnp.zeros((nt,) + o_ref.shape[1:], F32)

    def body(t, carry):
        g = t if shift is None else lax.rem(t + shift, nt)
        off = pl.multiple_of(g * tile, tile)
        b = base_ref[0:1, pl.ds(off, tile)]
        fz, fx, fy = [frac_ref[i, :, pl.ds(off, tile)] for i in range(3)]
        z0 = b // npl
        x0 = b // CY % nx
        y0 = b % CY
        iz = lax.broadcasted_iota(jnp.int32, (nz, tile), 0)
        whi, wlo = split2(jnp.where(iz == z0, 1.0 - fz, jnp.where(iz == z0 + 1, fz, 0.0)))
        w = jnp.concatenate([whi, wlo, whi, wlo], axis=0)
        iy = lax.broadcasted_iota(jnp.int32, (CY, tile), 0)
        wy = jnp.where(iy == y0, 1.0 - fy, jnp.where(iy == y0 + 1, fy, 0.0))
        wx = [jnp.where(x0 == x, 1.0 - fx, jnp.where(x0 == x - 1, fx, 0.0)) for x in range(nx)]
        rows = []
        for f in range(nf):
            p = jnp.dot(a_ref[f * npl:(f + 1) * npl, :], w, preferred_element_type=F32)
            acc = wx[0] * p[:CY]
            for x in range(1, nx):
                acc = acc + wx[x] * p[x * CY:(x + 1) * CY]
            r = jnp.sum(acc * wy, axis=0, keepdims=True)
            rows += [r[:, i * 128:(i + 1) * 128] for i in range(tile // 128)]
        o_ref[info_ref[1] + t] = jnp.concatenate(rows, axis=0)
        return carry

    lax.fori_loop(0, nt, body, 0, unroll=unroll)


def split_into(a_ref, row, v):
    n, nz = v.shape
    hi, lo = split2(v)
    for i, part in enumerate((hi, hi, lo, lo)):
        a_ref[row:row + n, i * nz:(i + 1) * nz] = part


def interp_kernel(turn_any, f_any, base_any, frac_any, o_ref, a_ref, f_ref, base_ref, frac_ref, turn_ref, sems, *, tile, blocks, turned):
    nf, nz, npl = f_ref.shape
    copies = [pltpu.make_async_copy(f_any.at[f], f_ref.at[f], sems.at[f]) for f in range(nf)]
    copies += [pltpu.make_async_copy(base_any, base_ref, sems.at[nf])]
    copies += [pltpu.make_async_copy(frac_any, frac_ref, sems.at[nf + 1])]
    copies += [pltpu.make_async_copy(turn_any, turn_ref, sems.at[nf + 2])]
    for c in copies:
        c.start()
    for f in range(nf):
        copies[f].wait()
        split_into(a_ref, f * npl, f_ref[f].T)
    for c in copies[nf:]:
        c.wait()
    info_ref = places(turn_ref[0], base_ref.shape[1] // tile, blocks, turned)
    load_tiles(16, o_ref, info_ref, base_ref, frac_ref, a_ref, info_ref[0], nf, nz, npl, tile)


def interp(turn, fields, base, frac, tile, blocks, turned):
    nf, nz, npl = fields.shape
    slots = base.shape[-1]
    return pl.pallas_call(
        functools.partial(interp_kernel, tile=tile, blocks=blocks, turned=turned),
        out_shape=jax.ShapeDtypeStruct((2 * slots // tile, nf * tile // 128, 128), F32),
        in_specs=[ANY] * 4,
        out_specs=VM,
        scratch_shapes=[pltpu.VMEM((nf * npl, 4 * nz), BF), pltpu.VMEM(fields.shape, F32),
                        pltpu.VMEM(base.shape, jnp.int32), pltpu.VMEM(frac.shape, F32),
                        pltpu.SMEM((1,), jnp.int32), pltpu.SemaphoreType.DMA((nf + 3,))],
        compiler_params=CP,
        name="interp",
    )(turn, fields, base, frac)


def right_sides(start_ref, tiles, hl, hr, kap_ref, si, y, fs, lane):
    nf, nz, npl = start_ref.shape
    nt = npl // 128
    for f in range(nf):
        k = 1 if f == nf - 1 else 0
        v = tiles(f)
        rp = [pltpu.roll(u, CY, axis=1) for u in v]
        rm = [pltpu.roll(u, 128 - CY, axis=1) for u in v]
        left_in = hl if f == 0 else pltpu.roll(hl, 128 - f * CY, axis=1)
        by = (128 - CY - f * CY) % 128
        right_in = hr if by == 0 else pltpu.roll(hr, by, axis=1)
        for t in range(nt):
            left = jnp.where(lane < CY, left_in if t == 0 else rp[t-1], rp[t])
            right = jnp.where(lane >= 128 - CY, right_in if t == nt - 1 else rm[t+1], rm[t])
            side = pltpu.roll(v[t], 1, axis=1) + pltpu.roll(v[t], 127, axis=1)
            sl = slice(t * 128, (t + 1) * 128)
            r = (start_ref[f, :, sl] + kap_ref[k, :, sl] * (left + right + side)) * si[:, sl]
            y[:, f*npl+t*128:f*npl+(t+1)*128] = reduce_rhs(r, slice(k*npl + t*128, k*npl + (t+1)*128), fs)


def march_kernel(start_ref, kap_ref, al_ref, lo_ref, hi_ref, left_ref, right_ref, cells_ref,
                 f1t_ref, pay_ref, fac_ref, y, y2, g, q0, q1, p1, q2, p2, h, iv, si, gs):
    nf, nz, npl = start_ref.shape
    nt = npl // 128
    own = 2 * npl
    lane = lanes(nz)
    fringe = on_fringe(lane)
    inv = 1.0 / al_ref[...]
    si[...] = inv
    for k in range(2):
        g[:, k*npl:(k+1)*npl] = 2.0 + (1.0 + 4.0 * kap_ref[k]) * inv
    outer = []
    for i, (near, mine) in enumerate(((left_ref, lo_ref), (right_ref, hi_ref))):
        c3 = near[2]
        r32, r64, r96 = [pltpu.roll(c3, j, axis=1) for j in (32, 64, 96)]
        c = jnp.where(lane < CY, c3, jnp.where(lane < 2*CY, r32, r64))
        s = jnp.where(lane < CY, r64, jnp.where(lane < 2*CY, r96, jnp.where(lane < 3*CY, c3, r32)))
        inv = 1.0 / s
        g[:, own+i*128:own+(i+1)*128] = 2.0 + (1.0 + 4.0 * c) * inv
        v = near[0]
        z = jnp.where(fringe, 0.0, v)
        side = pltpu.roll(z, 1, axis=1) + pltpu.roll(z, 127, axis=1)
        outer.append((v + c * (near[1] + mine[0] + side)) * inv)
    fs = (q0, q1, p1, q2, p2)
    factor(g, q0, q1, p1, q2, p2, h, iv)

    def clear(v):
        return jnp.where(fringe, 0.0, v)

    right_sides(start_ref, lambda f: [clear(start_ref[f, :, t*128:(t+1)*128]) for t in range(nt)],
                left_ref[0], right_ref[0], kap_ref, si, y, fs, lane)
    for i in range(2):
        y[:, nf*npl+i*128:nf*npl+(i+1)*128] = reduce_rhs(outer[i], slice(own+i*128, own+(i+1)*128), fs)

    def widen(v):
        m, p = v[:, :npl], v[:, npl:own]
        return jnp.concatenate([m] * (nf - 1) + [p, v[:, own:]], axis=1)

    def widen_own(v):
        m, p = v[:, :npl], v[:, npl:own]
        return jnp.concatenate([m] * (nf - 1) + [p], axis=1)

    substitute(y, h, iv, widen)

    def first(f):
        return [clear(y[:, f*npl+t*128:f*npl+(t+1)*128]) for t in range(nt)]

    right_sides(start_ref, first, y[:, nf*npl:nf*npl+128], y[:, nf*npl+128:nf*npl+256], kap_ref, si, y2, fs, lane)
    substitute(y2, h, iv, widen_own)
    for f in range(nf):
        for t in range(nt):
            j = f * nt + t
            pay_ref[j*nz:(j+1)*nz, :] = y2[:, f*npl+t*128:f*npl+(t+1)*128]
    for f in range(nf):
        v = first(f)
        for t in range(nt):
            f1t_ref[f*npl+t*128:f*npl+(t+1)*128, :] = v[t].T
    nx = npl // CY
    half = nf * 2 * nx
    ln = lane % half
    x, side, deep = ln // 2 % nx, ln % 2, jnp.where(lane >= half, 2, 1)
    src = x % (128 // CY) * CY + jnp.where(side == 0, deep, CY - 1 - deep)

    def pick(get):
        out = None
        for t in range(nt):
            v = jnp.take_along_axis(get(t), src, axis=1)
            out = v if out is None else jnp.where(x // (128 // CY) == t, v, out)
        return out

    ck = [pick(lambda t, k=k: kap_ref[k, :, t*128:(t+1)*128]) for k in range(2)]
    c = jnp.where(ln // (2 * nx) == nf - 1, ck[1], ck[0])
    inv = pick(lambda t: si[:, t*128:(t+1)*128])
    cs = c * inv
    gg = 2.0 + (inv + 4.0 * cs)
    j = nf * nt
    pay_ref[j*nz:(j+1)*nz, :] = cs
    pay_ref[(j+1)*nz:(j+2)*nz, :] = gg
    pay_ref[(j+2)*nz:, :] = cells_ref[...].astype(F32)
    gs[...] = gg
    refs = [fac_ref.at[i*nz:(i+1)*nz] for i in range(7)]
    factor(gs, *refs)
    fac_ref[7*nz:, :] = cs


def march(start, kappa, along, low, high, left, right, cells):
    nf, nz, npl = start.shape
    nt = npl // 128
    rows = (nf * nt + 2) * nz + cells.shape[0]
    w = 2 * npl + 256
    return pl.pallas_call(
        march_kernel,
        out_shape=(jax.ShapeDtypeStruct((nf * npl, nz), F32), jax.ShapeDtypeStruct((rows, 128), F32),
                   jax.ShapeDtypeStruct((8 * nz, 128), F32)),
        in_specs=[VM] * 8,
        out_specs=(VM, VM, VM),
        scratch_shapes=[pltpu.VMEM((nz, nf*npl+256), F32), pltpu.VMEM((nz, nf*npl), F32)]
        + [pltpu.VMEM((nz, w), F32)] * 8 + [pltpu.VMEM((nz, npl), F32), pltpu.VMEM((nz, 128), F32)],
        compiler_params=CP,
        name="march",
    )(start, kappa, along, low, high, left, right, cells)


def place_small(shift, arr_ref, row0, cell_row, slots, nf, nz, npl):
    rows = arr_ref.shape[1]
    per = rows // nf
    tile = per * 128
    nt = slots // tile
    nx = npl // CY
    nq = 2 * nx
    zo, av = [], []
    for t in range(nt):
        c = cell_row(lax.rem(t + shift, nt), tile)
        cz = c // npl
        q = c // CY % nx * 2 + c % 2
        zo.append((lax.broadcasted_iota(jnp.int32, (nz, tile), 0) == cz).astype(F32).astype(BF))
        oh = lax.broadcasted_iota(jnp.int32, (nq, tile), 0) == q
        a = arr_ref[row0 + t]
        his, los = [], []
        for f in range(nf):
            row = jnp.concatenate([a[f*per+i:f*per+i+1] for i in range(per)], axis=1)
            hi, lo = split2(jnp.where(oh, row, 0.0))
            his.append(hi)
            los.append(lo)
        av.append(jnp.concatenate(his + los, axis=0))
    zo = jnp.concatenate(zo, axis=1)
    av = jnp.concatenate(av, axis=1)
    return lax.dot_general(zo, av, (((1,), (1,)), ((), ())), preferred_element_type=F32)


def spots(k, nf, npl, low, high):
    nq = 2 * npl // CY
    return k // nq % nf * npl + k % nq // 2 * CY + jnp.where(k % 2 == 0, low, high)


def relay_kernel(turn_ref, arr_ref, cells_ref, f1t_ref, fac_ref, base_ref, frac_ref, o_ref, e_ref, a_ref, ys, *, tile, nf, edges, blocks, turned):
    nz = f1t_ref.shape[1]
    info_ref = places(turn_ref[0], base_ref.shape[1] // tile, blocks, turned)
    npl = f1t_ref.shape[0] // nf
    slots = base_ref.shape[1]
    half = nf * 2 * npl // CY
    lane = lanes(nz)

    def cell_row(g, tile):
        return cells_ref[0:1, pl.ds(pl.multiple_of(g * tile, tile), tile)]

    sm = place_small(info_ref[0], arr_ref, info_ref[1], cell_row, slots, nf, nz, npl)
    fr = sm + pltpu.roll(sm, half, axis=1)
    fac = [fac_ref.at[i*nz:(i+1)*nz] for i in range(8)]
    ys[...] = reduce_rhs(fac[7][...] * fr, slice(0, 128), fac[:5])
    substitute(ys, fac[5], fac[6], same)
    e = ys[...]
    e_ref[...] = e
    hi, lo = split2(e)
    both = jnp.where(lane < half, hi.astype(F32), pltpu.roll(lo.astype(F32), half, axis=1))
    terms = jnp.concatenate([sm.astype(BF), both.astype(BF)], axis=1)
    k = lax.broadcasted_iota(jnp.int32, (1, 256), 1)
    target = jnp.where(k < 128, spots(k, nf, npl, 0, CY - 1), spots(k, nf, npl, 1, CY - 2))
    for f in range(nf):
        row = lax.broadcasted_iota(jnp.int32, (npl, 256), 0) + f * npl
        put = (row == target).astype(F32).astype(BF)
        add = lax.dot_general(put, terms, (((1,), (1,)), ((), ())), preferred_element_type=F32)
        split_into(a_ref, f * npl, f1t_ref[f*npl:(f+1)*npl, :] + add)
    load_tiles(UNROLL, o_ref, info_ref, base_ref, frac_ref, a_ref, None, nf, nz, npl, tile)
    if edges:
        turned = e.T
        nt = slots // tile
        nq = half // nf
        for col, by in ((nq - 2, 1), (0, nt - 1)):
            rows = jnp.concatenate([turned[f*nq+col:f*nq+col+2] for f in range(nf)], axis=0)
            o_ref[nt - info_ref[1] + lax.rem(info_ref[2] + by, nt)] = rows


def relay(turn, arrived, cells, f1t, fac, base, frac, tile, nf, edges, blocks, turned):
    nz = f1t.shape[1]
    return pl.pallas_call(
        functools.partial(relay_kernel, tile=tile, nf=nf, edges=edges, blocks=blocks, turned=turned),
        out_shape=(jax.ShapeDtypeStruct(arrived.shape, F32), jax.ShapeDtypeStruct((nz, 128), F32)),
        in_specs=[SM] + [VM] * 6,
        out_specs=(VM, VM),
        scratch_shapes=[pltpu.VMEM((f1t.shape[0], 4 * nz), BF), pltpu.VMEM((nz, 128), F32)],
        compiler_params=CP,
        name="relay",
    )(turn, arrived, cells, f1t, fac, base, frac)


def finish_kernel(turn_ref, arr_any, own_ref, moved_ref, e_any, came_any, *refs, edges, blocks, turned):
    if edges:
        out_any, *refs = refs
    else:
        el_ref, er_ref, out_any, *refs = refs
    arr_ref, e_ref, o_ref, pay_ref, ys, gs, *fac, sems = refs
    nf, nz, npl = o_ref.shape
    nt = npl // 128
    nx = npl // CY
    nq = 2 * nx
    half = nf * nq
    j = nf * nt
    cells0 = (j + 2) * nz
    slots = (pay_ref.shape[0] - cells0) * 128
    lines = slice(j * nz, pay_ref.shape[0])
    rest = slice(0, j * nz)
    came = pltpu.make_async_copy(arr_any, arr_ref, sems.at[2])
    came.start()

    def copies(ref, e):
        pairs = [(ref.at[s], pay_ref.at[s]) for s in (lines, rest)] + [(e, e_ref)]
        return [pltpu.make_async_copy(a, b, sems.at[i]) for i, (a, b) in zip((0, 1, 3), pairs)]

    back = lax.axis_index("mesh")

    @pl.when(back == 0)
    def _():
        for c in copies(own_ref, e_any):
            c.start()

    @pl.when(back != 0)
    def _():
        for c in copies(moved_ref, came_any):
            c.start()

    info_ref = places(turn_ref[0], arr_ref.shape[0] // 2, blocks, turned)
    held = copies(own_ref, e_any)
    lane = lanes(nz)
    q = lane % nq
    held[0].wait()
    gs[...] = pay_ref[(j+1)*nz:(j+2)*nz, :]
    factor(gs, *fac)
    came.wait()
    held[2].wait()
    e = e_ref[...]
    if edges:
        chunks = arr_ref.shape[0] // 2
        el = arr_ref[chunks - info_ref[1] + lax.rem(info_ref[4] + chunks - 1, chunks)]
        er = arr_ref[chunks - info_ref[1] + lax.rem(info_ref[4] + 1, chunks)]
        none = jnp.zeros((nq - 4, nz), F32)
        parts = []
        for f in range(nf):
            parts += [el[2*f:2*f+2], none, er[2*f:2*f+2]]
        parts = jnp.concatenate(parts, axis=0)
        outer = jnp.concatenate([parts, parts], axis=0).T
        left = right = outer
    else:
        left = pltpu.roll(el_ref[...], 128 - (nq - 2), axis=1)
        right = pltpu.roll(er_ref[...], nq - 2, axis=1)
    left = jnp.where(q < 2, left, pltpu.roll(e, 2, axis=1))
    right = jnp.where(q >= nq - 2, right, pltpu.roll(e, 126, axis=1))
    deep = pltpu.roll(e, half, axis=1)

    def cell_row(g, tile):
        per = tile // 128
        rows = [pay_ref[pl.ds(cells0 + g * per + i, 1), :] for i in range(per)]
        return jnp.concatenate(rows, axis=1).astype(jnp.int32)

    sm = place_small(info_ref[0], arr_ref, info_ref[1], cell_row, slots, nf, nz, npl)
    fr = sm + pltpu.roll(sm, half, axis=1)
    cs = pay_ref[j*nz:(j+1)*nz, :]
    r = cs * jnp.where(lane < half, fr + left + right, deep)
    ys[...] = reduce_rhs(r, slice(0, 128), fac[:5])
    substitute(ys, fac[5], fac[6], same)
    hi, lo = split2(ys[...])
    terms = jnp.concatenate([sm.astype(BF), hi, lo], axis=1)
    k = lax.broadcasted_iota(jnp.int32, (384, 1), 0)
    near = jnp.where(k % 128 < half, 1, 2)
    target = jnp.where(k < 128, spots(k, nf, npl, 0, CY - 1), spots(k, nf, npl, near, CY - 1 - near))
    fringe = on_fringe(lane)
    held[1].wait()
    leave = [pltpu.make_async_copy(o_ref.at[f], out_any.at[f], sems.at[4 + f]) for f in range(nf)]
    for f in range(nf):
        put = (lax.broadcasted_iota(jnp.int32, (384, npl), 1) + f * npl == target).astype(F32).astype(BF)
        add = jnp.dot(terms, put, preferred_element_type=F32)
        for t in range(nt):
            v = pay_ref[(f*nt+t)*nz:(f*nt+t+1)*nz, :]
            o_ref[f, :, t*128:(t+1)*128] = jnp.where(fringe, 0.0, v) + add[:, t*128:(t+1)*128]
        leave[f].start()
    for c in leave:
        c.wait()


def finish(turn, shape, arrived, own, moved, e, blocks, turned):
    nz = shape[1]
    return pl.pallas_call(
        functools.partial(finish_kernel, edges=len(e) == 2, blocks=blocks, turned=turned),
        out_shape=jax.ShapeDtypeStruct(shape, F32),
        in_specs=[SM] + [ANY] * 5 + [VM] * (len(e) - 2),
        out_specs=ANY,
        scratch_shapes=[pltpu.VMEM(v.shape, F32) for v in (arrived, e[0])] + [pltpu.VMEM(shape, F32), pltpu.VMEM(own.shape, F32)]
        + [pltpu.VMEM((nz, 128), F32)] * 9 + [pltpu.SemaphoreType.DMA((4 + shape[0],))],
        compiler_params=WHOLE,
        name="finish",
    )(turn, arrived, own, moved, *e)


TILE = 256
UNROLL = 4


def exchange(values, blocks, cap, nf):
    if cap == TILE:
        return lax.all_to_all(values, ("mesh", "blk"), 0, 0, tiled=True)
    halves = values.reshape(2, -1, nf, TILE).transpose(0, 2, 1, 3).reshape(2, nf, blocks, cap)
    sent = halves.transpose(0, 2, 1, 3).reshape(2 * blocks, nf, cap)
    got = lax.all_to_all(sent, ("mesh", "blk"), 0, 0, tiled=True)
    got = got.reshape(2, blocks, nf, cap).transpose(0, 2, 1, 3).reshape(2, nf, -1, TILE)
    return got.transpose(0, 2, 1, 3).reshape(values.shape)


def turn(values, cap, by):
    groups = values.reshape(values.shape[:-1] + (-1, cap))
    return jnp.roll(groups, -by, axis=-2).reshape(values.shape)


def local(rotation_step, field_state, diffusivity, stretch, donor_base, donor_frac, fringe_cell):
    on_back = lax.axis_index("mesh") == 1
    blocks = lax.axis_size("blk")
    rotation = rotation_step[0]
    start, kappa, along = field_state[0, 0], diffusivity[0, 0], stretch[0, 0]
    base, frac, cells = donor_base[0, 0], donor_frac[0, 0], fringe_cell[0, 0]
    nf = start.shape[0]
    slots = base.shape[0]
    cap = slots // blocks
    turned = cap != TILE
    send0, frac0, cells0 = base, frac, cells
    if turned:
        by = jnp.where(on_back, 0, rotation)
        send0, frac0, cells0 = turn(base, cap, by), turn(frac, cap, by), turn(cells, cap, by)
    edges = cap == TILE and 2 * nf == nf * TILE // 128
    row = (1, slots)
    low, high = pack(start, kappa, along)
    left = lax.ppermute(high, "blk", [(i, (i + 1) % blocks) for i in range(blocks)])
    right = lax.ppermute(low, "blk", [((i + 1) % blocks, i) for i in range(blocks)])
    values = interp(rotation_step, start, send0.reshape(row), frac0.reshape(3, 1, slots), TILE, blocks, turned)

    def branch(distance):
        def shift(v, off, blade):
            pairs = [(i, (i + off) % blocks) for i in range(blocks)] if blade else []
            pairs = pairs + [(blocks + i, blocks + (i + distance + off) % blocks) for i in range(blocks)]
            return lax.ppermute(v, ("mesh", "blk"), pairs)

        def run(pay, step, arrived, f1t, fac, base, frac, cells0):
            moved = shift(pay, 0, False)
            values, e = relay(
                step, arrived, cells0.reshape(row), f1t, fac, base.reshape(row), frac.reshape(3, 1, slots), TILE, nf, edges,
                blocks, turned,
            )
            arrived = exchange(values, blocks, cap, nf)
            near = () if edges else (shift(e, 1, True), shift(e, -1, True))
            return arrived, moved, e, shift(e, 0, False), *near

        return run

    values, left, right = lax.optimization_barrier((values, left, right))
    arrived = exchange(values, blocks, cap, nf)
    f1t, pay, fac = march(start, kappa, along, low, high, left, right, cells0.reshape(-1, 128))
    arrived, moved, e, came, *near = lax.switch(
        rotation - 1, [branch(d) for d in range(1, TURN_MOST + 1)], pay, rotation_step, arrived, f1t, fac, base, frac, cells0
    )
    return finish(rotation_step, start.shape, arrived, pay, moved, (e, came, *near), blocks, turned)[None, None]


def solution(mesh):
    placed = (
        P(),
        P("mesh", "blk", None, None, None),
        P("mesh", "blk", None, None, None),
        P("mesh", "blk", None, None),
        P("mesh", "blk", None),
        P("mesh", "blk", None, None),
        P("mesh", "blk", None),
    )
    return jax.shard_map(
        local,
        mesh=mesh,
        in_specs=placed,
        out_specs=P("mesh", "blk", None, None, None),
        check_vma=False,
    )
```

```python
import functools
import jax
import jax.numpy as jnp
from jax import lax
from jax.experimental import pallas as pl
from jax.experimental.pallas import tpu as pltpu
from jax.sharding import PartitionSpec as P

CY = 32
ITERS = 2
TURN_MOST = 7
F32, BF = jnp.float32, jnp.bfloat16
VM = pl.BlockSpec(memory_space=pltpu.VMEM)
SM = pl.BlockSpec(memory_space=pltpu.SMEM)
ANY = pl.BlockSpec(memory_space=pl.ANY)
WHOLE = pltpu.CompilerParams(vmem_limit_bytes=64 * 1024 * 1024)
CP = pltpu.CompilerParams(vmem_limit_bytes=48 * 1024 * 1024)


def split2(v):
    hi = v.astype(BF)
    lo = (v - hi.astype(F32)).astype(BF)
    return hi, lo


def down(v, k):
    return pltpu.roll(v, k, axis=0)
def up(v, k):
    return pltpu.roll(v, v.shape[0] - k, axis=0)

def factor(g_ref, q0, q1, p1, q2, p2, h, iv):
    nz, w = g_ref.shape
    for c in range(0, w, 128):
        s = slice(c, c+128)
        z = lax.broadcasted_iota(jnp.int32, (nz, 128), 0)
        g = g_ref[:, s]
        q = 1.0 / g
        q0[:, s] = q
        qd = jnp.where(z >= 1, down(q, 1), 0.0)
        qu = jnp.where(z < nz-1, up(q, 1), 0.0)
        g = g - qd - qu
        p = jnp.where(z >= 2, qd, 0.0)
        for k, (qr, pr) in ((2, (q1, p1)), (4, (q2, p2))):
            q = 1.0 / g
            qr[:, s] = q
            pr[:, s] = p
            pq = p * q
            ppq = p * pq
            g = g - p * p * down(q, k) - up(ppq, k)
            p = p * down(pq, k)
            p = jnp.where(z >= 2*k, p, 0.0)
        g_ref[:, s] = g
        h[:, s] = p
    prev = None
    for r in range(0, nz, 8):
        g = g_ref[r:r+8, :]
        if prev is None:
            hk = jnp.zeros_like(g)
        else:
            p = h[r:r+8, :]
            hk = p * prev
            g = g - p * hk
        prev = 1.0 / g
        h[r:r+8, :] = hk
        iv[r:r+8, :] = prev

def reduce_rhs(r, s, fs):
    q0, q1, p1, q2, p2 = fs
    nz = r.shape[0]
    z = lax.broadcasted_iota(jnp.int32, r.shape, 0)
    w = q0[:, s] * r
    r = r + jnp.where(z >= 1, down(w, 1), 0.0) + jnp.where(z < nz-1, up(w, 1), 0.0)
    for k, qr, pr in ((2, q1, p1), (4, q2, p2)):
        w = qr[:, s] * r
        p = pr[:, s]
        r = r + p * down(w, k) + up(p * w, k)
    return r


def substitute(y, h, iv, widen):
    nz = y.shape[0]
    prev = y[0:8, :]
    for r in range(8, nz, 8):
        prev = y[r:r+8, :] + widen(h[r:r+8, :]) * prev
        y[r:r+8, :] = prev
    prev = prev * widen(iv[nz-8:nz, :])
    y[nz-8:nz, :] = prev
    for r in range(nz-16, -1, -8):
        prev = y[r:r+8, :] * widen(iv[r:r+8, :]) + widen(h[r+8:r+16, :]) * prev
        y[r:r+8, :] = prev


def same(v):
    return v


def lanes(nz):
    return lax.broadcasted_iota(jnp.int32, (nz, 128), 1)


def on_fringe(lane):
    return (lane % CY == 0) | (lane % CY == CY - 1)


def pack_planes(get, nf, t, x, lane):
    out = None
    for f in range(nf):
        v = get(f, t)
        by = (f - x) * CY % 128
        v = v if by == 0 else pltpu.roll(v, by, axis=1)
        out = v if out is None else jnp.where(lane >= f * CY, v, out)
    return out


def pack_kernel(f_any, kap_any, al_any, lo_any, hi_any, f_ref, kap_ref, al_ref, lo_ref, hi_ref, sems):
    nf, nz, npl = f_ref.shape
    copies = [pltpu.make_async_copy(f_any.at[f], f_ref.at[f], sems.at[f]) for f in range(nf)]
    copies += [pltpu.make_async_copy(kap_any.at[k], kap_ref.at[k], sems.at[nf + k]) for k in range(2)]
    copies += [pltpu.make_async_copy(al_any, al_ref, sems.at[nf + 2])]
    for c in copies:
        c.start()
    lane = lanes(nz)
    per, nt = 128 // CY, npl // 128

    def field(f, t):
        return f_ref[f, :, t*128:(t+1)*128]

    def coef(f, t):
        sl = slice(t*128, (t+1)*128)
        return kap_ref[f, :, sl] if f < 2 else al_ref[:, sl]

    sides = ((lo_ref, lo_any, 0, 0, 1), (hi_ref, hi_any, nt - 1, per - 1, -1))
    back = [pltpu.make_async_copy(ref.at[j], out.at[j], sems.at[nf + 3 + 3 * i + j])
            for i, (ref, out, *_) in enumerate(sides) for j in range(3)]
    for c in copies[:nf]:
        c.wait()
    for i, (ref, _, t, x, step) in enumerate(sides):
        ref[0] = pack_planes(field, nf, t, x, lane)
        back[3 * i].start()
        ref[1] = pack_planes(field, nf, t, x + step, lane)
        back[3 * i + 1].start()
    for c in copies[nf:]:
        c.wait()
    for i, (ref, _, t, x, step) in enumerate(sides):
        ref[2] = pack_planes(coef, 3, t, x, lane)
        back[3 * i + 2].start()
    for c in back:
        c.wait()


def pack(fields, kappa, along):
    nf, nz, npl = fields.shape
    sh = jax.ShapeDtypeStruct((3, nz, nf * CY), F32)
    return pl.pallas_call(
        pack_kernel,
        out_shape=(sh, sh),
        in_specs=[ANY] * 3,
        out_specs=(ANY, ANY),
        scratch_shapes=[pltpu.VMEM(v.shape, F32) for v in (fields, kappa, along, sh, sh)]
        + [pltpu.SemaphoreType.DMA((nf + 9,))],
        compiler_params=WHOLE,
        name="pack",
    )(fields, kappa, along)


def places(turn, tiles, blocks, turned):
    back = lax.axis_index("mesh")
    me = lax.axis_index("blk")
    by = 0 if turned else turn * (1 - back)
    return by, tiles * (1 - back), lax.rem(me + turn * back, blocks), back, lax.rem(me + blocks - turn * back, blocks)


def load_tiles(unroll, o_ref, info_ref, base_ref, frac_ref, a_ref, shift, nf, nz, npl, tile):
    nx = npl // CY
    nt = base_ref.shape[1] // tile
    o_ref[pl.ds(nt - info_ref[1], nt)] = jnp.zeros((nt,) + o_ref.shape[1:], F32)

    def body(t, carry):
        g = t if shift is None else lax.rem(t + shift, nt)
        off = pl.multiple_of(g * tile, tile)
        b = base_ref[0:1, pl.ds(off, tile)]
        fz, fx, fy = [frac_ref[i, :, pl.ds(off, tile)] for i in range(3)]
        z0 = b // npl
        x0 = b // CY % nx
        y0 = b % CY
        iz = lax.broadcasted_iota(jnp.int32, (nz, tile), 0)
        whi, wlo = split2(jnp.where(iz == z0, 1.0 - fz, jnp.where(iz == z0 + 1, fz, 0.0)))
        w = jnp.concatenate([whi, wlo, whi, wlo], axis=0)
        iy = lax.broadcasted_iota(jnp.int32, (CY, tile), 0)
        wy = jnp.where(iy == y0, 1.0 - fy, jnp.where(iy == y0 + 1, fy, 0.0))
        wx = [jnp.where(x0 == x, 1.0 - fx, jnp.where(x0 == x - 1, fx, 0.0)) for x in range(nx)]
        rows = []
        for f in range(nf):
            p = jnp.dot(a_ref[f * npl:(f + 1) * npl, :], w, preferred_element_type=F32)
            acc = wx[0] * p[:CY]
            for x in range(1, nx):
                acc = acc + wx[x] * p[x * CY:(x + 1) * CY]
            r = jnp.sum(acc * wy, axis=0, keepdims=True)
            rows += [r[:, i * 128:(i + 1) * 128] for i in range(tile // 128)]
        o_ref[info_ref[1] + t] = jnp.concatenate(rows, axis=0)
        return carry

    lax.fori_loop(0, nt, body, 0, unroll=unroll)


def split_into(a_ref, row, v):
    n, nz = v.shape
    hi, lo = split2(v)
    for i, part in enumerate((hi, hi, lo, lo)):
        a_ref[row:row + n, i * nz:(i + 1) * nz] = part


def interp_kernel(turn_any, f_any, base_any, frac_any, o_ref, a_ref, f_ref, base_ref, frac_ref, turn_ref, sems, *, tile, blocks, turned):
    nf, nz, npl = f_ref.shape
    copies = [pltpu.make_async_copy(f_any.at[f], f_ref.at[f], sems.at[f]) for f in range(nf)]
    copies += [pltpu.make_async_copy(base_any, base_ref, sems.at[nf])]
    copies += [pltpu.make_async_copy(frac_any, frac_ref, sems.at[nf + 1])]
    copies += [pltpu.make_async_copy(turn_any, turn_ref, sems.at[nf + 2])]
    for c in copies:
        c.start()
    for f in range(nf):
        copies[f].wait()
        split_into(a_ref, f * npl, f_ref[f].T)
    for c in copies[nf:]:
        c.wait()
    info_ref = places(turn_ref[0], base_ref.shape[1] // tile, blocks, turned)
    load_tiles(16, o_ref, info_ref, base_ref, frac_ref, a_ref, info_ref[0], nf, nz, npl, tile)


def interp(turn, fields, base, frac, tile, blocks, turned):
    nf, nz, npl = fields.shape
    slots = base.shape[-1]
    return pl.pallas_call(
        functools.partial(interp_kernel, tile=tile, blocks=blocks, turned=turned),
        out_shape=jax.ShapeDtypeStruct((2 * slots // tile, nf * tile // 128, 128), F32),
        in_specs=[ANY] * 4,
        out_specs=VM,
        scratch_shapes=[pltpu.VMEM((nf * npl, 4 * nz), BF), pltpu.VMEM(fields.shape, F32),
                        pltpu.VMEM(base.shape, jnp.int32), pltpu.VMEM(frac.shape, F32),
                        pltpu.SMEM((1,), jnp.int32), pltpu.SemaphoreType.DMA((nf + 3,))],
        compiler_params=CP,
        name="interp",
    )(turn, fields, base, frac)


def right_sides(start_ref, tiles, hl, hr, kap_ref, si, y, fs, lane):
    nf, nz, npl = start_ref.shape
    nt = npl // 128
    for f in range(nf):
        k = 1 if f == nf - 1 else 0
        v = tiles(f)
        rp = [pltpu.roll(u, CY, axis=1) for u in v]
        rm = [pltpu.roll(u, 128 - CY, axis=1) for u in v]
        left_in = hl if f == 0 else pltpu.roll(hl, 128 - f * CY, axis=1)
        by = (128 - CY - f * CY) % 128
        right_in = hr if by == 0 else pltpu.roll(hr, by, axis=1)
        for t in range(nt):
            left = jnp.where(lane < CY, left_in if t == 0 else rp[t-1], rp[t])
            right = jnp.where(lane >= 128 - CY, right_in if t == nt - 1 else rm[t+1], rm[t])
            side = pltpu.roll(v[t], 1, axis=1) + pltpu.roll(v[t], 127, axis=1)
            sl = slice(t * 128, (t + 1) * 128)
            r = (start_ref[f, :, sl] + kap_ref[k, :, sl] * (left + right + side)) * si[:, sl]
            y[:, f*npl+t*128:f*npl+(t+1)*128] = reduce_rhs(r, slice(k*npl + t*128, k*npl + (t+1)*128), fs)


def march_kernel(start_ref, kap_ref, al_ref, lo_ref, hi_ref, left_ref, right_ref, cells_ref,
                 f1t_ref, pay_ref, fac_ref, y, y2, g, q0, q1, p1, q2, p2, h, iv, si, gs):
    nf, nz, npl = start_ref.shape
    nt = npl // 128
    own = 2 * npl
    lane = lanes(nz)
    fringe = on_fringe(lane)
    inv = 1.0 / al_ref[...]
    si[...] = inv
    for k in range(2):
        g[:, k*npl:(k+1)*npl] = 2.0 + (1.0 + 4.0 * kap_ref[k]) * inv
    outer = []
    for i, (near, mine) in enumerate(((left_ref, lo_ref), (right_ref, hi_ref))):
        c3 = near[2]
        r32, r64, r96 = [pltpu.roll(c3, j, axis=1) for j in (32, 64, 96)]
        c = jnp.where(lane < CY, c3, jnp.where(lane < 2*CY, r32, r64))
        s = jnp.where(lane < CY, r64, jnp.where(lane < 2*CY, r96, jnp.where(lane < 3*CY, c3, r32)))
        inv = 1.0 / s
        g[:, own+i*128:own+(i+1)*128] = 2.0 + (1.0 + 4.0 * c) * inv
        v = near[0]
        z = jnp.where(fringe, 0.0, v)
        side = pltpu.roll(z, 1, axis=1) + pltpu.roll(z, 127, axis=1)
        outer.append((v + c * (near[1] + mine[0] + side)) * inv)
    fs = (q0, q1, p1, q2, p2)
    factor(g, q0, q1, p1, q2, p2, h, iv)

    def clear(v):
        return jnp.where(fringe, 0.0, v)

    right_sides(start_ref, lambda f: [clear(start_ref[f, :, t*128:(t+1)*128]) for t in range(nt)],
                left_ref[0], right_ref[0], kap_ref, si, y, fs, lane)
    for i in range(2):
        y[:, nf*npl+i*128:nf*npl+(i+1)*128] = reduce_rhs(outer[i], slice(own+i*128, own+(i+1)*128), fs)

    def widen(v):
        m, p = v[:, :npl], v[:, npl:own]
        return jnp.concatenate([m] * (nf - 1) + [p, v[:, own:]], axis=1)

    def widen_own(v):
        m, p = v[:, :npl], v[:, npl:own]
        return jnp.concatenate([m] * (nf - 1) + [p], axis=1)

    substitute(y, h, iv, widen)

    def first(f):
        return [clear(y[:, f*npl+t*128:f*npl+(t+1)*128]) for t in range(nt)]

    right_sides(start_ref, first, y[:, nf*npl:nf*npl+128], y[:, nf*npl+128:nf*npl+256], kap_ref, si, y2, fs, lane)
    substitute(y2, h, iv, widen_own)
    for f in range(nf):
        for t in range(nt):
            j = f * nt + t
            pay_ref[j*nz:(j+1)*nz, :] = y2[:, f*npl+t*128:f*npl+(t+1)*128]
    for f in range(nf):
        v = first(f)
        for t in range(nt):
            f1t_ref[f*npl+t*128:f*npl+(t+1)*128, :] = v[t].T
    nx = npl // CY
    half = nf * 2 * nx
    ln = lane % half
    x, side, deep = ln // 2 % nx, ln % 2, jnp.where(lane >= half, 2, 1)
    src = x % (128 // CY) * CY + jnp.where(side == 0, deep, CY - 1 - deep)

    def pick(get):
        out = None
        for t in range(nt):
            v = jnp.take_along_axis(get(t), src, axis=1)
            out = v if out is None else jnp.where(x // (128 // CY) == t, v, out)
        return out

    ck = [pick(lambda t, k=k: kap_ref[k, :, t*128:(t+1)*128]) for k in range(2)]
    c = jnp.where(ln // (2 * nx) == nf - 1, ck[1], ck[0])
    inv = pick(lambda t: si[:, t*128:(t+1)*128])
    cs = c * inv
    gg = 2.0 + (inv + 4.0 * cs)
    j = nf * nt
    few = (lane // (4 * nx) % 2) * (nf - 1) * 2 * nx + (lane // (2 * nx) % 2) * half + ln % (2 * nx)
    pay_ref[j*nz:(j+1)*nz, :] = jnp.where(
        lane < half, jnp.take_along_axis(cs, few, axis=1), jnp.take_along_axis(gg, few, axis=1))
    pay_ref[(j+1)*nz:, :] = cells_ref[...].astype(F32)
    gs[...] = gg
    refs = [fac_ref.at[i*nz:(i+1)*nz] for i in range(7)]
    factor(gs, *refs)
    fac_ref[7*nz:, :] = cs


def march(start, kappa, along, low, high, left, right, cells):
    nf, nz, npl = start.shape
    nt = npl // 128
    rows = (nf * nt + 1) * nz + cells.shape[0]
    w = 2 * npl + 256
    return pl.pallas_call(
        march_kernel,
        out_shape=(jax.ShapeDtypeStruct((nf * npl, nz), F32), jax.ShapeDtypeStruct((rows, 128), F32),
                   jax.ShapeDtypeStruct((8 * nz, 128), F32)),
        in_specs=[VM] * 8,
        out_specs=(VM, VM, VM),
        scratch_shapes=[pltpu.VMEM((nz, nf*npl+256), F32), pltpu.VMEM((nz, nf*npl), F32)]
        + [pltpu.VMEM((nz, w), F32)] * 8 + [pltpu.VMEM((nz, npl), F32), pltpu.VMEM((nz, 128), F32)],
        compiler_params=CP,
        name="march",
    )(start, kappa, along, low, high, left, right, cells)


def place_small(shift, arr_ref, row0, cell_row, slots, nf, nz, npl):
    rows = arr_ref.shape[1]
    per = rows // nf
    tile = per * 128
    nt = slots // tile
    nx = npl // CY
    nq = 2 * nx
    zo, av = [], []
    for t in range(nt):
        c = cell_row(lax.rem(t + shift, nt), tile)
        cz = c // npl
        q = c // CY % nx * 2 + c % 2
        zo.append((lax.broadcasted_iota(jnp.int32, (nz, tile), 0) == cz).astype(F32).astype(BF))
        oh = lax.broadcasted_iota(jnp.int32, (nq, tile), 0) == q
        a = arr_ref[row0 + t]
        his, los = [], []
        for f in range(nf):
            row = jnp.concatenate([a[f*per+i:f*per+i+1] for i in range(per)], axis=1)
            hi, lo = split2(jnp.where(oh, row, 0.0))
            his.append(hi)
            los.append(lo)
        av.append(jnp.concatenate(his + los, axis=0))
    zo = jnp.concatenate(zo, axis=1)
    av = jnp.concatenate(av, axis=1)
    return lax.dot_general(zo, av, (((1,), (1,)), ((), ())), preferred_element_type=F32)


def spots(k, nf, npl, low, high):
    nq = 2 * npl // CY
    return k // nq % nf * npl + k % nq // 2 * CY + jnp.where(k % 2 == 0, low, high)


def relay_kernel(turn_ref, arr_ref, cells_ref, f1t_ref, fac_ref, base_ref, frac_ref, o_ref, e_ref, a_ref, ys, *, tile, nf, edges, blocks, turned):
    nz = f1t_ref.shape[1]
    info_ref = places(turn_ref[0], base_ref.shape[1] // tile, blocks, turned)
    npl = f1t_ref.shape[0] // nf
    slots = base_ref.shape[1]
    half = nf * 2 * npl // CY
    lane = lanes(nz)

    def cell_row(g, tile):
        return cells_ref[0:1, pl.ds(pl.multiple_of(g * tile, tile), tile)]

    sm = place_small(info_ref[0], arr_ref, info_ref[1], cell_row, slots, nf, nz, npl)
    fr = sm + pltpu.roll(sm, half, axis=1)
    fac = [fac_ref.at[i*nz:(i+1)*nz] for i in range(8)]
    ys[...] = reduce_rhs(fac[7][...] * fr, slice(0, 128), fac[:5])
    substitute(ys, fac[5], fac[6], same)
    e = ys[...]
    low = lax.broadcasted_iota(jnp.int32, (nz // 2, 128), 1) < half
    e_ref[...] = jnp.where(low, e[:nz//2], pltpu.roll(e[nz//2:], half, axis=1))
    hi, lo = split2(e)
    both = jnp.where(lane < half, hi.astype(F32), pltpu.roll(lo.astype(F32), half, axis=1))
    terms = jnp.concatenate([sm.astype(BF), both.astype(BF)], axis=1)
    k = lax.broadcasted_iota(jnp.int32, (1, 256), 1)
    target = jnp.where(k < 128, spots(k, nf, npl, 0, CY - 1), spots(k, nf, npl, 1, CY - 2))
    for f in range(nf):
        row = lax.broadcasted_iota(jnp.int32, (npl, 256), 0) + f * npl
        put = (row == target).astype(F32).astype(BF)
        add = lax.dot_general(put, terms, (((1,), (1,)), ((), ())), preferred_element_type=F32)
        split_into(a_ref, f * npl, f1t_ref[f*npl:(f+1)*npl, :] + add)
    load_tiles(UNROLL, o_ref, info_ref, base_ref, frac_ref, a_ref, None, nf, nz, npl, tile)
    if edges:
        turned = e.T
        nt = slots // tile
        nq = half // nf
        for col, by in ((nq - 2, 1), (0, nt - 1)):
            rows = jnp.concatenate([turned[f*nq+col:f*nq+col+2] for f in range(nf)], axis=0)
            o_ref[nt - info_ref[1] + lax.rem(info_ref[2] + by, nt)] = rows


def relay(turn, arrived, cells, f1t, fac, base, frac, tile, nf, edges, blocks, turned):
    nz = f1t.shape[1]
    return pl.pallas_call(
        functools.partial(relay_kernel, tile=tile, nf=nf, edges=edges, blocks=blocks, turned=turned),
        out_shape=(jax.ShapeDtypeStruct(arrived.shape, F32), jax.ShapeDtypeStruct((nz // 2, 128), F32)),
        in_specs=[SM] + [VM] * 6,
        out_specs=(VM, VM),
        scratch_shapes=[pltpu.VMEM((f1t.shape[0], 4 * nz), BF), pltpu.VMEM((nz, 128), F32)],
        compiler_params=CP,
        name="relay",
    )(turn, arrived, cells, f1t, fac, base, frac)


def unfold(v):
    return jnp.concatenate([v, pltpu.roll(v, 64, axis=1)], axis=0)


def finish_kernel(turn_ref, arr_any, own_ref, moved_ref, e_any, came_any, *refs, edges, blocks, turned):
    if edges:
        out_any, *refs = refs
    else:
        el_ref, er_ref, out_any, *refs = refs
    arr_ref, e_ref, o_ref, pay_ref, ys, gs, *fac, sems = refs
    nf, nz, npl = o_ref.shape
    nt = npl // 128
    nx = npl // CY
    nq = 2 * nx
    half = nf * nq
    j = nf * nt
    cells0 = (j + 1) * nz
    slots = (pay_ref.shape[0] - cells0) * 128
    lines = slice(j * nz, pay_ref.shape[0])
    rest = slice(0, j * nz)
    came = pltpu.make_async_copy(arr_any, arr_ref, sems.at[2])
    came.start()

    def copies(ref, e):
        pairs = [(ref.at[s], pay_ref.at[s]) for s in (lines, rest)] + [(e, e_ref)]
        return [pltpu.make_async_copy(a, b, sems.at[i]) for i, (a, b) in zip((0, 1, 3), pairs)]

    back = lax.axis_index("mesh")

    @pl.when(back == 0)
    def _():
        for c in copies(own_ref, e_any):
            c.start()

    @pl.when(back != 0)
    def _():
        for c in copies(moved_ref, came_any):
            c.start()

    info_ref = places(turn_ref[0], arr_ref.shape[0] // 2, blocks, turned)
    held = copies(own_ref, e_any)
    lane = lanes(nz)
    q = lane % nq
    held[0].wait()
    ln = lane % half
    few = ln // nq // (nf - 1) * 2 * nq + lane // half * nq + ln % nq
    table = pay_ref[j*nz:(j+1)*nz, :]
    cs = jnp.take_along_axis(table, few, axis=1)
    gs[...] = jnp.take_along_axis(table, few + half, axis=1)
    factor(gs, *fac)
    came.wait()
    held[2].wait()
    e = unfold(e_ref[...])
    if edges:
        chunks = arr_ref.shape[0] // 2
        el = arr_ref[chunks - info_ref[1] + lax.rem(info_ref[4] + chunks - 1, chunks)]
        er = arr_ref[chunks - info_ref[1] + lax.rem(info_ref[4] + 1, chunks)]
        none = jnp.zeros((nq - 4, nz), F32)
        parts = []
        for f in range(nf):
            parts += [el[2*f:2*f+2], none, er[2*f:2*f+2]]
        parts = jnp.concatenate(parts, axis=0)
        outer = jnp.concatenate([parts, parts], axis=0).T
        left = right = outer
    else:
        left = pltpu.roll(unfold(el_ref[...]), 128 - (nq - 2), axis=1)
        right = pltpu.roll(unfold(er_ref[...]), nq - 2, axis=1)
    left = jnp.where(q < 2, left, pltpu.roll(e, 2, axis=1))
    right = jnp.where(q >= nq - 2, right, pltpu.roll(e, 126, axis=1))
    deep = pltpu.roll(e, half, axis=1)

    def cell_row(g, tile):
        per = tile // 128
        rows = [pay_ref[pl.ds(cells0 + g * per + i, 1), :] for i in range(per)]
        return jnp.concatenate(rows, axis=1).astype(jnp.int32)

    sm = place_small(info_ref[0], arr_ref, info_ref[1], cell_row, slots, nf, nz, npl)
    fr = sm + pltpu.roll(sm, half, axis=1)
    r = cs * jnp.where(lane < half, fr + left + right, deep)
    ys[...] = reduce_rhs(r, slice(0, 128), fac[:5])
    substitute(ys, fac[5], fac[6], same)
    hi, lo = split2(ys[...])
    terms = jnp.concatenate([sm.astype(BF), hi, lo], axis=1)
    k = lax.broadcasted_iota(jnp.int32, (384, 1), 0)
    near = jnp.where(k % 128 < half, 1, 2)
    target = jnp.where(k < 128, spots(k, nf, npl, 0, CY - 1), spots(k, nf, npl, near, CY - 1 - near))
    fringe = on_fringe(lane)
    held[1].wait()
    leave = [pltpu.make_async_copy(o_ref.at[f], out_any.at[f], sems.at[4 + f]) for f in range(nf)]
    for f in range(nf):
        put = (lax.broadcasted_iota(jnp.int32, (384, npl), 1) + f * npl == target).astype(F32).astype(BF)
        add = jnp.dot(terms, put, preferred_element_type=F32)
        for t in range(nt):
            v = pay_ref[(f*nt+t)*nz:(f*nt+t+1)*nz, :]
            o_ref[f, :, t*128:(t+1)*128] = jnp.where(fringe, 0.0, v) + add[:, t*128:(t+1)*128]
        leave[f].start()
    for c in leave:
        c.wait()


def finish(turn, shape, arrived, own, moved, e, blocks, turned):
    nz = shape[1]
    return pl.pallas_call(
        functools.partial(finish_kernel, edges=len(e) == 2, blocks=blocks, turned=turned),
        out_shape=jax.ShapeDtypeStruct(shape, F32),
        in_specs=[SM] + [ANY] * 5 + [VM] * (len(e) - 2),
        out_specs=ANY,
        scratch_shapes=[pltpu.VMEM(v.shape, F32) for v in (arrived, e[0])] + [pltpu.VMEM(shape, F32), pltpu.VMEM(own.shape, F32)]
        + [pltpu.VMEM((nz, 128), F32)] * 9 + [pltpu.SemaphoreType.DMA((4 + shape[0],))],
        compiler_params=CP,
        name="finish",
    )(turn, arrived, own, moved, *e)


TILE = 256
UNROLL = 4


def exchange(values, blocks, cap, nf):
    if cap == TILE:
        return lax.all_to_all(values, ("mesh", "blk"), 0, 0, tiled=True)
    halves = values.reshape(2, -1, nf, TILE).transpose(0, 2, 1, 3).reshape(2, nf, blocks, cap)
    sent = halves.transpose(0, 2, 1, 3).reshape(2 * blocks, nf, cap)
    got = lax.all_to_all(sent, ("mesh", "blk"), 0, 0, tiled=True)
    got = got.reshape(2, blocks, nf, cap).transpose(0, 2, 1, 3).reshape(2, nf, -1, TILE)
    return got.transpose(0, 2, 1, 3).reshape(values.shape)


def turn(values, cap, by):
    groups = values.reshape(values.shape[:-1] + (-1, cap))
    return jnp.roll(groups, -by, axis=-2).reshape(values.shape)


def local(rotation_step, field_state, diffusivity, stretch, donor_base, donor_frac, fringe_cell):
    on_back = lax.axis_index("mesh") == 1
    blocks = lax.axis_size("blk")
    rotation = rotation_step[0]
    start, kappa, along = field_state[0, 0], diffusivity[0, 0], stretch[0, 0]
    base, frac, cells = donor_base[0, 0], donor_frac[0, 0], fringe_cell[0, 0]
    nf = start.shape[0]
    slots = base.shape[0]
    cap = slots // blocks
    turned = cap != TILE
    send0, frac0, cells0 = base, frac, cells
    if turned:
        by = jnp.where(on_back, 0, rotation)
        send0, frac0, cells0 = turn(base, cap, by), turn(frac, cap, by), turn(cells, cap, by)
    edges = cap == TILE and 2 * nf == nf * TILE // 128
    row = (1, slots)
    low, high = pack(start, kappa, along)
    left = lax.ppermute(high, "blk", [(i, (i + 1) % blocks) for i in range(blocks)])
    right = lax.ppermute(low, "blk", [((i + 1) % blocks, i) for i in range(blocks)])
    values = interp(rotation_step, start, send0.reshape(row), frac0.reshape(3, 1, slots), TILE, blocks, turned)

    def branch(distance):
        def shift(v, off, blade):
            pairs = [(i, (i + off) % blocks) for i in range(blocks)] if blade else []
            pairs = pairs + [(blocks + i, blocks + (i + distance + off) % blocks) for i in range(blocks)]
            return lax.ppermute(v, ("mesh", "blk"), pairs)

        def run(pay, step, arrived, f1t, fac, base, frac, cells0):
            moved = shift(pay, 0, False)
            values, e = relay(
                step, arrived, cells0.reshape(row), f1t, fac, base.reshape(row), frac.reshape(3, 1, slots), TILE, nf, edges,
                blocks, turned,
            )
            arrived = exchange(values, blocks, cap, nf)
            near = () if edges else (shift(e, 1, True), shift(e, -1, True))
            return arrived, moved, e, shift(e, 0, False), *near

        return run

    values, left, right = lax.optimization_barrier((values, left, right))
    arrived = exchange(values, blocks, cap, nf)
    f1t, pay, fac = march(start, kappa, along, low, high, left, right, cells0.reshape(-1, 128))
    arrived, moved, e, came, *near = lax.switch(
        rotation - 1, [branch(d) for d in range(1, TURN_MOST + 1)], pay, rotation_step, arrived, f1t, fac, base, frac, cells0
    )
    return finish(rotation_step, start.shape, arrived, pay, moved, (e, came, *near), blocks, turned)[None, None]


def solution(mesh):
    placed = (
        P(),
        P("mesh", "blk", None, None, None),
        P("mesh", "blk", None, None, None),
        P("mesh", "blk", None, None),
        P("mesh", "blk", None),
        P("mesh", "blk", None, None),
        P("mesh", "blk", None),
    )
    return jax.shard_map(
        local,
        mesh=mesh,
        in_specs=placed,
        out_specs=P("mesh", "blk", None, None, None),
        check_vma=False,
    )
```

```python
import functools
import jax
import jax.numpy as jnp
from jax import lax
from jax.experimental import pallas as pl
from jax.experimental.pallas import tpu as pltpu
from jax.sharding import PartitionSpec as P

CY = 32
ITERS = 2
TURN_MOST = 7
F32, BF = jnp.float32, jnp.bfloat16
VM = pl.BlockSpec(memory_space=pltpu.VMEM)
SM = pl.BlockSpec(memory_space=pltpu.SMEM)
ANY = pl.BlockSpec(memory_space=pl.ANY)
WHOLE = pltpu.CompilerParams(vmem_limit_bytes=64 * 1024 * 1024)
CP = pltpu.CompilerParams(vmem_limit_bytes=48 * 1024 * 1024)


def split2(v):
    hi = v.astype(BF)
    lo = (v - hi.astype(F32)).astype(BF)
    return hi, lo


def down(v, k):
    return pltpu.roll(v, k, axis=0)
def up(v, k):
    return pltpu.roll(v, v.shape[0] - k, axis=0)

def factor(g_ref, q0, q1, p1, q2, p2, h, iv):
    nz, w = g_ref.shape
    for c in range(0, w, 128):
        s = slice(c, c+128)
        z = lax.broadcasted_iota(jnp.int32, (nz, 128), 0)
        g = g_ref[:, s]
        q = 1.0 / g
        q0[:, s] = q
        qd = jnp.where(z >= 1, down(q, 1), 0.0)
        qu = jnp.where(z < nz-1, up(q, 1), 0.0)
        g = g - qd - qu
        p = jnp.where(z >= 2, qd, 0.0)
        for k, (qr, pr) in ((2, (q1, p1)), (4, (q2, p2))):
            q = 1.0 / g
            qr[:, s] = q
            pr[:, s] = p
            pq = p * q
            ppq = p * pq
            g = g - p * p * down(q, k) - up(ppq, k)
            p = p * down(pq, k)
            p = jnp.where(z >= 2*k, p, 0.0)
        g_ref[:, s] = g
        h[:, s] = p
    prev = None
    for r in range(0, nz, 8):
        g = g_ref[r:r+8, :]
        if prev is None:
            hk = jnp.zeros_like(g)
        else:
            p = h[r:r+8, :]
            hk = p * prev
            g = g - p * hk
        prev = 1.0 / g
        h[r:r+8, :] = hk
        iv[r:r+8, :] = prev

def reduce_rhs(r, s, fs):
    q0, q1, p1, q2, p2 = fs
    nz = r.shape[0]
    z = lax.broadcasted_iota(jnp.int32, r.shape, 0)
    w = q0[:, s] * r
    r = r + jnp.where(z >= 1, down(w, 1), 0.0) + jnp.where(z < nz-1, up(w, 1), 0.0)
    for k, qr, pr in ((2, q1, p1), (4, q2, p2)):
        w = qr[:, s] * r
        p = pr[:, s]
        r = r + p * down(w, k) + up(p * w, k)
    return r


def substitute(y, h, iv, widen):
    nz = y.shape[0]
    prev = y[0:8, :]
    for r in range(8, nz, 8):
        prev = y[r:r+8, :] + widen(h[r:r+8, :]) * prev
        y[r:r+8, :] = prev
    prev = prev * widen(iv[nz-8:nz, :])
    y[nz-8:nz, :] = prev
    for r in range(nz-16, -1, -8):
        prev = y[r:r+8, :] * widen(iv[r:r+8, :]) + widen(h[r+8:r+16, :]) * prev
        y[r:r+8, :] = prev


def same(v):
    return v


def lanes(nz):
    return lax.broadcasted_iota(jnp.int32, (nz, 128), 1)


def on_fringe(lane):
    return (lane % CY == 0) | (lane % CY == CY - 1)


def pack_planes(get, nf, t, x, lane):
    out = None
    for f in range(nf):
        v = get(f, t)
        by = (f - x) * CY % 128
        v = v if by == 0 else pltpu.roll(v, by, axis=1)
        out = v if out is None else jnp.where(lane >= f * CY, v, out)
    return out


def fold(v):
    n = v.shape[0] // 4
    tail = jnp.concatenate([pltpu.roll(v[3*n:], 128 - CY - i * CY, axis=1) for i in range(3)], axis=0)
    lane = lax.broadcasted_iota(jnp.int32, tail.shape, 1)
    return jnp.where(lane < 3 * CY, v[:3*n], tail)


def unfold3(v):
    n = v.shape[0] // 3
    a, b, c = [pltpu.roll(v[i*n:(i+1)*n], (i + 1) * CY, axis=1) for i in range(3)]
    lane = lax.broadcasted_iota(jnp.int32, a.shape, 1)
    return jnp.concatenate([v, jnp.where(lane < CY, a, jnp.where(lane < 2 * CY, b, c))], axis=0)


def pack_kernel(f_any, kap_any, al_any, lo_any, hi_any, f_ref, kap_ref, al_ref, lo_ref, hi_ref, sems):
    nf, nz, npl = f_ref.shape
    copies = [pltpu.make_async_copy(f_any.at[f], f_ref.at[f], sems.at[f]) for f in range(nf)]
    copies += [pltpu.make_async_copy(kap_any.at[k], kap_ref.at[k], sems.at[nf + k]) for k in range(2)]
    copies += [pltpu.make_async_copy(al_any, al_ref, sems.at[nf + 2])]
    for c in copies:
        c.start()
    lane = lanes(nz)
    per, nt = 128 // CY, npl // 128

    def field(f, t):
        return f_ref[f, :, t*128:(t+1)*128]

    def coef(f, t):
        sl = slice(t*128, (t+1)*128)
        return kap_ref[f, :, sl] if f < 2 else al_ref[:, sl]

    sides = ((lo_ref, lo_any, 0, 0, 1), (hi_ref, hi_any, nt - 1, per - 1, -1))
    parts = [slice(0, nz), slice(nz, 2 * nz), slice(2 * nz, 2 * nz + nz * 3 // 4)]
    back = [pltpu.make_async_copy(ref.at[p], out.at[p], sems.at[nf + 3 + 3 * i + j])
            for i, (ref, out, *_) in enumerate(sides) for j, p in enumerate(parts)]
    for c in copies[:nf]:
        c.wait()
    for i, (ref, _, t, x, step) in enumerate(sides):
        ref[parts[0]] = pack_planes(field, nf, t, x, lane)
        back[3 * i].start()
        ref[parts[1]] = pack_planes(field, nf, t, x + step, lane)
        back[3 * i + 1].start()
    for c in copies[nf:]:
        c.wait()
    for i, (ref, _, t, x, step) in enumerate(sides):
        ref[parts[2]] = fold(pack_planes(coef, 3, t, x, lane))
        back[3 * i + 2].start()
    for c in back:
        c.wait()


def pack(fields, kappa, along):
    nf, nz, npl = fields.shape
    sh = jax.ShapeDtypeStruct((2 * nz + nz * 3 // 4, nf * CY), F32)
    return pl.pallas_call(
        pack_kernel,
        out_shape=(sh, sh),
        in_specs=[ANY] * 3,
        out_specs=(ANY, ANY),
        scratch_shapes=[pltpu.VMEM(v.shape, F32) for v in (fields, kappa, along, sh, sh)]
        + [pltpu.SemaphoreType.DMA((nf + 9,))],
        compiler_params=WHOLE,
        name="pack",
    )(fields, kappa, along)


def places(turn, tiles, blocks, turned):
    back = lax.axis_index("mesh")
    me = lax.axis_index("blk")
    by = 0 if turned else turn * (1 - back)
    return by, tiles * (1 - back), lax.rem(me + turn * back, blocks), back, lax.rem(me + blocks - turn * back, blocks)


def load_tiles(unroll, o_ref, info_ref, base_ref, frac_ref, a_ref, shift, nf, nz, npl, tile, t_ref=None):
    nx = npl // CY
    nt = base_ref.shape[1] // tile
    o_ref[pl.ds(nt - info_ref[1], nt)] = jnp.zeros((nt,) + o_ref.shape[1:], F32)

    def body(t, carry):
        g = t if shift is None else lax.rem(t + shift, nt)
        off = pl.multiple_of(g * tile, tile)
        b = base_ref[0:1, pl.ds(off, tile)]
        fz, fx, fy = [frac_ref[i, :, pl.ds(off, tile)] for i in range(3)]
        z0 = b // npl
        x0 = b // CY % nx
        y0 = b % CY
        iz = lax.broadcasted_iota(jnp.int32, (nz, tile), 0)
        whi, wlo = split2(jnp.where(iz == z0, 1.0 - fz, jnp.where(iz == z0 + 1, fz, 0.0)))
        w = jnp.concatenate([whi, wlo, whi, wlo], axis=0)
        iy = lax.broadcasted_iota(jnp.int32, (CY, tile), 0)
        wy = jnp.where(iy == y0, 1.0 - fy, jnp.where(iy == y0 + 1, fy, 0.0))
        wx = [jnp.where(x0 == x, 1.0 - fx, jnp.where(x0 == x - 1, fx, 0.0)) for x in range(nx)]
        rows = []
        for f in range(nf if t_ref is None else nf - 1):
            p = jnp.dot(a_ref[f * npl:(f + 1) * npl, :], w, preferred_element_type=F32)
            acc = wx[0] * p[:CY]
            for x in range(1, nx):
                acc = acc + wx[x] * p[x * CY:(x + 1) * CY]
            r = jnp.sum(acc * wy, axis=0, keepdims=True)
            rows += [r[:, i * 128:(i + 1) * 128] for i in range(tile // 128)]
        for i in range(tile // 128 if t_ref is not None else 0):
            sl = slice(i * 128, (i + 1) * 128)
            low = jnp.broadcast_to(z0[:, sl], (8, 128))
            high = low + 1
            total = None
            for y in range(0, CY, 8):
                at0 = at1 = None
                for x in range(nx):
                    v = t_ref[x * CY + y:x * CY + y + 8, :]
                    v0 = wx[x][:, sl] * jnp.take_along_axis(v, low, axis=1)
                    v1 = wx[x][:, sl] * jnp.take_along_axis(v, high, axis=1)
                    at0 = v0 if at0 is None else at0 + v0
                    at1 = v1 if at1 is None else at1 + v1
                v = (at0 * (1.0 - fz[:, sl]) + at1 * fz[:, sl]) * wy[y:y + 8, sl]
                total = v if total is None else total + v
            rows.append(jnp.sum(total, axis=0, keepdims=True))
        o_ref[info_ref[1] + t] = jnp.concatenate(rows, axis=0)
        return carry

    lax.fori_loop(0, nt, body, 0, unroll=unroll)


def split_into(a_ref, row, v):
    n, nz = v.shape
    hi, lo = split2(v)
    for i, part in enumerate((hi, hi, lo, lo)):
        a_ref[row:row + n, i * nz:(i + 1) * nz] = part


def interp_kernel(turn_any, f_ref, base_any, frac_any, o_ref, a_ref, base_ref, frac_ref, turn_ref, sems, *, tile, blocks, turned):
    nf, nz, npl = f_ref.shape
    pairs = ((base_any, base_ref), (frac_any, frac_ref), (turn_any, turn_ref))
    copies = [pltpu.make_async_copy(a, b, sems.at[i]) for i, (a, b) in enumerate(pairs)]
    for c in copies:
        c.start()
    for f in range(nf):
        split_into(a_ref, f * npl, f_ref[f].T)
    for c in copies:
        c.wait()
    info_ref = places(turn_ref[0], base_ref.shape[1] // tile, blocks, turned)
    load_tiles(16, o_ref, info_ref, base_ref, frac_ref, a_ref, info_ref[0], nf, nz, npl, tile)


def interp(turn, fields, base, frac, tile, blocks, turned):
    nf, nz, npl = fields.shape
    slots = base.shape[-1]
    return pl.pallas_call(
        functools.partial(interp_kernel, tile=tile, blocks=blocks, turned=turned),
        out_shape=jax.ShapeDtypeStruct((2 * slots // tile, nf * tile // 128, 128), F32),
        in_specs=[ANY, VM, ANY, ANY],
        out_specs=VM,
        scratch_shapes=[pltpu.VMEM((nf * npl, 4 * nz), BF),
                        pltpu.VMEM(base.shape, jnp.int32), pltpu.VMEM(frac.shape, F32),
                        pltpu.SMEM((1,), jnp.int32), pltpu.SemaphoreType.DMA((3,))],
        compiler_params=CP,
        name="interp",
    )(turn, fields, base, frac)


def right_sides(start_ref, tiles, hl, hr, kap_ref, si, y, fs, lane):
    nf, nz, npl = start_ref.shape
    nt = npl // 128
    for f in range(nf):
        k = 1 if f == nf - 1 else 0
        v = tiles(f)
        rp = [pltpu.roll(u, CY, axis=1) for u in v]
        rm = [pltpu.roll(u, 128 - CY, axis=1) for u in v]
        left_in = hl if f == 0 else pltpu.roll(hl, 128 - f * CY, axis=1)
        by = (128 - CY - f * CY) % 128
        right_in = hr if by == 0 else pltpu.roll(hr, by, axis=1)
        for t in range(nt):
            left = jnp.where(lane < CY, left_in if t == 0 else rp[t-1], rp[t])
            right = jnp.where(lane >= 128 - CY, right_in if t == nt - 1 else rm[t+1], rm[t])
            side = pltpu.roll(v[t], 1, axis=1) + pltpu.roll(v[t], 127, axis=1)
            sl = slice(t * 128, (t + 1) * 128)
            r = (start_ref[f, :, sl] + kap_ref[k, :, sl] * (left + right + side)) * si[:, sl]
            y[:, f*npl+t*128:f*npl+(t+1)*128] = reduce_rhs(r, slice(k*npl + t*128, k*npl + (t+1)*128), fs)


def march_kernel(start_ref, kap_ref, al_ref, lo_ref, hi_ref, left_ref, right_ref, cells_ref,
                 f1t_ref, pay_ref, fac_ref, y, y2, g, q0, q1, p1, q2, p2, h, iv, si, gs):
    nf, nz, npl = start_ref.shape
    nt = npl // 128
    own = 2 * npl
    lane = lanes(nz)
    fringe = on_fringe(lane)
    inv = 1.0 / al_ref[...]
    si[...] = inv
    for k in range(2):
        g[:, k*npl:(k+1)*npl] = 2.0 + (1.0 + 4.0 * kap_ref[k]) * inv
    outer = []
    for i, (near, mine) in enumerate(((left_ref, lo_ref), (right_ref, hi_ref))):
        c3 = unfold3(near[2*nz:, :])
        r32, r64, r96 = [pltpu.roll(c3, j, axis=1) for j in (32, 64, 96)]
        c = jnp.where(lane < CY, c3, jnp.where(lane < 2*CY, r32, r64))
        s = jnp.where(lane < CY, r64, jnp.where(lane < 2*CY, r96, jnp.where(lane < 3*CY, c3, r32)))
        inv = 1.0 / s
        g[:, own+i*128:own+(i+1)*128] = 2.0 + (1.0 + 4.0 * c) * inv
        v = near[:nz, :]
        z = jnp.where(fringe, 0.0, v)
        side = pltpu.roll(z, 1, axis=1) + pltpu.roll(z, 127, axis=1)
        outer.append((v + c * (near[nz:2*nz, :] + mine[:nz, :] + side)) * inv)
    fs = (q0, q1, p1, q2, p2)
    factor(g, q0, q1, p1, q2, p2, h, iv)

    def clear(v):
        return jnp.where(fringe, 0.0, v)

    right_sides(start_ref, lambda f: [clear(start_ref[f, :, t*128:(t+1)*128]) for t in range(nt)],
                left_ref[:nz, :], right_ref[:nz, :], kap_ref, si, y, fs, lane)
    for i in range(2):
        y[:, nf*npl+i*128:nf*npl+(i+1)*128] = reduce_rhs(outer[i], slice(own+i*128, own+(i+1)*128), fs)

    def widen(v):
        m, p = v[:, :npl], v[:, npl:own]
        return jnp.concatenate([m] * (nf - 1) + [p, v[:, own:]], axis=1)

    def widen_own(v):
        m, p = v[:, :npl], v[:, npl:own]
        return jnp.concatenate([m] * (nf - 1) + [p], axis=1)

    substitute(y, h, iv, widen)

    def first(f):
        return [clear(y[:, f*npl+t*128:f*npl+(t+1)*128]) for t in range(nt)]

    right_sides(start_ref, first, y[:, nf*npl:nf*npl+128], y[:, nf*npl+128:nf*npl+256], kap_ref, si, y2, fs, lane)
    substitute(y2, h, iv, widen_own)
    for f in range(nf):
        for t in range(nt):
            j = f * nt + t
            pay_ref[j*nz:(j+1)*nz, :] = y2[:, f*npl+t*128:f*npl+(t+1)*128]
    for f in range(nf):
        v = first(f)
        for t in range(nt):
            f1t_ref[f*npl+t*128:f*npl+(t+1)*128, :] = v[t].T
    nx = npl // CY
    half = nf * 2 * nx
    ln = lane % half
    x, side, deep = ln // 2 % nx, ln % 2, jnp.where(lane >= half, 2, 1)
    src = x % (128 // CY) * CY + jnp.where(side == 0, deep, CY - 1 - deep)

    def pick(get):
        out = None
        for t in range(nt):
            v = jnp.take_along_axis(get(t), src, axis=1)
            out = v if out is None else jnp.where(x // (128 // CY) == t, v, out)
        return out

    ck = [pick(lambda t, k=k: kap_ref[k, :, t*128:(t+1)*128]) for k in range(2)]
    c = jnp.where(ln // (2 * nx) == nf - 1, ck[1], ck[0])
    inv = pick(lambda t: si[:, t*128:(t+1)*128])
    cs = c * inv
    gg = 2.0 + (inv + 4.0 * cs)
    j = nf * nt
    few = (lane // (4 * nx) % 2) * (nf - 1) * 2 * nx + (lane // (2 * nx) % 2) * half + ln % (2 * nx)
    pay_ref[j*nz:(j+1)*nz, :] = jnp.where(
        lane < half, jnp.take_along_axis(cs, few, axis=1), jnp.take_along_axis(gg, few, axis=1))
    pay_ref[(j+1)*nz:, :] = cells_ref[...].astype(F32)
    gs[...] = gg
    refs = [fac_ref.at[i*nz:(i+1)*nz] for i in range(7)]
    factor(gs, *refs)
    fac_ref[7*nz:, :] = cs


def march(start, kappa, along, low, high, left, right, cells):
    nf, nz, npl = start.shape
    nt = npl // 128
    rows = (nf * nt + 1) * nz + cells.shape[0]
    w = 2 * npl + 256
    return pl.pallas_call(
        march_kernel,
        out_shape=(jax.ShapeDtypeStruct((nf * npl, nz), F32), jax.ShapeDtypeStruct((rows, 128), F32),
                   jax.ShapeDtypeStruct((8 * nz, 128), F32)),
        in_specs=[VM] * 8,
        out_specs=(VM, VM, VM),
        scratch_shapes=[pltpu.VMEM((nz, nf*npl+256), F32), pltpu.VMEM((nz, nf*npl), F32)]
        + [pltpu.VMEM((nz, w), F32)] * 8 + [pltpu.VMEM((nz, npl), F32), pltpu.VMEM((nz, 128), F32)],
        compiler_params=CP,
        name="march",
    )(start, kappa, along, low, high, left, right, cells)


def place_small(shift, arr_ref, row0, cell_row, slots, nf, nz, npl):
    rows = arr_ref.shape[1]
    per = rows // nf
    tile = per * 128
    nt = slots // tile
    nx = npl // CY
    nq = 2 * nx
    zo, av = [], []
    for t in range(nt):
        c = cell_row(lax.rem(t + shift, nt), tile)
        cz = c // npl
        q = c // CY % nx * 2 + c % 2
        zo.append((lax.broadcasted_iota(jnp.int32, (nz, tile), 0) == cz).astype(F32).astype(BF))
        oh = lax.broadcasted_iota(jnp.int32, (nq, tile), 0) == q
        a = arr_ref[row0 + t]
        his, los = [], []
        for f in range(nf):
            row = jnp.concatenate([a[f*per+i:f*per+i+1] for i in range(per)], axis=1)
            hi, lo = split2(jnp.where(oh, row, 0.0))
            his.append(hi)
            los.append(lo)
        av.append(jnp.concatenate(his + los, axis=0))
    zo = jnp.concatenate(zo, axis=1)
    av = jnp.concatenate(av, axis=1)
    return lax.dot_general(zo, av, (((1,), (1,)), ((), ())), preferred_element_type=F32)


def spots(k, nf, npl, low, high):
    nq = 2 * npl // CY
    return k // nq % nf * npl + k % nq // 2 * CY + jnp.where(k % 2 == 0, low, high)


def relay_kernel(turn_ref, arr_ref, cells_ref, f1t_ref, fac_ref, base_ref, frac_ref, o_ref, e_ref, a_ref, ys, t_ref, *, tile, nf, edges, blocks, turned):
    nz = f1t_ref.shape[1]
    info_ref = places(turn_ref[0], base_ref.shape[1] // tile, blocks, turned)
    npl = f1t_ref.shape[0] // nf
    slots = base_ref.shape[1]
    half = nf * 2 * npl // CY
    lane = lanes(nz)

    def cell_row(g, tile):
        return cells_ref[0:1, pl.ds(pl.multiple_of(g * tile, tile), tile)]

    sm = place_small(info_ref[0], arr_ref, info_ref[1], cell_row, slots, nf, nz, npl)
    fr = sm + pltpu.roll(sm, half, axis=1)
    fac = [fac_ref.at[i*nz:(i+1)*nz] for i in range(8)]
    ys[...] = reduce_rhs(fac[7][...] * fr, slice(0, 128), fac[:5])
    substitute(ys, fac[5], fac[6], same)
    e = ys[...]
    low = lax.broadcasted_iota(jnp.int32, (nz // 2, 128), 1) < half
    e_ref[...] = jnp.where(low, e[:nz//2], pltpu.roll(e[nz//2:], half, axis=1))
    hi, lo = split2(e)
    both = jnp.where(lane < half, hi.astype(F32), pltpu.roll(lo.astype(F32), half, axis=1))
    terms = jnp.concatenate([sm.astype(BF), both.astype(BF)], axis=1)
    k = lax.broadcasted_iota(jnp.int32, (1, 256), 1)
    target = jnp.where(k < 128, spots(k, nf, npl, 0, CY - 1), spots(k, nf, npl, 1, CY - 2))
    for f in range(nf):
        row = lax.broadcasted_iota(jnp.int32, (npl, 256), 0) + f * npl
        put = (row == target).astype(F32).astype(BF)
        add = lax.dot_general(put, terms, (((1,), (1,)), ((), ())), preferred_element_type=F32)
        v = f1t_ref[f*npl:(f+1)*npl, :] + add
        if f < nf - 1:
            split_into(a_ref, f * npl, v)
        else:
            t_ref[...] = v
    load_tiles(UNROLL, o_ref, info_ref, base_ref, frac_ref, a_ref, None, nf, nz, npl, tile, t_ref)
    if edges:
        turned = e.T
        nt = slots // tile
        nq = half // nf
        for col, by in ((nq - 2, 1), (0, nt - 1)):
            rows = jnp.concatenate([turned[f*nq+col:f*nq+col+2] for f in range(nf)], axis=0)
            o_ref[nt - info_ref[1] + lax.rem(info_ref[2] + by, nt)] = rows


def relay(turn, arrived, cells, f1t, fac, base, frac, tile, nf, edges, blocks, turned):
    nz = f1t.shape[1]
    return pl.pallas_call(
        functools.partial(relay_kernel, tile=tile, nf=nf, edges=edges, blocks=blocks, turned=turned),
        out_shape=(jax.ShapeDtypeStruct(arrived.shape, F32), jax.ShapeDtypeStruct((nz // 2, 128), F32)),
        in_specs=[SM] + [VM] * 6,
        out_specs=(VM, VM),
        scratch_shapes=[pltpu.VMEM((f1t.shape[0], 4 * nz), BF), pltpu.VMEM((nz, 128), F32),
                        pltpu.VMEM((f1t.shape[0] // nf, nz), F32)],
        compiler_params=CP,
        name="relay",
    )(turn, arrived, cells, f1t, fac, base, frac)


def unfold(v):
    return jnp.concatenate([v, pltpu.roll(v, 64, axis=1)], axis=0)


def finish_kernel(turn_ref, arr_any, own_ref, moved_ref, e_any, came_any, *refs, edges, blocks, turned):
    if edges:
        out_any, *refs = refs
    else:
        el_ref, er_ref, out_any, *refs = refs
    arr_ref, e_ref, o_ref, pay_ref, ys, gs, *fac, sems = refs
    nf, nz, npl = o_ref.shape
    nt = npl // 128
    nx = npl // CY
    nq = 2 * nx
    half = nf * nq
    j = nf * nt
    cells0 = (j + 1) * nz
    slots = (pay_ref.shape[0] - cells0) * 128
    lines = slice(j * nz, pay_ref.shape[0])
    rest = slice(0, j * nz)
    came = pltpu.make_async_copy(arr_any, arr_ref, sems.at[2])
    came.start()

    def copies(ref, e):
        pairs = [(ref.at[s], pay_ref.at[s]) for s in (lines, rest)] + [(e, e_ref)]
        return [pltpu.make_async_copy(a, b, sems.at[i]) for i, (a, b) in zip((0, 1, 3), pairs)]

    back = lax.axis_index("mesh")

    @pl.when(back == 0)
    def _():
        for c in copies(own_ref, e_any):
            c.start()

    @pl.when(back != 0)
    def _():
        for c in copies(moved_ref, came_any):
            c.start()

    info_ref = places(turn_ref[0], arr_ref.shape[0] // 2, blocks, turned)
    held = copies(own_ref, e_any)
    lane = lanes(nz)
    q = lane % nq
    came.wait()
    held[0].wait()
    held[2].wait()
    ln = lane % half
    few = ln // nq // (nf - 1) * 2 * nq + lane // half * nq + ln % nq
    table = pay_ref[j*nz:(j+1)*nz, :]
    cs = jnp.take_along_axis(table, few, axis=1)
    gs[...] = jnp.take_along_axis(table, few + half, axis=1)
    factor(gs, *fac)
    e = unfold(e_ref[...])
    if edges:
        chunks = arr_ref.shape[0] // 2
        el = arr_ref[chunks - info_ref[1] + lax.rem(info_ref[4] + chunks - 1, chunks)]
        er = arr_ref[chunks - info_ref[1] + lax.rem(info_ref[4] + 1, chunks)]
        none = jnp.zeros((nq - 4, nz), F32)
        parts = []
        for f in range(nf):
            parts += [el[2*f:2*f+2], none, er[2*f:2*f+2]]
        parts = jnp.concatenate(parts, axis=0)
        outer = jnp.concatenate([parts, parts], axis=0).T
        left = right = outer
    else:
        left = pltpu.roll(unfold(el_ref[...]), 128 - (nq - 2), axis=1)
        right = pltpu.roll(unfold(er_ref[...]), nq - 2, axis=1)
    left = jnp.where(q < 2, left, pltpu.roll(e, 2, axis=1))
    right = jnp.where(q >= nq - 2, right, pltpu.roll(e, 126, axis=1))
    deep = pltpu.roll(e, half, axis=1)

    def cell_row(g, tile):
        per = tile // 128
        rows = [pay_ref[pl.ds(cells0 + g * per + i, 1), :] for i in range(per)]
        return jnp.concatenate(rows, axis=1).astype(jnp.int32)

    sm = place_small(info_ref[0], arr_ref, info_ref[1], cell_row, slots, nf, nz, npl)
    fr = sm + pltpu.roll(sm, half, axis=1)
    r = cs * jnp.where(lane < half, fr + left + right, deep)
    ys[...] = reduce_rhs(r, slice(0, 128), fac[:5])
    substitute(ys, fac[5], fac[6], same)
    hi, lo = split2(ys[...])
    terms = jnp.concatenate([sm.astype(BF), hi, lo], axis=1)
    k = lax.broadcasted_iota(jnp.int32, (384, 1), 0)
    near = jnp.where(k % 128 < half, 1, 2)
    target = jnp.where(k < 128, spots(k, nf, npl, 0, CY - 1), spots(k, nf, npl, near, CY - 1 - near))
    fringe = on_fringe(lane)
    held[1].wait()
    leave = [pltpu.make_async_copy(o_ref.at[f], out_any.at[f], sems.at[4 + f]) for f in range(nf)]
    for f in range(nf):
        put = (lax.broadcasted_iota(jnp.int32, (384, npl), 1) + f * npl == target).astype(F32).astype(BF)
        add = jnp.dot(terms, put, preferred_element_type=F32)
        for t in range(nt):
            v = pay_ref[(f*nt+t)*nz:(f*nt+t+1)*nz, :]
            o_ref[f, :, t*128:(t+1)*128] = jnp.where(fringe, 0.0, v) + add[:, t*128:(t+1)*128]
        leave[f].start()
    for c in leave:
        c.wait()


def finish(turn, shape, arrived, own, moved, e, blocks, turned):
    nz = shape[1]
    return pl.pallas_call(
        functools.partial(finish_kernel, edges=len(e) == 2, blocks=blocks, turned=turned),
        out_shape=jax.ShapeDtypeStruct(shape, F32),
        in_specs=[SM] + [ANY] * 5 + [VM] * (len(e) - 2),
        out_specs=ANY,
        scratch_shapes=[pltpu.VMEM(v.shape, F32) for v in (arrived, e[0])] + [pltpu.VMEM(shape, F32), pltpu.VMEM(own.shape, F32)]
        + [pltpu.VMEM((nz, 128), F32)] * 9 + [pltpu.SemaphoreType.DMA((4 + shape[0],))],
        compiler_params=CP,
        name="finish",
    )(turn, arrived, own, moved, *e)


TILE = 256
UNROLL = 4


def exchange(values, blocks, cap, nf):
    if cap == TILE:
        return lax.all_to_all(values, ("mesh", "blk"), 0, 0, tiled=True)
    halves = values.reshape(2, -1, nf, TILE).transpose(0, 2, 1, 3).reshape(2, nf, blocks, cap)
    sent = halves.transpose(0, 2, 1, 3).reshape(2 * blocks, nf, cap)
    got = lax.all_to_all(sent, ("mesh", "blk"), 0, 0, tiled=True)
    got = got.reshape(2, blocks, nf, cap).transpose(0, 2, 1, 3).reshape(2, nf, -1, TILE)
    return got.transpose(0, 2, 1, 3).reshape(values.shape)


def turn(values, cap, by):
    groups = values.reshape(values.shape[:-1] + (-1, cap))
    return jnp.roll(groups, -by, axis=-2).reshape(values.shape)


def local(rotation_step, field_state, diffusivity, stretch, donor_base, donor_frac, fringe_cell):
    on_back = lax.axis_index("mesh") == 1
    blocks = lax.axis_size("blk")
    rotation = rotation_step[0]
    start, kappa, along = field_state[0, 0], diffusivity[0, 0], stretch[0, 0]
    base, frac, cells = donor_base[0, 0], donor_frac[0, 0], fringe_cell[0, 0]
    nf = start.shape[0]
    slots = base.shape[0]
    cap = slots // blocks
    turned = cap != TILE
    send0, frac0, cells0 = base, frac, cells
    if turned:
        by = jnp.where(on_back, 0, rotation)
        send0, frac0, cells0 = turn(base, cap, by), turn(frac, cap, by), turn(cells, cap, by)
    edges = cap == TILE and 2 * nf == nf * TILE // 128
    row = (1, slots)
    low, high = pack(start, kappa, along)
    left = lax.ppermute(high, "blk", [(i, (i + 1) % blocks) for i in range(blocks)])
    right = lax.ppermute(low, "blk", [((i + 1) % blocks, i) for i in range(blocks)])
    values = interp(rotation_step, start, send0.reshape(row), frac0.reshape(3, 1, slots), TILE, blocks, turned)

    def branch(distance):
        def shift(v, off, blade):
            pairs = [(i, (i + off) % blocks) for i in range(blocks)] if blade else []
            pairs = pairs + [(blocks + i, blocks + (i + distance + off) % blocks) for i in range(blocks)]
            return lax.ppermute(v, ("mesh", "blk"), pairs)

        def run(pay, step, arrived, f1t, fac, base, frac, cells0):
            moved = shift(pay, 0, False)
            values, e = relay(
                step, arrived, cells0.reshape(row), f1t, fac, base.reshape(row), frac.reshape(3, 1, slots), TILE, nf, edges,
                blocks, turned,
            )
            arrived = exchange(values, blocks, cap, nf)
            near = () if edges else (shift(e, 1, True), shift(e, -1, True))
            return arrived, moved, e, shift(e, 0, False), *near

        return run

    values, left, right = lax.optimization_barrier((values, left, right))
    arrived = exchange(values, blocks, cap, nf)
    f1t, pay, fac = march(start, kappa, along, low, high, left, right, cells0.reshape(-1, 128))
    arrived, moved, e, came, *near = lax.switch(
        rotation - 1, [branch(d) for d in range(1, TURN_MOST + 1)], pay, rotation_step, arrived, f1t, fac, base, frac, cells0
    )
    return finish(rotation_step, start.shape, arrived, pay, moved, (e, came, *near), blocks, turned)[None, None]


def solution(mesh):
    placed = (
        P(),
        P("mesh", "blk", None, None, None),
        P("mesh", "blk", None, None, None),
        P("mesh", "blk", None, None),
        P("mesh", "blk", None),
        P("mesh", "blk", None, None),
        P("mesh", "blk", None),
    )
    return jax.shard_map(
        local,
        mesh=mesh,
        in_specs=placed,
        out_specs=P("mesh", "blk", None, None, None),
        check_vma=False,
    )
```

```python
import functools
import jax
import jax.numpy as jnp
from jax import lax
from jax.experimental import pallas as pl
from jax.experimental.pallas import tpu as pltpu
from jax.sharding import PartitionSpec as P

CY = 32
ITERS = 2
TURN_MOST = 7
F32, BF = jnp.float32, jnp.bfloat16
VM = pl.BlockSpec(memory_space=pltpu.VMEM)
SM = pl.BlockSpec(memory_space=pltpu.SMEM)
ANY = pl.BlockSpec(memory_space=pl.ANY)
WHOLE = pltpu.CompilerParams(vmem_limit_bytes=64 * 1024 * 1024)
CP = pltpu.CompilerParams(vmem_limit_bytes=48 * 1024 * 1024)


def split2(v):
    hi = v.astype(BF)
    lo = (v - hi.astype(F32)).astype(BF)
    return hi, lo


def down(v, k):
    return pltpu.roll(v, k, axis=0)
def up(v, k):
    return pltpu.roll(v, v.shape[0] - k, axis=0)

def factor(g_ref, q0, q1, p1, q2, p2, h, iv):
    nz, w = g_ref.shape
    for c in range(0, w, 128):
        s = slice(c, c+128)
        z = lax.broadcasted_iota(jnp.int32, (nz, 128), 0)
        g = g_ref[:, s]
        q = 1.0 / g
        q0[:, s] = q
        qd = jnp.where(z >= 1, down(q, 1), 0.0)
        qu = jnp.where(z < nz-1, up(q, 1), 0.0)
        g = g - qd - qu
        p = jnp.where(z >= 2, qd, 0.0)
        for k, (qr, pr) in ((2, (q1, p1)), (4, (q2, p2))):
            q = 1.0 / g
            qr[:, s] = q
            pr[:, s] = p
            pq = p * q
            ppq = p * pq
            g = g - p * p * down(q, k) - up(ppq, k)
            p = p * down(pq, k)
            p = jnp.where(z >= 2*k, p, 0.0)
        g_ref[:, s] = g
        h[:, s] = p
    prev = None
    for r in range(0, nz, 8):
        g = g_ref[r:r+8, :]
        if prev is None:
            hk = jnp.zeros_like(g)
        else:
            p = h[r:r+8, :]
            hk = p * prev
            g = g - p * hk
        prev = 1.0 / g
        h[r:r+8, :] = hk
        iv[r:r+8, :] = prev

def reduce_rhs(r, s, fs):
    q0, q1, p1, q2, p2 = fs
    nz = r.shape[0]
    z = lax.broadcasted_iota(jnp.int32, r.shape, 0)
    w = q0[:, s] * r
    r = r + jnp.where(z >= 1, down(w, 1), 0.0) + jnp.where(z < nz-1, up(w, 1), 0.0)
    for k, qr, pr in ((2, q1, p1), (4, q2, p2)):
        w = qr[:, s] * r
        p = pr[:, s]
        r = r + p * down(w, k) + up(p * w, k)
    return r


def substitute(y, h, iv, widen):
    nz = y.shape[0]
    prev = y[0:8, :]
    for r in range(8, nz, 8):
        prev = y[r:r+8, :] + widen(h[r:r+8, :]) * prev
        y[r:r+8, :] = prev
    prev = prev * widen(iv[nz-8:nz, :])
    y[nz-8:nz, :] = prev
    for r in range(nz-16, -1, -8):
        prev = y[r:r+8, :] * widen(iv[r:r+8, :]) + widen(h[r+8:r+16, :]) * prev
        y[r:r+8, :] = prev


def same(v):
    return v


def lanes(nz):
    return lax.broadcasted_iota(jnp.int32, (nz, 128), 1)


def on_fringe(lane):
    return (lane % CY == 0) | (lane % CY == CY - 1)


def pack_planes(get, nf, t, x, lane):
    out = None
    for f in range(nf):
        v = get(f, t)
        by = (f - x) * CY % 128
        v = v if by == 0 else pltpu.roll(v, by, axis=1)
        out = v if out is None else jnp.where(lane >= f * CY, v, out)
    return out


def fold(v):
    n = v.shape[0] // 4
    tail = jnp.concatenate([pltpu.roll(v[3*n:], 128 - CY - i * CY, axis=1) for i in range(3)], axis=0)
    lane = lax.broadcasted_iota(jnp.int32, tail.shape, 1)
    return jnp.where(lane < 3 * CY, v[:3*n], tail)


def unfold3(v):
    n = v.shape[0] // 3
    a, b, c = [pltpu.roll(v[i*n:(i+1)*n], (i + 1) * CY, axis=1) for i in range(3)]
    lane = lax.broadcasted_iota(jnp.int32, a.shape, 1)
    return jnp.concatenate([v, jnp.where(lane < CY, a, jnp.where(lane < 2 * CY, b, c))], axis=0)


def pack_kernel(f_any, kap_any, al_any, lo_any, hi_any, f_ref, kap_ref, al_ref, lo_ref, hi_ref, sems):
    nf, nz, npl = f_ref.shape
    copies = [pltpu.make_async_copy(f_any.at[f], f_ref.at[f], sems.at[f]) for f in range(nf)]
    copies += [pltpu.make_async_copy(kap_any.at[k], kap_ref.at[k], sems.at[nf + k]) for k in range(2)]
    copies += [pltpu.make_async_copy(al_any, al_ref, sems.at[nf + 2])]
    for c in copies:
        c.start()
    lane = lanes(nz)
    per, nt = 128 // CY, npl // 128

    def field(f, t):
        return f_ref[f, :, t*128:(t+1)*128]

    def coef(f, t):
        sl = slice(t*128, (t+1)*128)
        return kap_ref[f, :, sl] if f < 2 else al_ref[:, sl]

    sides = ((lo_ref, lo_any, 0, 0, 1), (hi_ref, hi_any, nt - 1, per - 1, -1))
    parts = [slice(0, nz), slice(nz, 2 * nz), slice(2 * nz, 2 * nz + nz * 3 // 4)]
    back = [pltpu.make_async_copy(ref.at[p], out.at[p], sems.at[nf + 3 + 3 * i + j])
            for i, (ref, out, *_) in enumerate(sides) for j, p in enumerate(parts)]
    for c in copies[:nf]:
        c.wait()
    for i, (ref, _, t, x, step) in enumerate(sides):
        ref[parts[0]] = pack_planes(field, nf, t, x, lane)
        back[3 * i].start()
        ref[parts[1]] = pack_planes(field, nf, t, x + step, lane)
        back[3 * i + 1].start()
    for c in copies[nf:]:
        c.wait()
    for i, (ref, _, t, x, step) in enumerate(sides):
        ref[parts[2]] = fold(pack_planes(coef, 3, t, x, lane))
        back[3 * i + 2].start()
    for c in back:
        c.wait()


def pack(fields, kappa, along):
    nf, nz, npl = fields.shape
    sh = jax.ShapeDtypeStruct((2 * nz + nz * 3 // 4, nf * CY), F32)
    return pl.pallas_call(
        pack_kernel,
        out_shape=(sh, sh),
        in_specs=[ANY] * 3,
        out_specs=(ANY, ANY),
        scratch_shapes=[pltpu.VMEM(v.shape, F32) for v in (fields, kappa, along, sh, sh)]
        + [pltpu.SemaphoreType.DMA((nf + 9,))],
        compiler_params=WHOLE,
        name="pack",
    )(fields, kappa, along)


def places(turn, tiles, blocks, turned):
    back = lax.axis_index("mesh")
    me = lax.axis_index("blk")
    by = 0 if turned else turn * (1 - back)
    return by, tiles * (1 - back), lax.rem(me + turn * back, blocks), back, lax.rem(me + blocks - turn * back, blocks)


def load_tiles(unroll, o_ref, info_ref, base_ref, frac_ref, a_ref, shift, nf, nz, npl, tile, t_ref=None):
    nx = npl // CY
    nt = base_ref.shape[1] // tile
    o_ref[pl.ds(nt - info_ref[1], nt)] = jnp.zeros((nt,) + o_ref.shape[1:], F32)

    def body(t, carry):
        g = t if shift is None else lax.rem(t + shift, nt)
        off = pl.multiple_of(g * tile, tile)
        b = base_ref[0:1, pl.ds(off, tile)]
        fz, fx, fy = [frac_ref[i, :, pl.ds(off, tile)] for i in range(3)]
        z0 = b // npl
        x0 = b // CY % nx
        y0 = b % CY
        iz = lax.broadcasted_iota(jnp.int32, (nz, tile), 0)
        whi, wlo = split2(jnp.where(iz == z0, 1.0 - fz, jnp.where(iz == z0 + 1, fz, 0.0)))
        w = jnp.concatenate([whi, wlo, whi, wlo], axis=0)
        iy = lax.broadcasted_iota(jnp.int32, (CY, tile), 0)
        wy = jnp.where(iy == y0, 1.0 - fy, jnp.where(iy == y0 + 1, fy, 0.0))
        wx = [jnp.where(x0 == x, 1.0 - fx, jnp.where(x0 == x - 1, fx, 0.0)) for x in range(nx)]
        rows = []
        for f in range(nf if t_ref is None else nf - 1):
            p = jnp.dot(a_ref[f * npl:(f + 1) * npl, :], w, preferred_element_type=F32)
            acc = wx[0] * p[:CY]
            for x in range(1, nx):
                acc = acc + wx[x] * p[x * CY:(x + 1) * CY]
            r = jnp.sum(acc * wy, axis=0, keepdims=True)
            rows += [r[:, i * 128:(i + 1) * 128] for i in range(tile // 128)]
        for i in range(tile // 128 if t_ref is not None else 0):
            sl = slice(i * 128, (i + 1) * 128)
            low = jnp.broadcast_to(z0[:, sl], (8, 128))
            high = low + 1
            total = None
            for y in range(0, CY, 8):
                at0 = at1 = None
                for x in range(nx):
                    v = t_ref[x * CY + y:x * CY + y + 8, :]
                    v0 = wx[x][:, sl] * jnp.take_along_axis(v, low, axis=1)
                    v1 = wx[x][:, sl] * jnp.take_along_axis(v, high, axis=1)
                    at0 = v0 if at0 is None else at0 + v0
                    at1 = v1 if at1 is None else at1 + v1
                v = (at0 * (1.0 - fz[:, sl]) + at1 * fz[:, sl]) * wy[y:y + 8, sl]
                total = v if total is None else total + v
            rows.append(jnp.sum(total, axis=0, keepdims=True))
        o_ref[info_ref[1] + t] = jnp.concatenate(rows, axis=0)
        return carry

    lax.fori_loop(0, nt, body, 0, unroll=unroll)


def split_into(a_ref, row, v):
    n, nz = v.shape
    hi, lo = split2(v)
    for i, part in enumerate((hi, hi, lo, lo)):
        a_ref[row:row + n, i * nz:(i + 1) * nz] = part


def interp_kernel(turn_any, f_ref, base_any, frac_any, o_ref, a_ref, base_ref, frac_ref, turn_ref, sems, *, tile, blocks, turned):
    nf, nz, npl = f_ref.shape
    pairs = ((base_any, base_ref), (frac_any, frac_ref), (turn_any, turn_ref))
    copies = [pltpu.make_async_copy(a, b, sems.at[i]) for i, (a, b) in enumerate(pairs)]
    for c in copies:
        c.start()
    for f in range(nf):
        split_into(a_ref, f * npl, f_ref[f].T)
    for c in copies:
        c.wait()
    info_ref = places(turn_ref[0], base_ref.shape[1] // tile, blocks, turned)
    load_tiles(16, o_ref, info_ref, base_ref, frac_ref, a_ref, info_ref[0], nf, nz, npl, tile)


def interp(turn, fields, base, frac, tile, blocks, turned):
    nf, nz, npl = fields.shape
    slots = base.shape[-1]
    return pl.pallas_call(
        functools.partial(interp_kernel, tile=tile, blocks=blocks, turned=turned),
        out_shape=jax.ShapeDtypeStruct((2 * slots // tile, nf * tile // 128, 128), F32),
        in_specs=[ANY, VM, ANY, ANY],
        out_specs=VM,
        scratch_shapes=[pltpu.VMEM((nf * npl, 4 * nz), BF),
                        pltpu.VMEM(base.shape, jnp.int32), pltpu.VMEM(frac.shape, F32),
                        pltpu.SMEM((1,), jnp.int32), pltpu.SemaphoreType.DMA((3,))],
        compiler_params=CP,
        name="interp",
    )(turn, fields, base, frac)


def right_sides(start_ref, tiles, hl, hr, kap_ref, si, y, fs, lane):
    nf, nz, npl = start_ref.shape
    nt = npl // 128
    for f in range(nf):
        k = 1 if f == nf - 1 else 0
        v = tiles(f)
        rp = [pltpu.roll(u, CY, axis=1) for u in v]
        rm = [pltpu.roll(u, 128 - CY, axis=1) for u in v]
        left_in = hl if f == 0 else pltpu.roll(hl, 128 - f * CY, axis=1)
        by = (128 - CY - f * CY) % 128
        right_in = hr if by == 0 else pltpu.roll(hr, by, axis=1)
        for t in range(nt):
            left = jnp.where(lane < CY, left_in if t == 0 else rp[t-1], rp[t])
            right = jnp.where(lane >= 128 - CY, right_in if t == nt - 1 else rm[t+1], rm[t])
            side = pltpu.roll(v[t], 1, axis=1) + pltpu.roll(v[t], 127, axis=1)
            sl = slice(t * 128, (t + 1) * 128)
            r = (start_ref[f, :, sl] + kap_ref[k, :, sl] * (left + right + side)) * si[:, sl]
            y[:, f*npl+t*128:f*npl+(t+1)*128] = reduce_rhs(r, slice(k*npl + t*128, k*npl + (t+1)*128), fs)


def march_kernel(start_ref, kap_ref, al_ref, lo_ref, hi_ref, left_ref, right_ref, cells_ref,
                 f1t_ref, pay_ref, fac_ref, y, y2, g, q0, q1, p1, q2, p2, h, iv, si, gs):
    nf, nz, npl = start_ref.shape
    nt = npl // 128
    own = 2 * npl
    lane = lanes(nz)
    fringe = on_fringe(lane)
    inv = 1.0 / al_ref[...]
    si[...] = inv
    for k in range(2):
        g[:, k*npl:(k+1)*npl] = 2.0 + (1.0 + 4.0 * kap_ref[k]) * inv
    outer = []
    for i, (near, mine) in enumerate(((left_ref, lo_ref), (right_ref, hi_ref))):
        c3 = unfold3(near[2*nz:, :])
        r32, r64, r96 = [pltpu.roll(c3, j, axis=1) for j in (32, 64, 96)]
        c = jnp.where(lane < CY, c3, jnp.where(lane < 2*CY, r32, r64))
        s = jnp.where(lane < CY, r64, jnp.where(lane < 2*CY, r96, jnp.where(lane < 3*CY, c3, r32)))
        inv = 1.0 / s
        g[:, own+i*128:own+(i+1)*128] = 2.0 + (1.0 + 4.0 * c) * inv
        v = near[:nz, :]
        z = jnp.where(fringe, 0.0, v)
        side = pltpu.roll(z, 1, axis=1) + pltpu.roll(z, 127, axis=1)
        outer.append((v + c * (near[nz:2*nz, :] + mine[:nz, :] + side)) * inv)
    fs = (q0, q1, p1, q2, p2)
    factor(g, q0, q1, p1, q2, p2, h, iv)

    def clear(v):
        return jnp.where(fringe, 0.0, v)

    right_sides(start_ref, lambda f: [clear(start_ref[f, :, t*128:(t+1)*128]) for t in range(nt)],
                left_ref[:nz, :], right_ref[:nz, :], kap_ref, si, y, fs, lane)
    for i in range(2):
        y[:, nf*npl+i*128:nf*npl+(i+1)*128] = reduce_rhs(outer[i], slice(own+i*128, own+(i+1)*128), fs)

    def widen(v):
        m, p = v[:, :npl], v[:, npl:own]
        return jnp.concatenate([m] * (nf - 1) + [p, v[:, own:]], axis=1)

    def widen_own(v):
        m, p = v[:, :npl], v[:, npl:own]
        return jnp.concatenate([m] * (nf - 1) + [p], axis=1)

    substitute(y, h, iv, widen)

    def first(f):
        return [clear(y[:, f*npl+t*128:f*npl+(t+1)*128]) for t in range(nt)]

    right_sides(start_ref, first, y[:, nf*npl:nf*npl+128], y[:, nf*npl+128:nf*npl+256], kap_ref, si, y2, fs, lane)
    substitute(y2, h, iv, widen_own)
    for f in range(nf):
        for t in range(nt):
            j = f * nt + t
            pay_ref[j*nz:(j+1)*nz, :] = y2[:, f*npl+t*128:f*npl+(t+1)*128]
    for f in range(nf):
        v = first(f)
        for t in range(nt):
            f1t_ref[f*npl+t*128:f*npl+(t+1)*128, :] = v[t].T
    nx = npl // CY
    half = nf * 2 * nx
    ln = lane % half
    x, side, deep = ln // 2 % nx, ln % 2, jnp.where(lane >= half, 2, 1)
    src = x % (128 // CY) * CY + jnp.where(side == 0, deep, CY - 1 - deep)

    def pick(get):
        out = None
        for t in range(nt):
            v = jnp.take_along_axis(get(t), src, axis=1)
            out = v if out is None else jnp.where(x // (128 // CY) == t, v, out)
        return out

    ck = [pick(lambda t, k=k: kap_ref[k, :, t*128:(t+1)*128]) for k in range(2)]
    c = jnp.where(ln // (2 * nx) == nf - 1, ck[1], ck[0])
    inv = pick(lambda t: si[:, t*128:(t+1)*128])
    cs = c * inv
    gg = 2.0 + (inv + 4.0 * cs)
    j = nf * nt
    few = (lane // (4 * nx) % 2) * (nf - 1) * 2 * nx + (lane // (2 * nx) % 2) * half + ln % (2 * nx)
    one = (lane - half) // (2 * nx) % 2 * half + ln % (2 * nx)
    table = jnp.where(lane < half, jnp.take_along_axis(cs, few, axis=1), jnp.take_along_axis(inv, one, axis=1))
    kept = cells_ref[...].astype(F32)
    kept = jnp.concatenate([jnp.zeros((128 - kept.shape[0], nz), F32), kept], axis=0).T
    pay_ref[j*nz:(j+1)*nz, :] = jnp.where(lane < half + 4 * nx, table, kept)
    gs[...] = gg
    refs = [fac_ref.at[i*nz:(i+1)*nz] for i in range(7)]
    factor(gs, *refs)
    fac_ref[7*nz:, :] = cs


def march(start, kappa, along, low, high, left, right, cells):
    nf, nz, npl = start.shape
    nt = npl // 128
    assert cells.shape[0] <= 128 - nf * 2 * npl // CY - 4 * npl // CY
    rows = (nf * nt + 1) * nz
    w = 2 * npl + 256
    return pl.pallas_call(
        march_kernel,
        out_shape=(jax.ShapeDtypeStruct((nf * npl, nz), F32), jax.ShapeDtypeStruct((rows, 128), F32),
                   jax.ShapeDtypeStruct((8 * nz, 128), F32)),
        in_specs=[VM] * 8,
        out_specs=(VM, VM, VM),
        scratch_shapes=[pltpu.VMEM((nz, nf*npl+256), F32), pltpu.VMEM((nz, nf*npl), F32)]
        + [pltpu.VMEM((nz, w), F32)] * 8 + [pltpu.VMEM((nz, npl), F32), pltpu.VMEM((nz, 128), F32)],
        compiler_params=CP,
        name="march",
    )(start, kappa, along, low, high, left, right, cells)


def place_small(shift, arr_ref, row0, cell_row, slots, nf, nz, npl):
    rows = arr_ref.shape[1]
    per = rows // nf
    tile = per * 128
    nt = slots // tile
    nx = npl // CY
    nq = 2 * nx
    zo, av = [], []
    for t in range(nt):
        c = cell_row(lax.rem(t + shift, nt), tile)
        cz = c // npl
        q = c // CY % nx * 2 + c % 2
        zo.append((lax.broadcasted_iota(jnp.int32, (nz, tile), 0) == cz).astype(F32).astype(BF))
        oh = lax.broadcasted_iota(jnp.int32, (nq, tile), 0) == q
        a = arr_ref[row0 + t]
        his, los = [], []
        for f in range(nf):
            row = jnp.concatenate([a[f*per+i:f*per+i+1] for i in range(per)], axis=1)
            hi, lo = split2(jnp.where(oh, row, 0.0))
            his.append(hi)
            los.append(lo)
        av.append(jnp.concatenate(his + los, axis=0))
    zo = jnp.concatenate(zo, axis=1)
    av = jnp.concatenate(av, axis=1)
    return lax.dot_general(zo, av, (((1,), (1,)), ((), ())), preferred_element_type=F32)


def spots(k, nf, npl, low, high):
    nq = 2 * npl // CY
    return k // nq % nf * npl + k % nq // 2 * CY + jnp.where(k % 2 == 0, low, high)


def relay_kernel(turn_ref, arr_ref, cells_ref, f1t_ref, fac_ref, base_ref, frac_ref, o_ref, e_ref, a_ref, ys, t_ref, *, tile, nf, edges, blocks, turned):
    nz = f1t_ref.shape[1]
    info_ref = places(turn_ref[0], base_ref.shape[1] // tile, blocks, turned)
    npl = f1t_ref.shape[0] // nf
    slots = base_ref.shape[1]
    half = nf * 2 * npl // CY
    lane = lanes(nz)

    def cell_row(g, tile):
        return cells_ref[0:1, pl.ds(pl.multiple_of(g * tile, tile), tile)]

    sm = place_small(info_ref[0], arr_ref, info_ref[1], cell_row, slots, nf, nz, npl)
    fr = sm + pltpu.roll(sm, half, axis=1)
    fac = [fac_ref.at[i*nz:(i+1)*nz] for i in range(8)]
    ys[...] = reduce_rhs(fac[7][...] * fr, slice(0, 128), fac[:5])
    substitute(ys, fac[5], fac[6], same)
    e = ys[...]
    low = lax.broadcasted_iota(jnp.int32, (nz // 2, 128), 1) < half
    e_ref[...] = jnp.where(low, e[:nz//2], pltpu.roll(e[nz//2:], half, axis=1))
    hi, lo = split2(e)
    both = jnp.where(lane < half, hi.astype(F32), pltpu.roll(lo.astype(F32), half, axis=1))
    terms = jnp.concatenate([sm.astype(BF), both.astype(BF)], axis=1)
    k = lax.broadcasted_iota(jnp.int32, (1, 256), 1)
    target = jnp.where(k < 128, spots(k, nf, npl, 0, CY - 1), spots(k, nf, npl, 1, CY - 2))
    for f in range(nf):
        row = lax.broadcasted_iota(jnp.int32, (npl, 256), 0) + f * npl
        put = (row == target).astype(F32).astype(BF)
        add = lax.dot_general(put, terms, (((1,), (1,)), ((), ())), preferred_element_type=F32)
        v = f1t_ref[f*npl:(f+1)*npl, :] + add
        if f < nf - 1:
            split_into(a_ref, f * npl, v)
        else:
            t_ref[...] = v
    load_tiles(UNROLL, o_ref, info_ref, base_ref, frac_ref, a_ref, None, nf, nz, npl, tile, t_ref)
    if edges:
        turned = e.T
        nt = slots // tile
        nq = half // nf
        for col, by in ((nq - 2, 1), (0, nt - 1)):
            rows = jnp.concatenate([turned[f*nq+col:f*nq+col+2] for f in range(nf)], axis=0)
            o_ref[nt - info_ref[1] + lax.rem(info_ref[2] + by, nt)] = rows


def relay(turn, arrived, cells, f1t, fac, base, frac, tile, nf, edges, blocks, turned):
    nz = f1t.shape[1]
    return pl.pallas_call(
        functools.partial(relay_kernel, tile=tile, nf=nf, edges=edges, blocks=blocks, turned=turned),
        out_shape=(jax.ShapeDtypeStruct(arrived.shape, F32), jax.ShapeDtypeStruct((nz // 2, 128), F32)),
        in_specs=[SM] + [VM] * 6,
        out_specs=(VM, VM),
        scratch_shapes=[pltpu.VMEM((f1t.shape[0], 4 * nz), BF), pltpu.VMEM((nz, 128), F32),
                        pltpu.VMEM((f1t.shape[0] // nf, nz), F32)],
        compiler_params=CP,
        name="relay",
    )(turn, arrived, cells, f1t, fac, base, frac)


def unfold(v):
    return jnp.concatenate([v, pltpu.roll(v, 64, axis=1)], axis=0)


def finish_kernel(turn_ref, arr_any, own_ref, moved_ref, e_any, came_any, *refs, edges, blocks, turned):
    if edges:
        out_any, *refs = refs
    else:
        el_ref, er_ref, out_any, *refs = refs
    arr_ref, e_ref, o_ref, pay_ref, turned_ref, ys, gs, *fac, sems = refs
    nf, nz, npl = o_ref.shape
    nt = npl // 128
    nx = npl // CY
    nq = 2 * nx
    half = nf * nq
    j = nf * nt
    slots = arr_ref.shape[0] // 2 * arr_ref.shape[1] // nf * 128
    cells0 = 128 - slots // 128
    lines = slice(j * nz, pay_ref.shape[0])
    rest = slice(0, j * nz)
    came = pltpu.make_async_copy(arr_any, arr_ref, sems.at[2])
    came.start()

    def copies(ref, e):
        pairs = [(ref.at[s], pay_ref.at[s]) for s in (lines, rest)] + [(e, e_ref)]
        return [pltpu.make_async_copy(a, b, sems.at[i]) for i, (a, b) in zip((0, 1, 3), pairs)]

    back = lax.axis_index("mesh")

    @pl.when(back == 0)
    def _():
        for c in copies(own_ref, e_any):
            c.start()

    @pl.when(back != 0)
    def _():
        for c in copies(moved_ref, came_any):
            c.start()

    info_ref = places(turn_ref[0], arr_ref.shape[0] // 2, blocks, turned)
    held = copies(own_ref, e_any)
    lane = lanes(nz)
    q = lane % nq
    came.wait()
    held[0].wait()
    held[2].wait()
    ln = lane % half
    few = ln // nq // (nf - 1) * 2 * nq + lane // half * nq + ln % nq
    table = pay_ref[j*nz:(j+1)*nz, :]
    cs = jnp.take_along_axis(table, few, axis=1)
    inv = jnp.take_along_axis(table, half + lane // half * nq + ln % nq, axis=1)
    gs[...] = 2.0 + (inv + 4.0 * cs)
    turned_ref[...] = table.T
    factor(gs, *fac)
    e = unfold(e_ref[...])
    if edges:
        chunks = arr_ref.shape[0] // 2
        el = arr_ref[chunks - info_ref[1] + lax.rem(info_ref[4] + chunks - 1, chunks)]
        er = arr_ref[chunks - info_ref[1] + lax.rem(info_ref[4] + 1, chunks)]
        none = jnp.zeros((nq - 4, nz), F32)
        parts = []
        for f in range(nf):
            parts += [el[2*f:2*f+2], none, er[2*f:2*f+2]]
        parts = jnp.concatenate(parts, axis=0)
        outer = jnp.concatenate([parts, parts], axis=0).T
        left = right = outer
    else:
        left = pltpu.roll(unfold(el_ref[...]), 128 - (nq - 2), axis=1)
        right = pltpu.roll(unfold(er_ref[...]), nq - 2, axis=1)
    left = jnp.where(q < 2, left, pltpu.roll(e, 2, axis=1))
    right = jnp.where(q >= nq - 2, right, pltpu.roll(e, 126, axis=1))
    deep = pltpu.roll(e, half, axis=1)

    def cell_row(g, tile):
        per = tile // 128
        rows = [turned_ref[pl.ds(cells0 + g * per + i, 1), :] for i in range(per)]
        return jnp.concatenate(rows, axis=1).astype(jnp.int32)

    sm = place_small(info_ref[0], arr_ref, info_ref[1], cell_row, slots, nf, nz, npl)
    fr = sm + pltpu.roll(sm, half, axis=1)
    r = cs * jnp.where(lane < half, fr + left + right, deep)
    ys[...] = reduce_rhs(r, slice(0, 128), fac[:5])
    substitute(ys, fac[5], fac[6], same)
    hi, lo = split2(ys[...])
    terms = jnp.concatenate([sm.astype(BF), hi, lo], axis=1)
    k = lax.broadcasted_iota(jnp.int32, (384, 1), 0)
    near = jnp.where(k % 128 < half, 1, 2)
    target = jnp.where(k < 128, spots(k, nf, npl, 0, CY - 1), spots(k, nf, npl, near, CY - 1 - near))
    fringe = on_fringe(lane)
    held[1].wait()
    leave = [pltpu.make_async_copy(o_ref.at[f], out_any.at[f], sems.at[4 + f]) for f in range(nf)]
    for f in range(nf):
        put = (lax.broadcasted_iota(jnp.int32, (384, npl), 1) + f * npl == target).astype(F32).astype(BF)
        add = jnp.dot(terms, put, preferred_element_type=F32)
        for t in range(nt):
            v = pay_ref[(f*nt+t)*nz:(f*nt+t+1)*nz, :]
            o_ref[f, :, t*128:(t+1)*128] = jnp.where(fringe, 0.0, v) + add[:, t*128:(t+1)*128]
        leave[f].start()
    for c in leave:
        c.wait()


def finish(turn, shape, arrived, own, moved, e, blocks, turned):
    nz = shape[1]
    return pl.pallas_call(
        functools.partial(finish_kernel, edges=len(e) == 2, blocks=blocks, turned=turned),
        out_shape=jax.ShapeDtypeStruct(shape, F32),
        in_specs=[SM] + [ANY] * 5 + [VM] * (len(e) - 2),
        out_specs=ANY,
        scratch_shapes=[pltpu.VMEM(v.shape, F32) for v in (arrived, e[0])] + [pltpu.VMEM(shape, F32), pltpu.VMEM(own.shape, F32)]
        + [pltpu.VMEM((nz, 128), F32)] * 10 + [pltpu.SemaphoreType.DMA((4 + shape[0],))],
        compiler_params=CP,
        name="finish",
    )(turn, arrived, own, moved, *e)


TILE = 256
UNROLL = 4


def exchange(values, blocks, cap, nf):
    if cap == TILE:
        return lax.all_to_all(values, ("mesh", "blk"), 0, 0, tiled=True)
    halves = values.reshape(2, -1, nf, TILE).transpose(0, 2, 1, 3).reshape(2, nf, blocks, cap)
    sent = halves.transpose(0, 2, 1, 3).reshape(2 * blocks, nf, cap)
    got = lax.all_to_all(sent, ("mesh", "blk"), 0, 0, tiled=True)
    got = got.reshape(2, blocks, nf, cap).transpose(0, 2, 1, 3).reshape(2, nf, -1, TILE)
    return got.transpose(0, 2, 1, 3).reshape(values.shape)


def turn(values, cap, by):
    groups = values.reshape(values.shape[:-1] + (-1, cap))
    return jnp.roll(groups, -by, axis=-2).reshape(values.shape)


def local(rotation_step, field_state, diffusivity, stretch, donor_base, donor_frac, fringe_cell):
    on_back = lax.axis_index("mesh") == 1
    blocks = lax.axis_size("blk")
    rotation = rotation_step[0]
    start, kappa, along = field_state[0, 0], diffusivity[0, 0], stretch[0, 0]
    base, frac, cells = donor_base[0, 0], donor_frac[0, 0], fringe_cell[0, 0]
    nf = start.shape[0]
    slots = base.shape[0]
    cap = slots // blocks
    turned = cap != TILE
    send0, frac0, cells0 = base, frac, cells
    if turned:
        by = jnp.where(on_back, 0, rotation)
        send0, frac0, cells0 = turn(base, cap, by), turn(frac, cap, by), turn(cells, cap, by)
    edges = cap == TILE and 2 * nf == nf * TILE // 128
    row = (1, slots)
    low, high = pack(start, kappa, along)
    left = lax.ppermute(high, "blk", [(i, (i + 1) % blocks) for i in range(blocks)])
    right = lax.ppermute(low, "blk", [((i + 1) % blocks, i) for i in range(blocks)])
    values = interp(rotation_step, start, send0.reshape(row), frac0.reshape(3, 1, slots), TILE, blocks, turned)

    def branch(distance):
        def shift(v, off, blade):
            pairs = [(i, (i + off) % blocks) for i in range(blocks)] if blade else []
            pairs = pairs + [(blocks + i, blocks + (i + distance + off) % blocks) for i in range(blocks)]
            return lax.ppermute(v, ("mesh", "blk"), pairs)

        def run(pay, step, arrived, f1t, fac, base, frac, cells0):
            moved = shift(pay, 0, False)
            values, e = relay(
                step, arrived, cells0.reshape(row), f1t, fac, base.reshape(row), frac.reshape(3, 1, slots), TILE, nf, edges,
                blocks, turned,
            )
            arrived = exchange(values, blocks, cap, nf)
            near = () if edges else (shift(e, 1, True), shift(e, -1, True))
            return arrived, moved, e, shift(e, 0, False), *near

        return run

    values, left, right = lax.optimization_barrier((values, left, right))
    arrived = exchange(values, blocks, cap, nf)
    f1t, pay, fac = march(start, kappa, along, low, high, left, right, cells0.reshape(-1, 128))
    arrived, moved, e, came, *near = lax.switch(
        rotation - 1, [branch(d) for d in range(1, TURN_MOST + 1)], pay, rotation_step, arrived, f1t, fac, base, frac, cells0
    )
    return finish(rotation_step, start.shape, arrived, pay, moved, (e, came, *near), blocks, turned)[None, None]


def solution(mesh):
    placed = (
        P(),
        P("mesh", "blk", None, None, None),
        P("mesh", "blk", None, None, None),
        P("mesh", "blk", None, None),
        P("mesh", "blk", None),
        P("mesh", "blk", None, None),
        P("mesh", "blk", None),
    )
    return jax.shard_map(
        local,
        mesh=mesh,
        in_specs=placed,
        out_specs=P("mesh", "blk", None, None, None),
        check_vma=False,
    )
```

```python
import functools
import jax
import jax.numpy as jnp
from jax import lax
from jax.experimental import pallas as pl
from jax.experimental.pallas import tpu as pltpu
from jax.sharding import PartitionSpec as P

CY = 32
ITERS = 2
TURN_MOST = 7
F32, BF = jnp.float32, jnp.bfloat16
VM = pl.BlockSpec(memory_space=pltpu.VMEM)
SM = pl.BlockSpec(memory_space=pltpu.SMEM)
ANY = pl.BlockSpec(memory_space=pl.ANY)
WHOLE = pltpu.CompilerParams(vmem_limit_bytes=64 * 1024 * 1024)
CP = pltpu.CompilerParams(vmem_limit_bytes=48 * 1024 * 1024)


def split2(v):
    hi = v.astype(BF)
    lo = (v - hi.astype(F32)).astype(BF)
    return hi, lo


def down(v, k):
    return pltpu.roll(v, k, axis=0)
def up(v, k):
    return pltpu.roll(v, v.shape[0] - k, axis=0)

def factor(g_ref, q0, q1, p1, q2, p2, h, iv):
    nz, w = g_ref.shape
    for c in range(0, w, 128):
        s = slice(c, c+128)
        z = lax.broadcasted_iota(jnp.int32, (nz, 128), 0)
        g = g_ref[:, s]
        q = 1.0 / g
        q0[:, s] = q
        qd = jnp.where(z >= 1, down(q, 1), 0.0)
        qu = jnp.where(z < nz-1, up(q, 1), 0.0)
        g = g - qd - qu
        p = jnp.where(z >= 2, qd, 0.0)
        for k, (qr, pr) in ((2, (q1, p1)), (4, (q2, p2))):
            q = 1.0 / g
            qr[:, s] = q
            pr[:, s] = p
            pq = p * q
            ppq = p * pq
            g = g - p * p * down(q, k) - up(ppq, k)
            p = p * down(pq, k)
            p = jnp.where(z >= 2*k, p, 0.0)
        g_ref[:, s] = g
        h[:, s] = p
    prev = None
    for r in range(0, nz, 8):
        g = g_ref[r:r+8, :]
        if prev is None:
            hk = jnp.zeros_like(g)
        else:
            p = h[r:r+8, :]
            hk = p * prev
            g = g - p * hk
        prev = 1.0 / g
        h[r:r+8, :] = hk
        iv[r:r+8, :] = prev

def reduce_rhs(r, s, fs):
    q0, q1, p1, q2, p2 = fs
    nz = r.shape[0]
    z = lax.broadcasted_iota(jnp.int32, r.shape, 0)
    w = q0[:, s] * r
    r = r + jnp.where(z >= 1, down(w, 1), 0.0) + jnp.where(z < nz-1, up(w, 1), 0.0)
    for k, qr, pr in ((2, q1, p1), (4, q2, p2)):
        w = qr[:, s] * r
        p = pr[:, s]
        r = r + p * down(w, k) + up(p * w, k)
    return r


def substitute(y, h, iv, widen):
    nz = y.shape[0]
    prev = y[0:8, :]
    for r in range(8, nz, 8):
        prev = y[r:r+8, :] + widen(h[r:r+8, :]) * prev
        y[r:r+8, :] = prev
    prev = prev * widen(iv[nz-8:nz, :])
    y[nz-8:nz, :] = prev
    for r in range(nz-16, -1, -8):
        prev = y[r:r+8, :] * widen(iv[r:r+8, :]) + widen(h[r+8:r+16, :]) * prev
        y[r:r+8, :] = prev


def same(v):
    return v


def lanes(nz):
    return lax.broadcasted_iota(jnp.int32, (nz, 128), 1)


def on_fringe(lane):
    return (lane % CY == 0) | (lane % CY == CY - 1)


def pack_planes(get, nf, t, x, lane):
    out = None
    for f in range(nf):
        v = get(f, t)
        by = (f - x) * CY % 128
        v = v if by == 0 else pltpu.roll(v, by, axis=1)
        out = v if out is None else jnp.where(lane >= f * CY, v, out)
    return out


def fold(v):
    n = v.shape[0] // 4
    tail = jnp.concatenate([pltpu.roll(v[3*n:], 128 - CY - i * CY, axis=1) for i in range(3)], axis=0)
    lane = lax.broadcasted_iota(jnp.int32, tail.shape, 1)
    return jnp.where(lane < 3 * CY, v[:3*n], tail)


def unfold3(v):
    n = v.shape[0] // 3
    a, b, c = [pltpu.roll(v[i*n:(i+1)*n], (i + 1) * CY, axis=1) for i in range(3)]
    lane = lax.broadcasted_iota(jnp.int32, a.shape, 1)
    return jnp.concatenate([v, jnp.where(lane < CY, a, jnp.where(lane < 2 * CY, b, c))], axis=0)


def pack_kernel(f_any, kap_any, al_any, lo_any, hi_any, f_ref, kap_ref, al_ref, lo_ref, hi_ref, sems):
    nf, nz, npl = f_ref.shape
    copies = [pltpu.make_async_copy(f_any.at[f], f_ref.at[f], sems.at[f]) for f in range(nf)]
    copies += [pltpu.make_async_copy(kap_any.at[k], kap_ref.at[k], sems.at[nf + k]) for k in range(2)]
    copies += [pltpu.make_async_copy(al_any, al_ref, sems.at[nf + 2])]
    for c in copies:
        c.start()
    lane = lanes(nz)
    per, nt = 128 // CY, npl // 128

    def field(f, t):
        return f_ref[f, :, t*128:(t+1)*128]

    def coef(f, t):
        sl = slice(t*128, (t+1)*128)
        return kap_ref[f, :, sl] if f < 2 else al_ref[:, sl]

    sides = ((lo_ref, lo_any, 0, 0, 1), (hi_ref, hi_any, nt - 1, per - 1, -1))
    parts = [slice(0, nz), slice(nz, 2 * nz), slice(2 * nz, 2 * nz + nz * 3 // 4)]
    back = [pltpu.make_async_copy(ref.at[p], out.at[p], sems.at[nf + 3 + 3 * i + j])
            for i, (ref, out, *_) in enumerate(sides) for j, p in enumerate(parts)]
    for c in copies[:nf]:
        c.wait()
    for i, (ref, _, t, x, step) in enumerate(sides):
        ref[parts[0]] = pack_planes(field, nf, t, x, lane)
        back[3 * i].start()
        ref[parts[1]] = pack_planes(field, nf, t, x + step, lane)
        back[3 * i + 1].start()
    for c in copies[nf:]:
        c.wait()
    for i, (ref, _, t, x, step) in enumerate(sides):
        ref[parts[2]] = fold(pack_planes(coef, 3, t, x, lane))
        back[3 * i + 2].start()
    for c in back:
        c.wait()


def pack(fields, kappa, along):
    nf, nz, npl = fields.shape
    sh = jax.ShapeDtypeStruct((2 * nz + nz * 3 // 4, nf * CY), F32)
    return pl.pallas_call(
        pack_kernel,
        out_shape=(sh, sh),
        in_specs=[ANY] * 3,
        out_specs=(ANY, ANY),
        scratch_shapes=[pltpu.VMEM(v.shape, F32) for v in (fields, kappa, along, sh, sh)]
        + [pltpu.SemaphoreType.DMA((nf + 9,))],
        compiler_params=WHOLE,
        name="pack",
    )(fields, kappa, along)


def places(turn, tiles, blocks, turned):
    back = lax.axis_index("mesh")
    me = lax.axis_index("blk")
    by = 0 if turned else turn * (1 - back)
    return by, tiles * (1 - back), lax.rem(me + turn * back, blocks), back, lax.rem(me + blocks - turn * back, blocks)


def load_tiles(unroll, o_ref, info_ref, base_ref, frac_ref, a_ref, shift, nf, nz, npl, tile, t_ref=None):
    nx = npl // CY
    nt = base_ref.shape[1] // tile
    o_ref[pl.ds(nt - info_ref[1], nt)] = jnp.zeros((nt,) + o_ref.shape[1:], F32)

    def body(t, carry):
        g = t if shift is None else lax.rem(t + shift, nt)
        off = pl.multiple_of(g * tile, tile)
        b = base_ref[0:1, pl.ds(off, tile)]
        fz, fx, fy = [frac_ref[i, :, pl.ds(off, tile)] for i in range(3)]
        z0 = b // npl
        x0 = b // CY % nx
        y0 = b % CY
        iz = lax.broadcasted_iota(jnp.int32, (nz, tile), 0)
        whi, wlo = split2(jnp.where(iz == z0, 1.0 - fz, jnp.where(iz == z0 + 1, fz, 0.0)))
        w = jnp.concatenate([whi, wlo, whi, wlo], axis=0)
        iy = lax.broadcasted_iota(jnp.int32, (CY, tile), 0)
        wy = jnp.where(iy == y0, 1.0 - fy, jnp.where(iy == y0 + 1, fy, 0.0))
        wx = [jnp.where(x0 == x, 1.0 - fx, jnp.where(x0 == x - 1, fx, 0.0)) for x in range(nx)]
        rows = []
        for f in range(nf if t_ref is None else nf - 1):
            p = jnp.dot(a_ref[f * npl:(f + 1) * npl, :], w, preferred_element_type=F32)
            acc = wx[0] * p[:CY]
            for x in range(1, nx):
                acc = acc + wx[x] * p[x * CY:(x + 1) * CY]
            r = jnp.sum(acc * wy, axis=0, keepdims=True)
            rows += [r[:, i * 128:(i + 1) * 128] for i in range(tile // 128)]
        for i in range(tile // 128 if t_ref is not None else 0):
            sl = slice(i * 128, (i + 1) * 128)
            low = jnp.broadcast_to(z0[:, sl], (8, 128))
            high = low + 1
            total = None
            for y in range(0, CY, 8):
                at0 = at1 = None
                for x in range(nx):
                    v = t_ref[x * CY + y:x * CY + y + 8, :]
                    v0 = wx[x][:, sl] * jnp.take_along_axis(v, low, axis=1)
                    v1 = wx[x][:, sl] * jnp.take_along_axis(v, high, axis=1)
                    at0 = v0 if at0 is None else at0 + v0
                    at1 = v1 if at1 is None else at1 + v1
                v = (at0 * (1.0 - fz[:, sl]) + at1 * fz[:, sl]) * wy[y:y + 8, sl]
                total = v if total is None else total + v
            rows.append(jnp.sum(total, axis=0, keepdims=True))
        o_ref[info_ref[1] + t] = jnp.concatenate(rows, axis=0)
        return carry

    lax.fori_loop(0, nt, body, 0, unroll=unroll)


def split_into(a_ref, row, v):
    n, nz = v.shape
    hi, lo = split2(v)
    for i, part in enumerate((hi, hi, lo, lo)):
        a_ref[row:row + n, i * nz:(i + 1) * nz] = part


def interp_kernel(turn_any, f_ref, base_any, frac_any, o_ref, a_ref, t_ref, base_ref, frac_ref, turn_ref, sems, *, tile, blocks, turned):
    nf, nz, npl = f_ref.shape
    pairs = ((base_any, base_ref), (frac_any, frac_ref), (turn_any, turn_ref))
    copies = [pltpu.make_async_copy(a, b, sems.at[i]) for i, (a, b) in enumerate(pairs)]
    for c in copies:
        c.start()
    for f in range(nf - 1):
        split_into(a_ref, f * npl, f_ref[f].T)
    t_ref[...] = f_ref[nf - 1].T
    for c in copies:
        c.wait()
    info_ref = places(turn_ref[0], base_ref.shape[1] // tile, blocks, turned)
    load_tiles(16, o_ref, info_ref, base_ref, frac_ref, a_ref, info_ref[0], nf, nz, npl, tile, t_ref)


def interp(turn, fields, base, frac, tile, blocks, turned):
    nf, nz, npl = fields.shape
    slots = base.shape[-1]
    return pl.pallas_call(
        functools.partial(interp_kernel, tile=tile, blocks=blocks, turned=turned),
        out_shape=jax.ShapeDtypeStruct((2 * slots // tile, nf * tile // 128, 128), F32),
        in_specs=[ANY, VM, ANY, ANY],
        out_specs=VM,
        scratch_shapes=[pltpu.VMEM((nf * npl, 4 * nz), BF), pltpu.VMEM((npl, nz), F32),
                        pltpu.VMEM(base.shape, jnp.int32), pltpu.VMEM(frac.shape, F32),
                        pltpu.SMEM((1,), jnp.int32), pltpu.SemaphoreType.DMA((3,))],
        compiler_params=CP,
        name="interp",
    )(turn, fields, base, frac)


def right_sides(start_ref, tiles, hl, hr, kap_ref, si, y, fs, lane):
    nf, nz, npl = start_ref.shape
    nt = npl // 128
    for f in range(nf):
        k = 1 if f == nf - 1 else 0
        v = tiles(f)
        rp = [pltpu.roll(u, CY, axis=1) for u in v]
        rm = [pltpu.roll(u, 128 - CY, axis=1) for u in v]
        left_in = hl if f == 0 else pltpu.roll(hl, 128 - f * CY, axis=1)
        by = (128 - CY - f * CY) % 128
        right_in = hr if by == 0 else pltpu.roll(hr, by, axis=1)
        for t in range(nt):
            left = jnp.where(lane < CY, left_in if t == 0 else rp[t-1], rp[t])
            right = jnp.where(lane >= 128 - CY, right_in if t == nt - 1 else rm[t+1], rm[t])
            side = pltpu.roll(v[t], 1, axis=1) + pltpu.roll(v[t], 127, axis=1)
            sl = slice(t * 128, (t + 1) * 128)
            r = (start_ref[f, :, sl] + kap_ref[k, :, sl] * (left + right + side)) * si[:, sl]
            y[:, f*npl+t*128:f*npl+(t+1)*128] = reduce_rhs(r, slice(k*npl + t*128, k*npl + (t+1)*128), fs)


def march_kernel(start_ref, kap_ref, al_ref, lo_ref, hi_ref, left_ref, right_ref, cells_ref,
                 f1t_ref, pay_ref, fac_ref, y, y2, g, q0, q1, p1, q2, p2, h, iv, si, gs):
    nf, nz, npl = start_ref.shape
    nt = npl // 128
    own = 2 * npl
    lane = lanes(nz)
    fringe = on_fringe(lane)
    inv = 1.0 / al_ref[...]
    si[...] = inv
    for k in range(2):
        g[:, k*npl:(k+1)*npl] = 2.0 + (1.0 + 4.0 * kap_ref[k]) * inv
    outer = []
    for i, (near, mine) in enumerate(((left_ref, lo_ref), (right_ref, hi_ref))):
        c3 = unfold3(near[2*nz:, :])
        r32, r64, r96 = [pltpu.roll(c3, j, axis=1) for j in (32, 64, 96)]
        c = jnp.where(lane < CY, c3, jnp.where(lane < 2*CY, r32, r64))
        s = jnp.where(lane < CY, r64, jnp.where(lane < 2*CY, r96, jnp.where(lane < 3*CY, c3, r32)))
        inv = 1.0 / s
        g[:, own+i*128:own+(i+1)*128] = 2.0 + (1.0 + 4.0 * c) * inv
        v = near[:nz, :]
        z = jnp.where(fringe, 0.0, v)
        side = pltpu.roll(z, 1, axis=1) + pltpu.roll(z, 127, axis=1)
        outer.append((v + c * (near[nz:2*nz, :] + mine[:nz, :] + side)) * inv)
    fs = (q0, q1, p1, q2, p2)
    factor(g, q0, q1, p1, q2, p2, h, iv)

    def clear(v):
        return jnp.where(fringe, 0.0, v)

    right_sides(start_ref, lambda f: [clear(start_ref[f, :, t*128:(t+1)*128]) for t in range(nt)],
                left_ref[:nz, :], right_ref[:nz, :], kap_ref, si, y, fs, lane)
    for i in range(2):
        y[:, nf*npl+i*128:nf*npl+(i+1)*128] = reduce_rhs(outer[i], slice(own+i*128, own+(i+1)*128), fs)

    def widen(v):
        m, p = v[:, :npl], v[:, npl:own]
        return jnp.concatenate([m] * (nf - 1) + [p, v[:, own:]], axis=1)

    def widen_own(v):
        m, p = v[:, :npl], v[:, npl:own]
        return jnp.concatenate([m] * (nf - 1) + [p], axis=1)

    substitute(y, h, iv, widen)

    def first(f):
        return [clear(y[:, f*npl+t*128:f*npl+(t+1)*128]) for t in range(nt)]

    right_sides(start_ref, first, y[:, nf*npl:nf*npl+128], y[:, nf*npl+128:nf*npl+256], kap_ref, si, y2, fs, lane)
    substitute(y2, h, iv, widen_own)
    for f in range(nf):
        for t in range(nt):
            j = f * nt + t
            pay_ref[j*nz:(j+1)*nz, :] = y2[:, f*npl+t*128:f*npl+(t+1)*128]
    for f in range(nf):
        v = first(f)
        for t in range(nt):
            f1t_ref[f*npl+t*128:f*npl+(t+1)*128, :] = v[t].T
    nx = npl // CY
    half = nf * 2 * nx
    ln = lane % half
    x, side, deep = ln // 2 % nx, ln % 2, jnp.where(lane >= half, 2, 1)
    src = x % (128 // CY) * CY + jnp.where(side == 0, deep, CY - 1 - deep)

    def pick(get):
        out = None
        for t in range(nt):
            v = jnp.take_along_axis(get(t), src, axis=1)
            out = v if out is None else jnp.where(x // (128 // CY) == t, v, out)
        return out

    ck = [pick(lambda t, k=k: kap_ref[k, :, t*128:(t+1)*128]) for k in range(2)]
    c = jnp.where(ln // (2 * nx) == nf - 1, ck[1], ck[0])
    inv = pick(lambda t: si[:, t*128:(t+1)*128])
    cs = c * inv
    gg = 2.0 + (inv + 4.0 * cs)
    j = nf * nt
    few = (lane // (4 * nx) % 2) * (nf - 1) * 2 * nx + (lane // (2 * nx) % 2) * half + ln % (2 * nx)
    pay_ref[j*nz:(j+1)*nz, :] = jnp.where(
        lane < half, jnp.take_along_axis(cs, few, axis=1), jnp.take_along_axis(gg, few, axis=1))
    pay_ref[(j+1)*nz:, :] = cells_ref[...].astype(F32)
    gs[...] = gg
    refs = [fac_ref.at[i*nz:(i+1)*nz] for i in range(7)]
    factor(gs, *refs)
    fac_ref[7*nz:, :] = cs


def march(start, kappa, along, low, high, left, right, cells):
    nf, nz, npl = start.shape
    nt = npl // 128
    rows = (nf * nt + 1) * nz + cells.shape[0]
    w = 2 * npl + 256
    return pl.pallas_call(
        march_kernel,
        out_shape=(jax.ShapeDtypeStruct((nf * npl, nz), F32), jax.ShapeDtypeStruct((rows, 128), F32),
                   jax.ShapeDtypeStruct((8 * nz, 128), F32)),
        in_specs=[VM] * 8,
        out_specs=(VM, VM, VM),
        scratch_shapes=[pltpu.VMEM((nz, nf*npl+256), F32), pltpu.VMEM((nz, nf*npl), F32)]
        + [pltpu.VMEM((nz, w), F32)] * 8 + [pltpu.VMEM((nz, npl), F32), pltpu.VMEM((nz, 128), F32)],
        compiler_params=CP,
        name="march",
    )(start, kappa, along, low, high, left, right, cells)


def place_small(shift, arr_ref, row0, cell_row, slots, nf, nz, npl):
    rows = arr_ref.shape[1]
    per = rows // nf
    tile = per * 128
    nt = slots // tile
    nx = npl // CY
    nq = 2 * nx
    zo, av = [], []
    for t in range(nt):
        c = cell_row(lax.rem(t + shift, nt), tile)
        cz = c // npl
        q = c // CY % nx * 2 + c % 2
        zo.append((lax.broadcasted_iota(jnp.int32, (nz, tile), 0) == cz).astype(F32).astype(BF))
        oh = lax.broadcasted_iota(jnp.int32, (nq, tile), 0) == q
        a = arr_ref[row0 + t]
        his, los = [], []
        for f in range(nf):
            row = jnp.concatenate([a[f*per+i:f*per+i+1] for i in range(per)], axis=1)
            hi, lo = split2(jnp.where(oh, row, 0.0))
            his.append(hi)
            los.append(lo)
        av.append(jnp.concatenate(his + los, axis=0))
    zo = jnp.concatenate(zo, axis=1)
    av = jnp.concatenate(av, axis=1)
    return lax.dot_general(zo, av, (((1,), (1,)), ((), ())), preferred_element_type=F32)


def spots(k, nf, npl, low, high):
    nq = 2 * npl // CY
    return k // nq % nf * npl + k % nq // 2 * CY + jnp.where(k % 2 == 0, low, high)


def relay_kernel(turn_ref, arr_ref, cells_ref, f1t_ref, fac_ref, base_ref, frac_ref, o_ref, e_ref, a_ref, ys, t_ref, *, tile, nf, edges, blocks, turned):
    nz = f1t_ref.shape[1]
    info_ref = places(turn_ref[0], base_ref.shape[1] // tile, blocks, turned)
    npl = f1t_ref.shape[0] // nf
    slots = base_ref.shape[1]
    half = nf * 2 * npl // CY
    lane = lanes(nz)

    def cell_row(g, tile):
        return cells_ref[0:1, pl.ds(pl.multiple_of(g * tile, tile), tile)]

    sm = place_small(info_ref[0], arr_ref, info_ref[1], cell_row, slots, nf, nz, npl)
    fr = sm + pltpu.roll(sm, half, axis=1)
    fac = [fac_ref.at[i*nz:(i+1)*nz] for i in range(8)]
    ys[...] = reduce_rhs(fac[7][...] * fr, slice(0, 128), fac[:5])
    substitute(ys, fac[5], fac[6], same)
    e = ys[...]
    low = lax.broadcasted_iota(jnp.int32, (nz // 2, 128), 1) < half
    e_ref[...] = jnp.where(low, e[:nz//2], pltpu.roll(e[nz//2:], half, axis=1))
    hi, lo = split2(e)
    both = jnp.where(lane < half, hi.astype(F32), pltpu.roll(lo.astype(F32), half, axis=1))
    terms = jnp.concatenate([sm.astype(BF), both.astype(BF)], axis=1)
    k = lax.broadcasted_iota(jnp.int32, (1, 256), 1)
    target = jnp.where(k < 128, spots(k, nf, npl, 0, CY - 1), spots(k, nf, npl, 1, CY - 2))
    for f in range(nf):
        row = lax.broadcasted_iota(jnp.int32, (npl, 256), 0) + f * npl
        put = (row == target).astype(F32).astype(BF)
        add = lax.dot_general(put, terms, (((1,), (1,)), ((), ())), preferred_element_type=F32)
        v = f1t_ref[f*npl:(f+1)*npl, :] + add
        if f < nf - 1:
            split_into(a_ref, f * npl, v)
        else:
            t_ref[...] = v
    load_tiles(UNROLL, o_ref, info_ref, base_ref, frac_ref, a_ref, None, nf, nz, npl, tile, t_ref)
    if edges:
        turned = e.T
        nt = slots // tile
        nq = half // nf
        for col, by in ((nq - 2, 1), (0, nt - 1)):
            rows = jnp.concatenate([turned[f*nq+col:f*nq+col+2] for f in range(nf)], axis=0)
            o_ref[nt - info_ref[1] + lax.rem(info_ref[2] + by, nt)] = rows


def relay(turn, arrived, cells, f1t, fac, base, frac, tile, nf, edges, blocks, turned):
    nz = f1t.shape[1]
    return pl.pallas_call(
        functools.partial(relay_kernel, tile=tile, nf=nf, edges=edges, blocks=blocks, turned=turned),
        out_shape=(jax.ShapeDtypeStruct(arrived.shape, F32), jax.ShapeDtypeStruct((nz // 2, 128), F32)),
        in_specs=[SM] + [VM] * 6,
        out_specs=(VM, VM),
        scratch_shapes=[pltpu.VMEM((f1t.shape[0], 4 * nz), BF), pltpu.VMEM((nz, 128), F32),
                        pltpu.VMEM((f1t.shape[0] // nf, nz), F32)],
        compiler_params=CP,
        name="relay",
    )(turn, arrived, cells, f1t, fac, base, frac)


def unfold(v):
    return jnp.concatenate([v, pltpu.roll(v, 64, axis=1)], axis=0)


def finish_kernel(turn_ref, arr_any, own_ref, moved_ref, e_any, came_any, *refs, edges, blocks, turned):
    if edges:
        out_any, *refs = refs
    else:
        el_ref, er_ref, out_any, *refs = refs
    arr_ref, e_ref, o_ref, pay_ref, ys, gs, *fac, sems = refs
    nf, nz, npl = o_ref.shape
    nt = npl // 128
    nx = npl // CY
    nq = 2 * nx
    half = nf * nq
    j = nf * nt
    cells0 = (j + 1) * nz
    slots = (pay_ref.shape[0] - cells0) * 128
    lines = slice(j * nz, pay_ref.shape[0])
    rest = slice(0, j * nz)
    came = pltpu.make_async_copy(arr_any, arr_ref, sems.at[2])
    came.start()

    def copies(ref, e):
        pairs = [(ref.at[s], pay_ref.at[s]) for s in (lines, rest)] + [(e, e_ref)]
        return [pltpu.make_async_copy(a, b, sems.at[i]) for i, (a, b) in zip((0, 1, 3), pairs)]

    back = lax.axis_index("mesh")

    @pl.when(back == 0)
    def _():
        for c in copies(own_ref, e_any):
            c.start()

    @pl.when(back != 0)
    def _():
        for c in copies(moved_ref, came_any):
            c.start()

    info_ref = places(turn_ref[0], arr_ref.shape[0] // 2, blocks, turned)
    held = copies(own_ref, e_any)
    lane = lanes(nz)
    q = lane % nq
    came.wait()
    held[0].wait()
    held[2].wait()
    ln = lane % half
    few = ln // nq // (nf - 1) * 2 * nq + lane // half * nq + ln % nq
    table = pay_ref[j*nz:(j+1)*nz, :]
    cs = jnp.take_along_axis(table, few, axis=1)
    gs[...] = jnp.take_along_axis(table, few + half, axis=1)
    factor(gs, *fac)
    e = unfold(e_ref[...])
    if edges:
        chunks = arr_ref.shape[0] // 2
        el = arr_ref[chunks - info_ref[1] + lax.rem(info_ref[4] + chunks - 1, chunks)]
        er = arr_ref[chunks - info_ref[1] + lax.rem(info_ref[4] + 1, chunks)]
        none = jnp.zeros((nq - 4, nz), F32)
        parts = []
        for f in range(nf):
            parts += [el[2*f:2*f+2], none, er[2*f:2*f+2]]
        parts = jnp.concatenate(parts, axis=0)
        outer = jnp.concatenate([parts, parts], axis=0).T
        left = right = outer
    else:
        left = pltpu.roll(unfold(el_ref[...]), 128 - (nq - 2), axis=1)
        right = pltpu.roll(unfold(er_ref[...]), nq - 2, axis=1)
    left = jnp.where(q < 2, left, pltpu.roll(e, 2, axis=1))
    right = jnp.where(q >= nq - 2, right, pltpu.roll(e, 126, axis=1))
    deep = pltpu.roll(e, half, axis=1)

    def cell_row(g, tile):
        per = tile // 128
        rows = [pay_ref[pl.ds(cells0 + g * per + i, 1), :] for i in range(per)]
        return jnp.concatenate(rows, axis=1).astype(jnp.int32)

    sm = place_small(info_ref[0], arr_ref, info_ref[1], cell_row, slots, nf, nz, npl)
    fr = sm + pltpu.roll(sm, half, axis=1)
    r = cs * jnp.where(lane < half, fr + left + right, deep)
    ys[...] = reduce_rhs(r, slice(0, 128), fac[:5])
    substitute(ys, fac[5], fac[6], same)
    hi, lo = split2(ys[...])
    terms = jnp.concatenate([sm.astype(BF), hi, lo], axis=1)
    k = lax.broadcasted_iota(jnp.int32, (384, 1), 0)
    near = jnp.where(k % 128 < half, 1, 2)
    target = jnp.where(k < 128, spots(k, nf, npl, 0, CY - 1), spots(k, nf, npl, near, CY - 1 - near))
    fringe = on_fringe(lane)
    held[1].wait()
    leave = [pltpu.make_async_copy(o_ref.at[f], out_any.at[f], sems.at[4 + f]) for f in range(nf)]
    for f in range(nf):
        put = (lax.broadcasted_iota(jnp.int32, (384, npl), 1) + f * npl == target).astype(F32).astype(BF)
        add = jnp.dot(terms, put, preferred_element_type=F32)
        for t in range(nt):
            v = pay_ref[(f*nt+t)*nz:(f*nt+t+1)*nz, :]
            o_ref[f, :, t*128:(t+1)*128] = jnp.where(fringe, 0.0, v) + add[:, t*128:(t+1)*128]
        leave[f].start()
    for c in leave:
        c.wait()


def finish(turn, shape, arrived, own, moved, e, blocks, turned):
    nz = shape[1]
    return pl.pallas_call(
        functools.partial(finish_kernel, edges=len(e) == 2, blocks=blocks, turned=turned),
        out_shape=jax.ShapeDtypeStruct(shape, F32),
        in_specs=[SM] + [ANY] * 5 + [VM] * (len(e) - 2),
        out_specs=ANY,
        scratch_shapes=[pltpu.VMEM(v.shape, F32) for v in (arrived, e[0])] + [pltpu.VMEM(shape, F32), pltpu.VMEM(own.shape, F32)]
        + [pltpu.VMEM((nz, 128), F32)] * 9 + [pltpu.SemaphoreType.DMA((4 + shape[0],))],
        compiler_params=CP,
        name="finish",
    )(turn, arrived, own, moved, *e)


TILE = 256
UNROLL = 4


def exchange(values, blocks, cap, nf):
    if cap == TILE:
        return lax.all_to_all(values, ("mesh", "blk"), 0, 0, tiled=True)
    halves = values.reshape(2, -1, nf, TILE).transpose(0, 2, 1, 3).reshape(2, nf, blocks, cap)
    sent = halves.transpose(0, 2, 1, 3).reshape(2 * blocks, nf, cap)
    got = lax.all_to_all(sent, ("mesh", "blk"), 0, 0, tiled=True)
    got = got.reshape(2, blocks, nf, cap).transpose(0, 2, 1, 3).reshape(2, nf, -1, TILE)
    return got.transpose(0, 2, 1, 3).reshape(values.shape)


def turn(values, cap, by):
    groups = values.reshape(values.shape[:-1] + (-1, cap))
    return jnp.roll(groups, -by, axis=-2).reshape(values.shape)


def local(rotation_step, field_state, diffusivity, stretch, donor_base, donor_frac, fringe_cell):
    on_back = lax.axis_index("mesh") == 1
    blocks = lax.axis_size("blk")
    rotation = rotation_step[0]
    start, kappa, along = field_state[0, 0], diffusivity[0, 0], stretch[0, 0]
    base, frac, cells = donor_base[0, 0], donor_frac[0, 0], fringe_cell[0, 0]
    nf = start.shape[0]
    slots = base.shape[0]
    cap = slots // blocks
    turned = cap != TILE
    send0, frac0, cells0 = base, frac, cells
    if turned:
        by = jnp.where(on_back, 0, rotation)
        send0, frac0, cells0 = turn(base, cap, by), turn(frac, cap, by), turn(cells, cap, by)
    edges = cap == TILE and 2 * nf == nf * TILE // 128
    row = (1, slots)
    low, high = pack(start, kappa, along)
    left = lax.ppermute(high, "blk", [(i, (i + 1) % blocks) for i in range(blocks)])
    right = lax.ppermute(low, "blk", [((i + 1) % blocks, i) for i in range(blocks)])
    values = interp(rotation_step, start, send0.reshape(row), frac0.reshape(3, 1, slots), TILE, blocks, turned)

    def branch(distance):
        def shift(v, off, blade):
            pairs = [(i, (i + off) % blocks) for i in range(blocks)] if blade else []
            pairs = pairs + [(blocks + i, blocks + (i + distance + off) % blocks) for i in range(blocks)]
            return lax.ppermute(v, ("mesh", "blk"), pairs)

        def run(pay, step, arrived, f1t, fac, base, frac, cells0):
            moved = shift(pay, 0, False)
            values, e = relay(
                step, arrived, cells0.reshape(row), f1t, fac, base.reshape(row), frac.reshape(3, 1, slots), TILE, nf, edges,
                blocks, turned,
            )
            arrived = exchange(values, blocks, cap, nf)
            near = () if edges else (shift(e, 1, True), shift(e, -1, True))
            return arrived, moved, e, shift(e, 0, False), *near

        return run

    values, left, right = lax.optimization_barrier((values, left, right))
    arrived = exchange(values, blocks, cap, nf)
    f1t, pay, fac = march(start, kappa, along, low, high, left, right, cells0.reshape(-1, 128))
    arrived, moved, e, came, *near = lax.switch(
        rotation - 1, [branch(d) for d in range(1, TURN_MOST + 1)], pay, rotation_step, arrived, f1t, fac, base, frac, cells0
    )
    return finish(rotation_step, start.shape, arrived, pay, moved, (e, came, *near), blocks, turned)[None, None]


def solution(mesh):
    placed = (
        P(),
        P("mesh", "blk", None, None, None),
        P("mesh", "blk", None, None, None),
        P("mesh", "blk", None, None),
        P("mesh", "blk", None),
        P("mesh", "blk", None, None),
        P("mesh", "blk", None),
    )
    return jax.shard_map(
        local,
        mesh=mesh,
        in_specs=placed,
        out_specs=P("mesh", "blk", None, None, None),
        check_vma=False,
    )
```
